32 devices in a mesh: dp: 4 (over y, x), side: 2 (over core), seq: 4 (over z).
Axes of the slice: x: 2, y: 2, z: 4, core: 2. Of those that a mesh axis runs over, the one named last changes fastest.
Arguments:
- tokens: bfloat16 [8192, 768], P(('dp', 'side', 'seq')), may hold values from -6 to 6
- head_in: bfloat16 [8192, 1024], P(('dp', 'side', 'seq')), may hold values from -6 to 6
- image_ids: int32 [8192], P(('dp', 'side', 'seq')), may hold values from 0 to 1, as said below
- out_cotangent: bfloat16 [8192, 768], P(('dp', 'side', 'seq')), may hold values from -6 to 6
- head_cotangent: bfloat16 [8192, 1024], P(('dp', 'side', 'seq')), may hold values from -6 to 6
- weight_attend: float32 [768, 2304], P(('dp', 'side', 'seq')), may hold values from -0.21875 to 0.21875
- weight_proj: float32 [768, 768], P(('dp', 'side', 'seq')), may hold values from -1.75 to 1.75
- weight_up: float32 [768, 3072], P(('dp', 'side', 'seq')), may hold values from -0.21875 to 0.21875
- weight_down: float32 [3072, 768], P(('dp', 'side', 'seq')), may hold values from -0.109375 to 0.109375
- weight_cond: float32 [768, 1024], P(('dp', 'side', 'seq')), may hold values from -0.21875 to 0.21875
- weight_mod: float32 [1024, 3072], P(('dp', 'side', 'seq')), may hold values from -0.1875 to 0.1875
- weight_inner: float32 [1024, 1024], P(('dp', 'side', 'seq')), may hold values from -0.1875 to 0.1875
- weight_outer: float32 [1024, 1024], P(('dp', 'side', 'seq')), may hold values from -0.1875 to 0.1875
- norm_params: float32 [768, 4], P(('dp', 'side', 'seq')), as said below
- mean_attend: float32 [768, 2304], P(('dp', 'side', 'seq')), may hold values from -0.375 to 0.375
- mean_proj: float32 [768, 768], P(('dp', 'side', 'seq')), may hold values from -0.375 to 0.375
- mean_up: float32 [768, 3072], P(('dp', 'side', 'seq')), may hold values from -0.375 to 0.375
- mean_down: float32 [3072, 768], P(('dp', 'side', 'seq')), may hold values from -0.375 to 0.375
- mean_cond: float32 [768, 1024], P(('dp', 'side', 'seq')), may hold values from -0.375 to 0.375
- mean_mod: float32 [1024, 3072], P(('dp', 'side', 'seq')), may hold values from -0.375 to 0.375
- mean_inner: float32 [1024, 1024], P(('dp', 'side', 'seq')), may hold values from -0.375 to 0.375
- mean_outer: float32 [1024, 1024], P(('dp', 'side', 'seq')), may hold values from -0.375 to 0.375
- mean_norms: float32 [768, 4], P(('dp', 'side', 'seq')), may hold values from -0.375 to 0.375
- square_attend: float32 [768, 2304], P(('dp', 'side', 'seq')), may hold values from 0.0085 to 0.135
- square_proj: float32 [768, 768], P(('dp', 'side', 'seq')), may hold values from 0.0021 to 0.034
- square_up: float32 [768, 3072], P(('dp', 'side', 'seq')), may hold values from 0.0085 to 0.135
- square_down: float32 [3072, 768], P(('dp', 'side', 'seq')), may hold values from 0.0085 to 0.135
- square_cond: float32 [768, 1024], P(('dp', 'side', 'seq')), may hold values from 0.0085 to 0.135
- square_mod: float32 [1024, 3072], P(('dp', 'side', 'seq')), may hold values from 0.0085 to 0.135
- square_inner: float32 [1024, 1024], P(('dp', 'side', 'seq')), may hold values from 0.0085 to 0.135
- square_outer: float32 [1024, 1024], P(('dp', 'side', 'seq')), may hold values from 0.0085 to 0.135
- square_norms: float32 [768, 4], P(('dp', 'side', 'seq')), may hold values from 0.0085 to 0.135
- ema_attend: float32 [768, 2304], P(('dp', 'side', 'seq')), may hold values from -0.21875 to 0.21875
- ema_proj: float32 [768, 768], P(('dp', 'side', 'seq')), may hold values from -1.75 to 1.75
- ema_up: float32 [768, 3072], P(('dp', 'side', 'seq')), may hold values from -0.21875 to 0.21875
- ema_down: float32 [3072, 768], P(('dp', 'side', 'seq')), may hold values from -0.109375 to 0.109375
- ema_cond: float32 [768, 1024], P(('dp', 'side', 'seq')), may hold values from -0.21875 to 0.21875
- ema_mod: float32 [1024, 3072], P(('dp', 'side', 'seq')), may hold values from -0.1875 to 0.1875
- ema_inner: float32 [1024, 1024], P(('dp', 'side', 'seq')), may hold values from -0.1875 to 0.1875
- ema_outer: float32 [1024, 1024], P(('dp', 'side', 'seq')), may hold values from -0.1875 to 0.1875
- ema_norms: float32 [768, 4], P(('dp', 'side', 'seq')), may hold values from -1 to 1.5
Outputs:
- block_out: bfloat16 [8192, 768], P(('dp', 'side', 'seq'))
- head_out: bfloat16 [8192, 1024], P(('dp', 'side', 'seq'))
- tokens_grad: float32 [8192, 768], P(('dp', 'side', 'seq'))
- head_in_grad: float32 [8192, 1024], P(('dp', 'side', 'seq'))
- grad_norm: float32 [], replicated
- new_attend: float32 [768, 2304], P(('dp', 'side', 'seq'))
- new_mean_attend: float32 [768, 2304], P(('dp', 'side', 'seq'))
- new_square_attend: float32 [768, 2304], P(('dp', 'side', 'seq'))
- new_proj: float32 [768, 768], P(('dp', 'side', 'seq'))
- new_mean_proj: float32 [768, 768], P(('dp', 'side', 'seq'))
- new_square_proj: float32 [768, 768], P(('dp', 'side', 'seq'))
- new_up: float32 [768, 3072], P(('dp', 'side', 'seq'))
- new_mean_up: float32 [768, 3072], P(('dp', 'side', 'seq'))
- new_square_up: float32 [768, 3072], P(('dp', 'side', 'seq'))
- new_down: float32 [3072, 768], P(('dp', 'side', 'seq'))
- new_mean_down: float32 [3072, 768], P(('dp', 'side', 'seq'))
- new_square_down: float32 [3072, 768], P(('dp', 'side', 'seq'))
- new_cond: float32 [768, 1024], P(('dp', 'side', 'seq'))
- new_mean_cond: float32 [768, 1024], P(('dp', 'side', 'seq'))
- new_square_cond: float32 [768, 1024], P(('dp', 'side', 'seq'))
- new_mod: float32 [1024, 3072], P(('dp', 'side', 'seq'))
- new_mean_mod: float32 [1024, 3072], P(('dp', 'side', 'seq'))
- new_square_mod: float32 [1024, 3072], P(('dp', 'side', 'seq'))
- new_inner: float32 [1024, 1024], P(('dp', 'side', 'seq'))
- new_mean_inner: float32 [1024, 1024], P(('dp', 'side', 'seq'))
- new_square_inner: float32 [1024, 1024], P(('dp', 'side', 'seq'))
- new_outer: float32 [1024, 1024], P(('dp', 'side', 'seq'))
- new_mean_outer: float32 [1024, 1024], P(('dp', 'side', 'seq'))
- new_square_outer: float32 [1024, 1024], P(('dp', 'side', 'seq'))
- new_norms: float32 [768, 4], P(('dp', 'side', 'seq'))
- new_mean_norms: float32 [768, 4], P(('dp', 'side', 'seq'))
- new_square_norms: float32 [768, 4], P(('dp', 'side', 'seq'))
- new_ema_attend: float32 [768, 2304], P(('dp', 'side', 'seq'))
- new_ema_proj: float32 [768, 768], P(('dp', 'side', 'seq'))
- new_ema_up: float32 [768, 3072], P(('dp', 'side', 'seq'))
- new_ema_down: float32 [3072, 768], P(('dp', 'side', 'seq'))
- new_ema_cond: float32 [768, 1024], P(('dp', 'side', 'seq'))
- new_ema_mod: float32 [1024, 3072], P(('dp', 'side', 'seq'))
- new_ema_inner: float32 [1024, 1024], P(('dp', 'side', 'seq'))
- new_ema_outer: float32 [1024, 1024], P(('dp', 'side', 'seq'))
- new_ema_norms: float32 [768, 4], P(('dp', 'side', 'seq'))
The draws below stay inside these ranges and needn't reach their ends.
Inputs may be any that keep to these rules, and one draw needn't show every extreme that they name: `image_ids`: within each device's block of 256 tokens the image numbers never fall; the visible and the masked block of a pair use the same numbers, with uneven counts. `norm_params`: columns 0 and 2 are gains between 0.2 and 1.8, columns 1 and 3 biases.
All inputs are finite; a program needn't handle non-finite values.
Results may differ from the reference program's by a relative error of at most 0.025.
Values may be sent and summed in bfloat16 or wider, within the bound.
A program may use at most 192 MiB of HBM per device.

```python
import math
import jax
import jax.numpy as jnp
from jax import lax

D = 768
HEADS = 12
HEAD_DIM = 64
FF = 3072
HW = 1024
TOK_DEV = 256
STEP = 5
IMGS = 2
TOKENS = 8192
N_DP = 4
N_SIDE = 2
N_SEQ = 4


def draw_image_ids(key, part):
    blocks = TOKENS // TOK_DEV
    first_key = jax.random.fold_in(key, 11)
    second_key = jax.random.fold_in(key, 12)
    first_draw = jax.random.randint(first_key, (blocks, TOK_DEV), 0, IMGS)
    second_draw = jax.random.randint(second_key, (blocks, TOK_DEV), 0, IMGS)
    picked = jnp.minimum(first_draw, second_draw)
    picked = picked.at[:, 0].set(0)
    picked = picked.at[:, TOK_DEV - 1].set(IMGS - 1)
    return jnp.sort(picked, axis=1).reshape(TOKENS).astype(jnp.int32)


def draw_norm_params(key, part):
    place = (jnp.arange(D, dtype=jnp.float32) / (D - 1))[:, None]
    column = jnp.arange(4)[None, :]
    rough_key = jax.random.fold_in(key, 21)
    bias_key = jax.random.fold_in(key, 22)
    rough = jax.random.uniform(rough_key, (D, 4), jnp.float32, 0.8, 1.2)
    gains = (0.25 + 1.25 * place) * rough
    biases = 0.3 * jnp.clip(jax.random.normal(bias_key, (D, 4), jnp.float32), -3.0, 3.0)
    return jnp.where(column % 2 == 0, gains, biases).astype(jnp.float32)


def steps_of(key, extent, cuts, least, high):
    loudness, own = 1.0, jax.random.fold_in(key, 6)
    for axis_at, blocks in cuts:
        heights = jnp.exp(jax.random.uniform(jax.random.fold_in(own, axis_at), (blocks,), jnp.float32, least / len(cuts), high / len(cuts)))
        loudness = loudness * jnp.repeat(heights, extent[axis_at] // blocks).reshape([-1 if axis == axis_at else 1 for axis in range(len(extent))])
    return loudness


def centred(stream_key, extent, deviation, reach, split=(), kind=jnp.bfloat16):
    entries = deviation * jax.random.normal(stream_key, extent, jnp.float32)
    if split:
        entries = entries * steps_of(stream_key, extent, split, -0.22, 0.18)
    return jnp.clip(entries, -reach, reach).astype(kind)


def setup_inputs(seed: int = 0) -> dict:
    streams_of = jax.random.split(jax.random.key(seed), 42)
    return {
        "tokens": centred(streams_of[0], (TOKENS, D), 1.0, 6.0, ((0, 32),)),
        "head_in": centred(streams_of[1], (TOKENS, HW), 1.0, 6.0, ((0, 32),)),
        "image_ids": draw_image_ids(jax.random.fold_in(streams_of[41], 71), 0),
        "out_cotangent": centred(streams_of[3], (TOKENS, D), 1.0, 6.0, ((0, 32),)),
        "head_cotangent": centred(streams_of[4], (TOKENS, HW), 1.0, 6.0, ((0, 32),)),
        "weight_attend": centred(streams_of[5], (D, 3 * D), D ** -0.5, 0.21875, ((0, 32),), jnp.float32),
        "weight_proj": centred(streams_of[6], (D, D), (D // 64) ** -0.5, 1.75, ((0, 32),), jnp.float32),
        "weight_up": centred(streams_of[7], (D, FF), D ** -0.5, 0.21875, ((0, 32),), jnp.float32),
        "weight_down": centred(streams_of[8], (FF, D), FF ** -0.5, 0.109375, ((0, 32),), jnp.float32),
        "weight_cond": centred(streams_of[9], (D, HW), D ** -0.5, 0.21875, ((0, 32),), jnp.float32),
        "weight_mod": centred(streams_of[10], (HW, 3 * HW), HW ** -0.5, 0.1875, ((0, 32),), jnp.float32),
        "weight_inner": centred(streams_of[11], (HW, HW), HW ** -0.5, 0.1875, ((0, 32),), jnp.float32),
        "weight_outer": centred(streams_of[12], (HW, HW), HW ** -0.5, 0.1875, ((0, 32),), jnp.float32),
        "norm_params": draw_norm_params(jax.random.fold_in(streams_of[41], 71), 0),
        "mean_attend": centred(streams_of[14], (D, 3 * D), 0.06, 0.375, ((0, 32),), jnp.float32),
        "mean_proj": centred(streams_of[15], (D, D), 0.06, 0.375, ((0, 32),), jnp.float32),
        "mean_up": centred(streams_of[16], (D, FF), 0.06, 0.375, ((0, 32),), jnp.float32),
        "mean_down": centred(streams_of[17], (FF, D), 0.06, 0.375, ((0, 32),), jnp.float32),
        "mean_cond": centred(streams_of[18], (D, HW), 0.06, 0.375, ((0, 32),), jnp.float32),
        "mean_mod": centred(streams_of[19], (HW, 3 * HW), 0.06, 0.375, ((0, 32),), jnp.float32),
        "mean_inner": centred(streams_of[20], (HW, HW), 0.06, 0.375, ((0, 32),), jnp.float32),
        "mean_outer": centred(streams_of[21], (HW, HW), 0.06, 0.375, ((0, 32),), jnp.float32),
        "mean_norms": centred(streams_of[22], (D, 4), 0.06, 0.375, ((0, 32),), jnp.float32),
        "square_attend": jnp.clip(jnp.exp(math.log(0.135) - 2.7652086 * jax.random.uniform(streams_of[23], (D, 3 * D), jnp.float32) ** steps_of(streams_of[23], (D, 3 * D), ((0, 32),), -0.2, 0.2)), 0.0085, 0.135),
        "square_proj": jnp.clip(jnp.exp(math.log(0.034) - 2.7844233 * jax.random.uniform(streams_of[24], (D, D), jnp.float32) ** steps_of(streams_of[24], (D, D), ((0, 32),), -0.2, 0.2)), 0.0021, 0.034),
        "square_up": jnp.clip(jnp.exp(math.log(0.135) - 2.7652086 * jax.random.uniform(streams_of[25], (D, FF), jnp.float32) ** steps_of(streams_of[25], (D, FF), ((0, 32),), -0.2, 0.2)), 0.0085, 0.135),
        "square_down": jnp.clip(jnp.exp(math.log(0.135) - 2.7652086 * jax.random.uniform(streams_of[26], (FF, D), jnp.float32) ** steps_of(streams_of[26], (FF, D), ((0, 32),), -0.2, 0.2)), 0.0085, 0.135),
        "square_cond": jnp.clip(jnp.exp(math.log(0.135) - 2.7652086 * jax.random.uniform(streams_of[27], (D, HW), jnp.float32) ** steps_of(streams_of[27], (D, HW), ((0, 32),), -0.2, 0.2)), 0.0085, 0.135),
        "square_mod": jnp.clip(jnp.exp(math.log(0.135) - 2.7652086 * jax.random.uniform(streams_of[28], (HW, 3 * HW), jnp.float32) ** steps_of(streams_of[28], (HW, 3 * HW), ((0, 32),), -0.2, 0.2)), 0.0085, 0.135),
        "square_inner": jnp.clip(jnp.exp(math.log(0.135) - 2.7652086 * jax.random.uniform(streams_of[29], (HW, HW), jnp.float32) ** steps_of(streams_of[29], (HW, HW), ((0, 32),), -0.2, 0.2)), 0.0085, 0.135),
        "square_outer": jnp.clip(jnp.exp(math.log(0.135) - 2.7652086 * jax.random.uniform(streams_of[30], (HW, HW), jnp.float32) ** steps_of(streams_of[30], (HW, HW), ((0, 32),), -0.2, 0.2)), 0.0085, 0.135),
        "square_norms": jnp.clip(jnp.exp(math.log(0.135) - 2.7652086 * jax.random.uniform(streams_of[31], (D, 4), jnp.float32) ** steps_of(streams_of[31], (D, 4), ((0, 32),), -0.2, 0.2)), 0.0085, 0.135),
        "ema_attend": centred(streams_of[32], (D, 3 * D), D ** -0.5, 0.21875, ((0, 32),), jnp.float32),
        "ema_proj": centred(streams_of[33], (D, D), (D // 64) ** -0.5, 1.75, ((0, 32),), jnp.float32),
        "ema_up": centred(streams_of[34], (D, FF), D ** -0.5, 0.21875, ((0, 32),), jnp.float32),
        "ema_down": centred(streams_of[35], (FF, D), FF ** -0.5, 0.109375, ((0, 32),), jnp.float32),
        "ema_cond": centred(streams_of[36], (D, HW), D ** -0.5, 0.21875, ((0, 32),), jnp.float32),
        "ema_mod": centred(streams_of[37], (HW, 3 * HW), HW ** -0.5, 0.1875, ((0, 32),), jnp.float32),
        "ema_inner": centred(streams_of[38], (HW, HW), HW ** -0.5, 0.1875, ((0, 32),), jnp.float32),
        "ema_outer": centred(streams_of[39], (HW, HW), HW ** -0.5, 0.1875, ((0, 32),), jnp.float32),
        "ema_norms": jnp.clip(-1.0 + 2.5 * jax.random.uniform(streams_of[40], (D, 4), jnp.float32) ** steps_of(streams_of[40], (D, 4), ((0, 32),), -0.2, 0.2), -1.0, 1.5),
    }


@jax.custom_vjp
def low(v):
    return lax.optimization_barrier(v.astype(jnp.bfloat16)).astype(jnp.float32)

@jax.custom_vjp
def low_back(v):
    return v

def low_keep(v):
    return (low(v), None)

def low_pass(kept, grad):
    return (grad,)

def back_keep(v):
    return (v, None)

def back_low(kept, grad):
    return (low(grad),)
low.defvjp(low_keep, low_pass)
low_back.defvjp(back_keep, back_low)
norm_eps = 1e-06
clip_limit = 2048.0
learn_rates = (0.03, 0.24, 0.03, 0.03, 0.03, 0.03, 0.03, 0.03, 0.4)
beta_first = 0.9
beta_second = 0.95
weight_decay = 0.02
adam_eps = 1e-08
ema_decay = 0.9999
masked_fill = -1e+30
highest = lax.Precision.HIGHEST

def product(left_side, right_side):
    return jnp.matmul(left_side, right_side, precision=highest)

def layer_norm(values):
    centre = values - lax.optimization_barrier(jnp.mean(values, axis=-1, keepdims=True))
    spread = lax.optimization_barrier(jnp.mean(centre * centre, axis=-1, keepdims=True))
    return centre * lax.rsqrt(spread + norm_eps)

def attend(query_rows, key_rows, value_rows, allowed):
    scores = jnp.einsum('thd,shd->hts', query_rows, key_rows, precision=highest) * HEAD_DIM ** (-0.5)
    scores = low_back(scores)
    scores = jnp.where(allowed[None], scores, masked_fill)
    largest = lax.optimization_barrier(jnp.max(scores, axis=-1, keepdims=True))
    powered = jnp.exp(scores - largest)
    weights = low(powered / lax.optimization_barrier(jnp.sum(powered, axis=-1, keepdims=True)))
    return jnp.einsum('hts,shd->thd', weights, value_rows, precision=highest)

def pair_attention(pieces):
    query_rows, key_rows, value_rows, pair_images = pieces
    visible = attend(query_rows[0], key_rows[0], value_rows[0], pair_images[0][:, None] == pair_images[0][None, :])
    all_keys = jnp.concatenate([key_rows[0], key_rows[1]], axis=0)
    all_values = jnp.concatenate([value_rows[0], value_rows[1]], axis=0)
    all_images = jnp.concatenate([pair_images[0], pair_images[1]], axis=0)
    masked = attend(query_rows[1], all_keys, all_values, pair_images[1][:, None] == all_images[None, :])
    return jnp.stack([visible, masked])

def to_pairs(tensor):
    shaped = tensor.reshape((N_DP, N_SIDE, N_SEQ, TOK_DEV) + tensor.shape[1:])
    moved = jnp.swapaxes(shaped, 1, 2)
    return moved.reshape((N_DP * N_SEQ, N_SIDE, TOK_DEV) + tensor.shape[1:])

def from_pairs(tensor):
    shaped = tensor.reshape((N_DP, N_SEQ, N_SIDE, TOK_DEV) + tensor.shape[3:])
    return jnp.swapaxes(shaped, 1, 2).reshape((TOKENS,) + tensor.shape[3:])

def forward(tokens, head_in, weight_attend, weight_proj, weight_up, weight_down, weight_cond, weight_mod, weight_inner, weight_outer, norm_params, image_ids):
    normed = low(layer_norm(tokens) * norm_params[:, 0] + norm_params[:, 1])
    mixed = low(low_back(product(normed, weight_attend)))
    query_rows = mixed[:, :D].reshape(TOKENS, HEADS, HEAD_DIM)
    key_rows = mixed[:, D:2 * D].reshape(TOKENS, HEADS, HEAD_DIM)
    value_rows = mixed[:, 2 * D:].reshape(TOKENS, HEADS, HEAD_DIM)
    paired = lax.map(jax.checkpoint(pair_attention), (to_pairs(query_rows), to_pairs(key_rows), to_pairs(value_rows), to_pairs(image_ids)))
    attended = low(low_back(from_pairs(paired).reshape(TOKENS, D)))
    hidden = tokens + low_back(product(attended, weight_proj))
    second = low(layer_norm(hidden) * norm_params[:, 2] + norm_params[:, 3])
    inner_pre = low_back(product(second, weight_up))
    activated = low(jax.nn.gelu(inner_pre, approximate=False))
    block_out = low(hidden + low_back(product(activated, weight_down)))
    condition = low_back(product(block_out, weight_cond))
    modulation = low_back(product(low(jax.nn.silu(condition)), weight_mod))
    head_shift = modulation[:, :HW]
    head_scale = modulation[:, HW:2 * HW]
    head_gate = modulation[:, 2 * HW:]
    shaped = low(layer_norm(head_in) * (1.0 + head_scale) + head_shift)
    middle = low_back(product(shaped, weight_inner))
    lifted = low(jax.nn.silu(middle))
    head_out = head_in + head_gate * low_back(product(lifted, weight_outer))
    return (block_out, head_out)

def adam_step(master, gradient, moment, square, decays, rate):
    new_moment = beta_first * moment + (1.0 - beta_first) * gradient
    new_square = beta_second * square + (1.0 - beta_second) * gradient * gradient
    moment_hat = new_moment / (1.0 - beta_first ** STEP)
    square_hat = new_square / (1.0 - beta_second ** STEP)
    shrunk = master * (1.0 - rate * weight_decay * decays)
    return (shrunk - rate * moment_hat / (jnp.sqrt(square_hat) + adam_eps), new_moment, new_square)

def average_factors():
    total = 1.0 - ema_decay ** STEP
    return (ema_decay * (1.0 - ema_decay ** (STEP - 1)) / total, (1.0 - ema_decay) / total)

def reference(tokens, head_in, image_ids, out_cotangent, head_cotangent, weight_attend, weight_proj, weight_up, weight_down, weight_cond, weight_mod, weight_inner, weight_outer, norm_params, mean_attend, mean_proj, mean_up, mean_down, mean_cond, mean_mod, mean_inner, mean_outer, mean_norms, square_attend, square_proj, square_up, square_down, square_cond, square_mod, square_inner, square_outer, square_norms, ema_attend, ema_proj, ema_up, ema_down, ema_cond, ema_mod, ema_inner, ema_outer, ema_norms):
    masters = [weight_attend, weight_proj, weight_up, weight_down, weight_cond, weight_mod, weight_inner, weight_outer, norm_params]
    moments = [mean_attend, mean_proj, mean_up, mean_down, mean_cond, mean_mod, mean_inner, mean_outer, mean_norms]
    squares = [square_attend, square_proj, square_up, square_down, square_cond, square_mod, square_inner, square_outer, square_norms]
    averages = [ema_attend, ema_proj, ema_up, ema_down, ema_cond, ema_mod, ema_inner, ema_outer, ema_norms]
    rounded = [master.astype(jnp.bfloat16).astype(jnp.float32) for master in masters]

    def wrapped(token_rows, head_rows, *params):
        return forward(token_rows, head_rows, *params, image_ids)
    outputs, backward = jax.vjp(wrapped, tokens.astype(jnp.float32), head_in.astype(jnp.float32), *rounded)
    block_out, head_out = outputs
    gradients = backward((out_cotangent.astype(jnp.float32), head_cotangent.astype(jnp.float32)))
    tokens_grad = gradients[0]
    head_in_grad = gradients[1]
    weight_grads = gradients[2:]
    total = sum((jnp.sum(gradient * gradient) for gradient in weight_grads))
    grad_norm = jnp.sqrt(total)
    factor = jnp.minimum(1.0, clip_limit / (grad_norm + 1e-06))
    keep_old, take_new = average_factors()
    results = []
    smoothed = []
    for position in range(9):
        decays = 1.0 if position < 8 else 0.0
        fresh = adam_step(masters[position], weight_grads[position] * factor, moments[position], squares[position], decays, learn_rates[position])
        results.extend(fresh)
        smoothed.append(keep_old * averages[position] + take_new * fresh[0])
    return (block_out.astype(jnp.bfloat16), head_out.astype(jnp.bfloat16), tokens_grad, head_in_grad, grad_norm) + tuple(results) + tuple(smoothed)
```

```python
import jax
import jax.numpy as jnp
from jax import lax
from jax.experimental import pallas as pl
from jax.experimental.pallas import tpu as pltpu
from jax.sharding import PartitionSpec as P

D = 768
HEADS = 12
HEAD_DIM = 64
HW = 1024
STEP = 5


norm_eps = 1e-06
clip_limit = 2048.0
learn_rates = (0.03, 0.24, 0.03, 0.03, 0.03, 0.03, 0.03, 0.03, 0.4)
beta_first = 0.9
beta_second = 0.95
weight_decay = 0.02
adam_eps = 1e-08
ema_decay = 0.9999
masked_fill = -1e30


MESH = pl.DeviceIdType.MESH
AXES = ("dp", "side", "seq")


def places():
    dp, side, seq = (lax.axis_index(name) for name in AXES)
    count = lax.axis_size("seq")
    near = dp + 1 - 2 * lax.rem(dp, 2)
    far = dp + 2 - 4 * (dp // 2)
    along = [lax.rem(seq + step, count) for step in range(1, count)]
    before = [lax.rem(seq + count - step, count) for step in range(1, count)]
    return dp, side, seq, near, far, along, before


def greet(peers):
    barrier = pltpu.get_barrier_semaphore()
    for peer in peers:
        pl.semaphore_signal(barrier, inc=1, device_id=peer, device_id_type=MESH)
    pl.semaphore_wait(barrier, len(peers))


def remote(source, target, send_sem, recv_sem, peer):
    return pltpu.make_async_remote_copy(
        src_ref=source,
        dst_ref=target,
        send_sem=send_sem,
        recv_sem=recv_sem,
        device_id=peer,
        device_id_type=MESH,
    )


class Gather:
    def __init__(self, chunks, masters, fulls, own, slabs, joined, sends, recvs, locs):
        self.chunks, self.masters, self.fulls = chunks, masters, fulls
        self.own, self.slabs, self.joined = own, slabs, joined
        self.sends, self.recvs, self.locs = sends, recvs, locs
        self.dp, self.side, self.seq, self.near, self.far, self.along, self.before = places()
        self.count = len(self.along) + 1
        self.started, self.inside = [], {}

    def rows(self, group, dp, side):
        size = self.count * self.masters[group].shape[0]
        return pl.multiple_of((dp * 2 + side) * size, 16), size

    def packed(self, group):
        return self.masters[group].shape[0] % 16 == 0

    def part(self, chunk, start, size):
        group, first, width = self.chunks[chunk]
        return self.fulls[group].at[pl.ds(pl.multiple_of(start, 16), size), pl.ds(first, width)]

    def send(self, chunk, which, source, target, peer):
        copy = remote(source, target, self.sends.at[chunk, which], self.recvs.at[chunk, which], peer)
        copy.start()
        self.started.append(copy)

    def arrived(self, chunk, which, target, peer):
        remote(target, target, self.sends.at[chunk, which], self.recvs.at[chunk, which], peer).wait_recv()

    def local(self, chunk, source, target):
        copy = pltpu.make_async_copy(source, target, self.locs.at[chunk])
        copy.start()
        self.inside[chunk] = copy

    def cast(self, group):
        rounded = self.masters[group][...].astype(jnp.bfloat16)
        if self.packed(group):
            self.own[group][...] = rounded
        else:
            self.slabs[group][self.seq] = rounded

    def first(self, chunk):
        group, start, width = self.chunks[chunk]
        columns = pl.ds(start, width)
        rows = self.masters[group].shape[0]
        base, _ = self.rows(group, self.dp, self.side)
        for step, peer in enumerate(self.along):
            if self.packed(group):
                source = self.own[group].at[:, columns]
                target = self.part(chunk, base + self.seq * rows, rows)
            else:
                source = target = self.slabs[group].at[self.seq, :, columns]
            self.send(chunk, step, source, target, (self.dp, self.side, peer))
        if self.packed(group):
            self.local(chunk, self.own[group].at[:, columns], self.part(chunk, base + self.seq * rows, rows))

    def second(self, chunk):
        group, start, width = self.chunks[chunk]
        columns = pl.ds(start, width)
        rows = self.masters[group].shape[0]
        base, size = self.rows(group, self.dp, self.side)
        for step, peer in enumerate(self.before):
            if self.packed(group):
                target = self.part(chunk, base + peer * rows, rows)
            else:
                target = self.slabs[group].at[peer, :, columns]
            self.arrived(chunk, step, target, (self.dp, self.side, peer))
        block = self.part(chunk, base, size)
        if self.packed(group):
            self.inside.pop(chunk).wait()
            source = block
        else:
            tile = 256
            joined, slab = self.joined[group], self.slabs[group]

            @pl.loop(0, width // tile)
            def _(at):
                span = pl.ds(pl.multiple_of(start + at * tile, tile), tile)
                stacked = [slab[place, :, span].astype(jnp.float32) for place in range(self.count)]
                joined[:, span] = jnp.concatenate(stacked, axis=0).astype(jnp.bfloat16)

            source = joined.at[:, columns]
            self.local(chunk, source, block)
        last = self.count - 1
        self.send(chunk, last, source, block, (self.near, self.side, self.seq))
        self.send(chunk, last + 1, source, block, (self.far, self.side, self.seq))
        self.send(chunk, last + 4, source, block, (self.dp, 1 - self.side, self.seq))

    def third(self, chunk):
        group = self.chunks[chunk][0]
        last = self.count - 1
        size = self.rows(group, self.dp, self.side)[1]
        half = size // 2
        other = (self.dp, 1 - self.side, self.seq)
        near, far = ((place, self.side, self.seq) for place in (self.near, self.far))
        base = self.rows(group, self.near, self.side)[0]
        block = self.part(chunk, base, size)
        self.arrived(chunk, last, block, near)
        piece = self.part(chunk, base, half)
        self.send(chunk, last + 3, piece, piece, far)
        self.send(chunk, last + 5, block, block, other)
        base = self.rows(group, self.far, self.side)[0]
        block = self.part(chunk, base, size)
        self.arrived(chunk, last + 1, block, far)
        piece = self.part(chunk, base + half, half)
        self.send(chunk, last + 2, piece, piece, near)
        self.send(chunk, last + 6, block, block, other)

    def fourth(self, chunk):
        group = self.chunks[chunk][0]
        last = self.count - 1
        base, size = self.rows(group, 3 - self.dp, self.side)
        half = size // 2
        self.arrived(chunk, last + 3, self.part(chunk, base, half), (self.far, self.side, self.seq))
        self.arrived(chunk, last + 2, self.part(chunk, base + half, half), (self.near, self.side, self.seq))
        block = self.part(chunk, base, size)
        self.send(chunk, last + 7, block, block, (self.dp, 1 - self.side, self.seq))

    def fifth(self, chunk):
        group = self.chunks[chunk][0]
        last = self.count - 1
        other = (self.dp, 1 - self.side, self.seq)
        for which, place in enumerate((self.dp, self.near, self.far, 3 - self.dp)):
            base, size = self.rows(group, place, 1 - self.side)
            self.arrived(chunk, last + 4 + which, self.part(chunk, base, size), other)

    def finish(self):
        for copy in self.started:
            copy.wait_send()
        for copy in self.inside.values():
            copy.wait()


def chunk_list(masters):
    chunks = []
    for group, shape in enumerate(masters):
        rows, width = shape
        step = width
        while rows * step > 32 * 1024 and step % 512 == 0:
            step //= 2
        if rows * step > 32 * 1024 and step % 384 == 0:
            step //= 3
        chunks += [(group, start, step) for start in range(0, width, step)]
    return chunks


def gather_kernel(chunks, *refs):
    masters, fulls = refs[:8], refs[8:16]
    rest = list(refs[16:])
    own, slabs, joined = {}, {}, {}
    for group in range(8):
        if masters[group].shape[0] % 16 == 0:
            own[group] = rest.pop(0)
        else:
            slabs[group] = rest.pop(0)
            joined[group] = rest.pop(0)
    sends, recvs, locs = rest
    dp, side, seq, near, far, along, _ = places()
    peers = [(near, side, seq), (far, side, seq), (dp, 1 - side, seq)]
    greet(peers + [(dp, side, place) for place in along])
    flow = Gather(chunks, masters, fulls, own, slabs, joined, sends, recvs, locs)
    total = len(chunks)
    for step in range(-2, total + 2):
        if 0 <= step + 2 < total:
            group, start, _ = chunks[step + 2]
            if start == 0:
                flow.cast(group)
            flow.first(step + 2)
        if 0 <= step < total:
            flow.second(step)
        if 0 <= step - 1 < total:
            flow.third(step - 1)
        if 0 <= step - 2 < total:
            flow.fourth(step - 2)
            flow.fifth(step - 2)
    flow.finish()


def gather_all(masters):
    devices = lax.axis_size("dp") * lax.axis_size("side") * lax.axis_size("seq")
    count = lax.axis_size("seq")
    chunks = chunk_list([master.shape for master in masters])
    scratch = []
    for master in masters:
        rows, width = master.shape
        if rows % 16 == 0:
            scratch.append(pltpu.VMEM((rows, width), jnp.bfloat16))
        else:
            scratch.append(pltpu.VMEM((count, rows, width), jnp.bfloat16))
            scratch.append(pltpu.VMEM((count * rows, width), jnp.bfloat16))
    total = len(chunks)
    scratch += [
        pltpu.SemaphoreType.DMA((total, count + 7)),
        pltpu.SemaphoreType.DMA((total, count + 7)),
        pltpu.SemaphoreType.DMA((total,)),
    ]
    vmem, anywhere = pl.BlockSpec(memory_space=pltpu.VMEM), pl.BlockSpec(memory_space=pl.ANY)
    return pl.pallas_call(
        lambda *refs: gather_kernel(chunks, *refs),
        out_shape=[
            jax.ShapeDtypeStruct((devices * m.shape[0], m.shape[1]), jnp.bfloat16) for m in masters
        ],
        in_specs=[vmem] * 8,
        out_specs=[anywhere] * 8,
        scratch_shapes=scratch,
        compiler_params=pltpu.CompilerParams(
            collective_id=0, has_side_effects=True, vmem_limit_bytes=48 * 2**20
        ),
        name="gather",
    )(*masters)


def shifted(value, axis, steps):
    count = lax.axis_size(axis)
    first, last = (max(0, -steps), min(count, count - steps))
    return lax.ppermute(value, axis, [(source, source + steps) for source in range(first, last)])


def layer_norm(values):
    centre = values - jnp.mean(values, axis=-1, keepdims=True)
    spread = jnp.mean(centre * centre, axis=-1, keepdims=True)
    return centre * lax.rsqrt(spread + norm_eps)


def scaled_norm(values, norm_gain, norm_bias):
    return layer_norm(values) * norm_gain + norm_bias


def modulated(values, head_shift, head_scale):
    return layer_norm(values) * (1.0 + head_scale) + head_shift


def gelu_exact(values):
    return jax.nn.gelu(values, approximate=False)


def matmul(left_side, right_side):
    return jnp.dot(left_side, right_side, preferred_element_type=jnp.float32)


def matmul_left(left_side, right_side):
    return lax.dot_general(
        left_side, right_side, (((0,), (0,)), ((), ())), preferred_element_type=jnp.float32
    )


def matmul_right(left_side, right_side):
    return lax.dot_general(
        left_side, right_side, (((1,), (1,)), ((), ())), preferred_element_type=jnp.float32
    )


def split_heads(tensor):
    return tensor.reshape(tensor.shape[0], HEADS, HEAD_DIM).transpose(1, 0, 2)


def join_heads(tensor):
    return tensor.transpose(1, 0, 2).reshape(tensor.shape[1], HEADS * HEAD_DIM)


def head_forward(stacked, allowed):
    query_rows, key_rows, value_rows = stacked
    scores = jnp.where(
        allowed, matmul_right(query_rows, key_rows) * HEAD_DIM ** (-0.5), masked_fill
    )
    largest = jnp.max(scores, axis=1, keepdims=True)
    powered = jnp.exp(scores - largest)
    totals = jnp.sum(powered, axis=1, keepdims=True)
    weights = (powered / totals).astype(jnp.bfloat16)
    attended = matmul(weights, value_rows).astype(jnp.bfloat16)
    return (attended, (largest + jnp.log(totals))[:, 0])


def head_backward(stacked, allowed):
    query_rows, key_rows, value_rows, log_total, grad_rows = stacked
    scores = jnp.where(
        allowed, matmul_right(query_rows, key_rows) * HEAD_DIM ** (-0.5), masked_fill
    )
    weights = jnp.exp(scores - log_total[:, None])
    grad_weights = matmul_right(grad_rows, value_rows)
    row_inner = jnp.sum(weights * grad_weights, axis=1, keepdims=True)
    grad_scores = (weights * (grad_weights - row_inner)).astype(jnp.bfloat16)
    grad_query = matmul(grad_scores, key_rows) * HEAD_DIM ** (-0.5)
    grad_keys = matmul_left(grad_scores, query_rows) * HEAD_DIM ** (-0.5)
    grad_values = matmul_left(weights.astype(jnp.bfloat16), grad_rows)
    return (grad_query, grad_keys, grad_values)


def adam_step(master, gradient, moment, square, decays, rate):
    new_moment = beta_first * moment + (1.0 - beta_first) * gradient
    new_square = beta_second * square + (1.0 - beta_second) * gradient * gradient
    moment_hat = new_moment / (1.0 - beta_first**STEP)
    square_hat = new_square / (1.0 - beta_second**STEP)
    shrunk = master * (1.0 - rate * weight_decay * decays)
    return (shrunk - rate * moment_hat / (jnp.sqrt(square_hat) + adam_eps), new_moment, new_square)


def average_factors():
    total = 1.0 - ema_decay**STEP
    return (ema_decay * (1.0 - ema_decay ** (STEP - 1)) / total, (1.0 - ema_decay) / total)


def body(
    tokens,
    head_in,
    image_ids,
    out_cotangent,
    head_cotangent,
    weight_attend,
    weight_proj,
    weight_up,
    weight_down,
    weight_cond,
    weight_mod,
    weight_inner,
    weight_outer,
    norm_params,
    mean_attend,
    mean_proj,
    mean_up,
    mean_down,
    mean_cond,
    mean_mod,
    mean_inner,
    mean_outer,
    mean_norms,
    square_attend,
    square_proj,
    square_up,
    square_down,
    square_cond,
    square_mod,
    square_inner,
    square_outer,
    square_norms,
    ema_attend,
    ema_proj,
    ema_up,
    ema_down,
    ema_cond,
    ema_mod,
    ema_inner,
    ema_outer,
    ema_norms,
):
    masters = (
        weight_attend,
        weight_proj,
        weight_up,
        weight_down,
        weight_cond,
        weight_mod,
        weight_inner,
        weight_outer,
    )
    if lax.axis_size("dp") == 4 and lax.axis_size("side") == 2 and weight_attend.shape[0] % 8 == 0:
        gathered = gather_all(masters)
    else:
        gathered = [
            lax.all_gather(master.astype(jnp.bfloat16), AXES, axis=0, tiled=True)
            for master in masters
        ]
    use_attend, use_proj, use_up, use_down, use_cond, use_mod, use_inner, use_outer = gathered
    use_norms = lax.all_gather(norm_params.astype(jnp.bfloat16), AXES, axis=0, tiled=True)
    norm_set = use_norms.astype(jnp.float32)
    inputs = tokens.astype(jnp.float32)
    row_count = tokens.shape[0]
    normed, first_back = jax.vjp(scaled_norm, inputs, norm_set[:, 0], norm_set[:, 1])
    normed_low = normed.astype(jnp.bfloat16)
    mixed_rows = matmul(normed_low, use_attend).astype(jnp.bfloat16)
    query_heads = split_heads(mixed_rows[:, :D])
    own_keys = split_heads(mixed_rows[:, D : 2 * D])
    own_values = split_heads(mixed_rows[:, 2 * D :])
    own_images = image_ids.astype(jnp.bfloat16)
    far_pair, far_images = shifted((mixed_rows[:, D:], own_images), "side", 1)
    both_keys = jnp.concatenate([split_heads(far_pair[:, :D]), own_keys], axis=1)
    both_values = jnp.concatenate([split_heads(far_pair[:, D:]), own_values], axis=1)
    near_allowed = own_images[:, None] == own_images[None, :]
    wide_allowed = own_images[:, None] == jnp.concatenate([far_images, own_images])[None, :]
    masked_side = lax.axis_index("side") == 1

    def visible_forward():
        return lax.map(
            lambda stacked: head_forward(stacked, near_allowed), (query_heads, own_keys, own_values)
        )

    def masked_forward():
        return lax.map(
            lambda stacked: head_forward(stacked, wide_allowed),
            (query_heads, both_keys, both_values),
        )

    attended_heads, log_totals = lax.cond(masked_side, masked_forward, visible_forward)
    attended = join_heads(attended_heads)
    hidden = inputs + matmul(attended, use_proj)
    second, second_back = jax.vjp(scaled_norm, hidden, norm_set[:, 2], norm_set[:, 3])
    second_low = second.astype(jnp.bfloat16)
    inner_pre = matmul(second_low, use_up)
    activated_full, gelu_back = jax.vjp(gelu_exact, inner_pre)
    activated = activated_full.astype(jnp.bfloat16)
    block_low = (hidden + matmul(activated, use_down)).astype(jnp.bfloat16)
    condition = matmul(block_low, use_cond)
    lifted_cond, cond_back = jax.vjp(jax.nn.silu, condition)
    cond_low = lifted_cond.astype(jnp.bfloat16)
    modulation = matmul(cond_low, use_mod)
    head_shift = modulation[:, :HW]
    head_scale = modulation[:, HW : 2 * HW]
    head_gate = modulation[:, 2 * HW :]
    head_rows = head_in.astype(jnp.float32)
    shaped, shaped_back = jax.vjp(modulated, head_rows, head_shift, head_scale)
    shaped_low = shaped.astype(jnp.bfloat16)
    middle = matmul(shaped_low, use_inner)
    lifted_full, middle_back = jax.vjp(jax.nn.silu, middle)
    lifted_rows = lifted_full.astype(jnp.bfloat16)
    branch = matmul(lifted_rows, use_outer)
    head_out = (head_rows + head_gate * branch).astype(jnp.bfloat16)
    head_grad = head_cotangent.astype(jnp.float32)
    grad_branch = (head_grad * head_gate).astype(jnp.bfloat16)
    grad_outer = matmul_left(lifted_rows, grad_branch)
    grad_middle = middle_back(matmul_right(grad_branch, use_outer))[0].astype(jnp.bfloat16)
    grad_inner = matmul_left(shaped_low, grad_middle)
    head_part, grad_shift, grad_scale = shaped_back(matmul_right(grad_middle, use_inner))
    head_in_grad = head_grad + head_part
    grad_modulation = jnp.concatenate([grad_shift, grad_scale, head_grad * branch], axis=1).astype(
        jnp.bfloat16
    )
    grad_mod = matmul_left(cond_low, grad_modulation)
    grad_condition = cond_back(matmul_right(grad_modulation, use_mod))[0].astype(jnp.bfloat16)
    grad_cond = matmul_left(block_low, grad_condition)
    grad_block = out_cotangent.astype(jnp.float32) + matmul_right(grad_condition, use_cond)
    grad_feed = grad_block.astype(jnp.bfloat16)
    grad_down = matmul_left(activated, grad_feed)
    grad_inner_pre = gelu_back(matmul_right(grad_feed, use_down))[0].astype(jnp.bfloat16)
    grad_up = matmul_left(second_low, grad_inner_pre)
    hidden_part, grad_gain_two, grad_bias_two = second_back(matmul_right(grad_inner_pre, use_up))
    grad_hidden = grad_block + hidden_part
    grad_proj_out = grad_hidden.astype(jnp.bfloat16)
    grad_proj = matmul_left(attended, grad_proj_out)
    grad_attended = split_heads(matmul_right(grad_proj_out, use_proj).astype(jnp.bfloat16))

    def visible_backward():
        grad_query, grad_keys, grad_values = lax.map(
            lambda stacked: head_backward(stacked, near_allowed),
            (query_heads, own_keys, own_values, log_totals, grad_attended),
        )
        zero_fill = jnp.zeros_like(grad_keys)
        return (
            grad_query,
            jnp.concatenate([zero_fill, grad_keys], axis=1),
            jnp.concatenate([zero_fill, grad_values], axis=1),
        )

    def masked_backward():
        return lax.map(
            lambda stacked: head_backward(stacked, wide_allowed),
            (query_heads, both_keys, both_values, log_totals, grad_attended),
        )

    grad_query, grad_keys, grad_values = lax.cond(masked_side, masked_backward, visible_backward)
    far_grad = jnp.concatenate(
        [join_heads(grad_keys[:, :row_count]), join_heads(grad_values[:, :row_count])], axis=1
    )
    returned = shifted(far_grad.astype(jnp.bfloat16), "side", -1).astype(far_grad.dtype)
    near_grad = (
        jnp.concatenate(
            [join_heads(grad_keys[:, row_count:]), join_heads(grad_values[:, row_count:])], axis=1
        )
        + returned
    )
    grad_mixed = jnp.concatenate([join_heads(grad_query), near_grad], axis=1).astype(jnp.bfloat16)
    grad_attend = matmul_left(normed_low, grad_mixed)
    tokens_part, grad_gain_one, grad_bias_one = first_back(matmul_right(grad_mixed, use_attend))
    tokens_grad = grad_hidden + tokens_part
    grad_norms = jnp.stack([grad_gain_one, grad_bias_one, grad_gain_two, grad_bias_two], axis=1)
    owned = (
        lax.psum_scatter(grad_attend, ("dp", "side", "seq"), scatter_dimension=0, tiled=True),
        lax.psum_scatter(grad_proj, ("dp", "side", "seq"), scatter_dimension=0, tiled=True),
        lax.psum_scatter(grad_up, ("dp", "side", "seq"), scatter_dimension=0, tiled=True),
        lax.psum_scatter(grad_down, ("dp", "side", "seq"), scatter_dimension=0, tiled=True),
        lax.psum_scatter(grad_cond, ("dp", "side", "seq"), scatter_dimension=0, tiled=True),
        lax.psum_scatter(grad_mod, ("dp", "side", "seq"), scatter_dimension=0, tiled=True),
        lax.psum_scatter(grad_inner, ("dp", "side", "seq"), scatter_dimension=0, tiled=True),
        lax.psum_scatter(grad_outer, ("dp", "side", "seq"), scatter_dimension=0, tiled=True),
        lax.psum_scatter(grad_norms, ("dp", "side", "seq"), scatter_dimension=0, tiled=True),
    )
    local_squares = sum((jnp.sum(gradient * gradient) for gradient in owned))
    grad_norm = jnp.sqrt(lax.psum(local_squares, ("dp", "side", "seq")))
    factor = jnp.minimum(1.0, clip_limit / (grad_norm + 1e-06))
    masters = [
        weight_attend,
        weight_proj,
        weight_up,
        weight_down,
        weight_cond,
        weight_mod,
        weight_inner,
        weight_outer,
        norm_params,
    ]
    moments = [
        mean_attend,
        mean_proj,
        mean_up,
        mean_down,
        mean_cond,
        mean_mod,
        mean_inner,
        mean_outer,
        mean_norms,
    ]
    squares = [
        square_attend,
        square_proj,
        square_up,
        square_down,
        square_cond,
        square_mod,
        square_inner,
        square_outer,
        square_norms,
    ]
    averages = [
        ema_attend,
        ema_proj,
        ema_up,
        ema_down,
        ema_cond,
        ema_mod,
        ema_inner,
        ema_outer,
        ema_norms,
    ]
    keep_old, take_new = average_factors()
    results = []
    smoothed = []
    for position in range(9):
        decays = 1.0 if position < 8 else 0.0
        fresh = adam_step(
            masters[position],
            owned[position] * factor,
            moments[position],
            squares[position],
            decays,
            learn_rates[position],
        )
        results.extend(fresh)
        smoothed.append(keep_old * averages[position] + take_new * fresh[0])
    return (
        (block_low, head_out, tokens_grad, head_in_grad, grad_norm)
        + tuple(results)
        + tuple(smoothed)
    )


def solution(mesh):
    in_specs = (
        P(("dp", "side", "seq"), None),
        P(("dp", "side", "seq"), None),
        P(("dp", "side", "seq")),
        P(("dp", "side", "seq"), None),
        P(("dp", "side", "seq"), None),
        P(("dp", "side", "seq"), None),
        P(("dp", "side", "seq"), None),
        P(("dp", "side", "seq"), None),
        P(("dp", "side", "seq"), None),
        P(("dp", "side", "seq"), None),
        P(("dp", "side", "seq"), None),
        P(("dp", "side", "seq"), None),
        P(("dp", "side", "seq"), None),
        P(("dp", "side", "seq"), None),
        P(("dp", "side", "seq"), None),
        P(("dp", "side", "seq"), None),
        P(("dp", "side", "seq"), None),
        P(("dp", "side", "seq"), None),
        P(("dp", "side", "seq"), None),
        P(("dp", "side", "seq"), None),
        P(("dp", "side", "seq"), None),
        P(("dp", "side", "seq"), None),
        P(("dp", "side", "seq"), None),
        P(("dp", "side", "seq"), None),
        P(("dp", "side", "seq"), None),
        P(("dp", "side", "seq"), None),
        P(("dp", "side", "seq"), None),
        P(("dp", "side", "seq"), None),
        P(("dp", "side", "seq"), None),
        P(("dp", "side", "seq"), None),
        P(("dp", "side", "seq"), None),
        P(("dp", "side", "seq"), None),
        P(("dp", "side", "seq"), None),
        P(("dp", "side", "seq"), None),
        P(("dp", "side", "seq"), None),
        P(("dp", "side", "seq"), None),
        P(("dp", "side", "seq"), None),
        P(("dp", "side", "seq"), None),
        P(("dp", "side", "seq"), None),
        P(("dp", "side", "seq"), None),
        P(("dp", "side", "seq"), None),
    )
    out_specs = (
        P(("dp", "side", "seq"), None),
        P(("dp", "side", "seq"), None),
        P(("dp", "side", "seq"), None),
        P(("dp", "side", "seq"), None),
        P(),
        P(("dp", "side", "seq"), None),
        P(("dp", "side", "seq"), None),
        P(("dp", "side", "seq"), None),
        P(("dp", "side", "seq"), None),
        P(("dp", "side", "seq"), None),
        P(("dp", "side", "seq"), None),
        P(("dp", "side", "seq"), None),
        P(("dp", "side", "seq"), None),
        P(("dp", "side", "seq"), None),
        P(("dp", "side", "seq"), None),
        P(("dp", "side", "seq"), None),
        P(("dp", "side", "seq"), None),
        P(("dp", "side", "seq"), None),
        P(("dp", "side", "seq"), None),
        P(("dp", "side", "seq"), None),
        P(("dp", "side", "seq"), None),
        P(("dp", "side", "seq"), None),
        P(("dp", "side", "seq"), None),
        P(("dp", "side", "seq"), None),
        P(("dp", "side", "seq"), None),
        P(("dp", "side", "seq"), None),
        P(("dp", "side", "seq"), None),
        P(("dp", "side", "seq"), None),
        P(("dp", "side", "seq"), None),
        P(("dp", "side", "seq"), None),
        P(("dp", "side", "seq"), None),
        P(("dp", "side", "seq"), None),
        P(("dp", "side", "seq"), None),
        P(("dp", "side", "seq"), None),
        P(("dp", "side", "seq"), None),
        P(("dp", "side", "seq"), None),
        P(("dp", "side", "seq"), None),
        P(("dp", "side", "seq"), None),
        P(("dp", "side", "seq"), None),
        P(("dp", "side", "seq"), None),
        P(("dp", "side", "seq"), None),
    )
    return jax.shard_map(body, mesh=mesh, in_specs=in_specs, out_specs=out_specs, check_vma=False)
```

```python
import functools
from types import SimpleNamespace

import jax
import jax.numpy as jnp
from jax import lax
from jax.experimental import pallas as pl
from jax.experimental.pallas import tpu as pltpu
from jax.sharding import PartitionSpec as P

D = 768
HEADS = 12
HEAD_DIM = 64
HW = 1024
STEP = 5


norm_eps = 1e-06
clip_limit = 2048.0
learn_rates = (0.03, 0.24, 0.03, 0.03, 0.03, 0.03, 0.03, 0.03, 0.4)
beta_first = 0.9
beta_second = 0.95
weight_decay = 0.02
adam_eps = 1e-08
ema_decay = 0.9999
masked_fill = -1e30

MESH = pl.DeviceIdType.MESH
AXES = ("dp", "side", "seq")


def places():
    dp, side, seq = (lax.axis_index(name) for name in AXES)
    count = lax.axis_size("seq")
    near = dp + 1 - 2 * lax.rem(dp, 2)
    far = dp + 2 - 4 * (dp // 2)
    along = [lax.rem(seq + step, count) for step in range(1, count)]
    before = [lax.rem(seq + count - step, count) for step in range(1, count)]
    return dp, side, seq, near, far, along, before


def greet(peers):
    barrier = pltpu.get_barrier_semaphore()
    for peer in peers:
        pl.semaphore_signal(barrier, inc=1, device_id=peer, device_id_type=MESH)
    pl.semaphore_wait(barrier, len(peers))


def remote(source, target, send_sem, recv_sem, peer):
    return pltpu.make_async_remote_copy(
        src_ref=source,
        dst_ref=target,
        send_sem=send_sem,
        recv_sem=recv_sem,
        device_id=peer,
        device_id_type=MESH,
    )


class Gather:
    def __init__(self, chunks, masters, fulls, own, slabs, joined, sends, recvs, locs):
        self.chunks, self.masters, self.fulls = chunks, masters, fulls
        self.own, self.slabs, self.joined = own, slabs, joined
        self.sends, self.recvs, self.locs = sends, recvs, locs
        self.dp, self.side, self.seq, self.near, self.far, self.along, self.before = places()
        self.count = len(self.along) + 1
        self.started, self.inside = [], {}

    def rows(self, group, dp, side):
        size = self.count * self.masters[group].shape[0]
        return pl.multiple_of((dp * 2 + side) * size, 16), size

    def packed(self, group):
        return self.masters[group].shape[0] % 16 == 0

    def part(self, chunk, start, size):
        group, first, width = self.chunks[chunk]
        return self.fulls[group].at[pl.ds(pl.multiple_of(start, 16), size), pl.ds(first, width)]

    def send(self, chunk, which, source, target, peer):
        copy = remote(source, target, self.sends.at[chunk, which], self.recvs.at[chunk, which], peer)
        copy.start()
        self.started.append(copy)

    def arrived(self, chunk, which, target, peer):
        remote(target, target, self.sends.at[chunk, which], self.recvs.at[chunk, which], peer).wait_recv()

    def local(self, chunk, source, target):
        copy = pltpu.make_async_copy(source, target, self.locs.at[chunk])
        copy.start()
        self.inside[chunk] = copy

    def cast(self, group):
        rounded = self.masters[group][...].astype(jnp.bfloat16)
        if self.packed(group):
            self.own[group][...] = rounded
        else:
            self.slabs[group][self.seq] = rounded

    def first(self, chunk):
        group, start, width = self.chunks[chunk]
        columns = pl.ds(start, width)
        rows = self.masters[group].shape[0]
        base, _ = self.rows(group, self.dp, self.side)
        for step, peer in enumerate(self.along):
            if self.packed(group):
                source = self.own[group].at[:, columns]
                target = self.part(chunk, base + self.seq * rows, rows)
            else:
                source = target = self.slabs[group].at[self.seq, :, columns]
            self.send(chunk, step, source, target, (self.dp, self.side, peer))
        if self.packed(group):
            self.local(chunk, self.own[group].at[:, columns], self.part(chunk, base + self.seq * rows, rows))

    def second(self, chunk):
        group, start, width = self.chunks[chunk]
        columns = pl.ds(start, width)
        rows = self.masters[group].shape[0]
        base, size = self.rows(group, self.dp, self.side)
        for step, peer in enumerate(self.before):
            if self.packed(group):
                target = self.part(chunk, base + peer * rows, rows)
            else:
                target = self.slabs[group].at[peer, :, columns]
            self.arrived(chunk, step, target, (self.dp, self.side, peer))
        block = self.part(chunk, base, size)
        if self.packed(group):
            self.inside.pop(chunk).wait()
            source = block
        else:
            tile = 256
            joined, slab = self.joined[group], self.slabs[group]

            @pl.loop(0, width // tile)
            def _(at):
                span = pl.ds(pl.multiple_of(start + at * tile, tile), tile)
                stacked = [slab[place, :, span].astype(jnp.float32) for place in range(self.count)]
                joined[:, span] = jnp.concatenate(stacked, axis=0).astype(jnp.bfloat16)

            source = joined.at[:, columns]
            self.local(chunk, source, block)
        last = self.count - 1
        self.send(chunk, last, source, block, (self.near, self.side, self.seq))
        self.send(chunk, last + 1, source, block, (self.far, self.side, self.seq))
        self.send(chunk, last + 4, source, block, (self.dp, 1 - self.side, self.seq))

    def third(self, chunk):
        group = self.chunks[chunk][0]
        last = self.count - 1
        size = self.rows(group, self.dp, self.side)[1]
        half = size // 2
        other = (self.dp, 1 - self.side, self.seq)
        near, far = ((place, self.side, self.seq) for place in (self.near, self.far))
        base = self.rows(group, self.near, self.side)[0]
        block = self.part(chunk, base, size)
        self.arrived(chunk, last, block, near)
        piece = self.part(chunk, base, half)
        self.send(chunk, last + 3, piece, piece, far)
        self.send(chunk, last + 5, block, block, other)
        base = self.rows(group, self.far, self.side)[0]
        block = self.part(chunk, base, size)
        self.arrived(chunk, last + 1, block, far)
        piece = self.part(chunk, base + half, half)
        self.send(chunk, last + 2, piece, piece, near)
        self.send(chunk, last + 6, block, block, other)

    def fourth(self, chunk):
        group = self.chunks[chunk][0]
        last = self.count - 1
        base, size = self.rows(group, 3 - self.dp, self.side)
        half = size // 2
        self.arrived(chunk, last + 3, self.part(chunk, base, half), (self.far, self.side, self.seq))
        self.arrived(chunk, last + 2, self.part(chunk, base + half, half), (self.near, self.side, self.seq))
        block = self.part(chunk, base, size)
        self.send(chunk, last + 7, block, block, (self.dp, 1 - self.side, self.seq))

    def fifth(self, chunk):
        group = self.chunks[chunk][0]
        last = self.count - 1
        other = (self.dp, 1 - self.side, self.seq)
        for which, place in enumerate((self.dp, self.near, self.far, 3 - self.dp)):
            base, size = self.rows(group, place, 1 - self.side)
            self.arrived(chunk, last + 4 + which, self.part(chunk, base, size), other)

    def finish(self):
        for copy in self.started:
            copy.wait_send()
        for copy in self.inside.values():
            copy.wait()


def chunk_list(masters):
    chunks = []
    for group, shape in enumerate(masters):
        rows, width = shape
        step = width
        while rows * step > 32 * 1024 and step % 512 == 0:
            step //= 2
        if rows * step > 32 * 1024 and step % 384 == 0:
            step //= 3
        chunks += [(group, start, step) for start in range(0, width, step)]
    return chunks


def shifted(value, axis, steps):
    count = lax.axis_size(axis)
    first, last = (max(0, -steps), min(count, count - steps))
    return lax.ppermute(value, axis, [(source, source + steps) for source in range(first, last)])


def layer_norm(values):
    centre = values - jnp.mean(values, axis=-1, keepdims=True)
    spread = jnp.mean(centre * centre, axis=-1, keepdims=True)
    return centre * lax.rsqrt(spread + norm_eps)


def scaled_norm(values, norm_gain, norm_bias):
    return layer_norm(values) * norm_gain + norm_bias


def modulated(values, head_shift, head_scale):
    return layer_norm(values) * (1.0 + head_scale) + head_shift


def gelu_exact(values):
    return jax.nn.gelu(values, approximate=False)


def matmul(left_side, right_side):
    return jnp.dot(left_side, right_side, preferred_element_type=jnp.float32)


def matmul_left(left_side, right_side):
    return lax.dot_general(
        left_side, right_side, (((0,), (0,)), ((), ())), preferred_element_type=jnp.float32
    )


def matmul_right(left_side, right_side):
    return lax.dot_general(
        left_side, right_side, (((1,), (1,)), ((), ())), preferred_element_type=jnp.float32
    )


def split_heads(tensor):
    return tensor.reshape(tensor.shape[0], HEADS, HEAD_DIM).transpose(1, 0, 2)


def join_heads(tensor):
    return tensor.transpose(1, 0, 2).reshape(tensor.shape[1], HEADS * HEAD_DIM)


def head_forward(stacked, allowed):
    query_rows, key_rows, value_rows = stacked
    scores = jnp.where(
        allowed, matmul_right(query_rows, key_rows) * HEAD_DIM ** (-0.5), masked_fill
    )
    largest = jnp.max(scores, axis=1, keepdims=True)
    powered = jnp.exp(scores - largest)
    totals = jnp.sum(powered, axis=1, keepdims=True)
    weights = (powered / totals).astype(jnp.bfloat16)
    attended = matmul(weights, value_rows).astype(jnp.bfloat16)
    return (attended, (largest + jnp.log(totals))[:, 0])


def head_backward(stacked, allowed):
    query_rows, key_rows, value_rows, log_total, grad_rows = stacked
    scores = jnp.where(
        allowed, matmul_right(query_rows, key_rows) * HEAD_DIM ** (-0.5), masked_fill
    )
    weights = jnp.exp(scores - log_total[:, None])
    grad_weights = matmul_right(grad_rows, value_rows)
    row_inner = jnp.sum(weights * grad_weights, axis=1, keepdims=True)
    grad_scores = (weights * (grad_weights - row_inner)).astype(jnp.bfloat16)
    grad_query = matmul(grad_scores, key_rows) * HEAD_DIM ** (-0.5)
    grad_keys = matmul_left(grad_scores, query_rows) * HEAD_DIM ** (-0.5)
    grad_values = matmul_left(weights.astype(jnp.bfloat16), grad_rows)
    return (grad_query, grad_keys, grad_values)


def adam_step(master, gradient, moment, square, decays, rate):
    new_moment = beta_first * moment + (1.0 - beta_first) * gradient
    new_square = beta_second * square + (1.0 - beta_second) * gradient * gradient
    moment_hat = new_moment / (1.0 - beta_first**STEP)
    square_hat = new_square / (1.0 - beta_second**STEP)
    shrunk = master * (1.0 - rate * weight_decay * decays)
    return (shrunk - rate * moment_hat / (jnp.sqrt(square_hat) + adam_eps), new_moment, new_square)


def average_factors():
    total = 1.0 - ema_decay**STEP
    return (ema_decay * (1.0 - ema_decay ** (STEP - 1)) / total, (1.0 - ema_decay) / total)


def norm_rows(values):
    centre = values - jnp.mean(values, axis=-1, keepdims=True)
    spread = jnp.mean(centre * centre, axis=-1, keepdims=True)
    scale = lax.rsqrt(spread + norm_eps)
    return centre * scale, scale


def span(at, size):
    return pl.ds(pl.multiple_of(at * size, size), size)


class Moves:
    def __init__(self, sems):
        self.sems, self.used, self.open = sems, 0, []

    def start(self, source, target):
        copy = pltpu.make_async_copy(source, target, self.sems.at[self.used])
        self.used += 1
        copy.start()
        self.open.append(copy)
        return copy

    def finish(self):
        for copy in self.open:
            copy.wait()
        self.open = []


class Swaps:
    def __init__(self, sends, recvs):
        self.sends, self.recvs, self.used, self.open = sends, recvs, 0, []

    def start(self, source, target, peer):
        copy = remote(source, target, self.sends.at[self.used], self.recvs.at[self.used], peer)
        self.used += 1
        copy.start()
        self.open.append(copy)
        return copy

    def finish(self):
        for copy in self.open:
            copy.wait_send()
        self.open = []


def relative(dp, near, far):
    return (dp, near, far, 3 - dp)


class LineSum:
    def __init__(self, box, swaps):
        self.box, self.swaps = box, swaps
        dp, side, seq, near, far, along, _ = places()
        self.count = len(along) + 1
        self.spots = (seq, self.count + dp * 2 + side)
        self.hops = (
            [(dp, side, place) for place in along],
            [(place, side, seq) for place in (near, far, 3 - dp)]
            + [(place, 1 - side, seq) for place in (dp, near, far, 3 - dp)],
        )
        self.waiting = []
        self.level = 0

    def launch(self, value):
        spot = self.spots[self.level]
        self.box[spot] = value
        for peer in self.hops[self.level]:
            self.waiting.append(self.swaps.start(self.box.at[spot], self.box.at[spot], peer))

    def land(self):
        for copy in self.waiting:
            copy.wait_recv()
        first, size = ((0, self.count), (self.count, 8))[self.level]
        total = self.box[first]
        for place in range(first + 1, first + size):
            total = total + self.box[place]
        self.waiting = []
        self.level += 1
        return total


def all_peers():
    dp, side, seq, near, far, along, _ = places()
    peers = [(place, side, seq) for place in (near, far, 3 - dp)]
    peers += [(place, 1 - side, seq) for place in (dp, near, far, 3 - dp)]
    return peers + [(dp, side, place) for place in along]


AHEAD_SEQ = 2
AHEAD_DP = 0
TASKS = 3


FORWARD_OUT = (
    ("block_low", D, jnp.bfloat16),
    ("head_out", HW, jnp.bfloat16),
    ("grad_branch", HW, jnp.bfloat16),
    ("grad_gate", HW, jnp.bfloat16),
    ("scale", HW, jnp.float32),
    ("slope_middle", HW, jnp.bfloat16),
    ("slope_cond", HW, jnp.bfloat16),
    ("slope_inner", 4 * D, jnp.bfloat16),
    ("hidden", D, jnp.float32),
    ("mixed", 3 * D, jnp.bfloat16),
    ("far_pair", 2 * D, jnp.bfloat16),
)
FORWARD_LOCAL = (
    ("normed", D, jnp.bfloat16),
    ("attended", D, jnp.bfloat16),
    ("second", D, jnp.bfloat16),
    ("activated", 4 * D, jnp.bfloat16),
    ("cond_low", HW, jnp.bfloat16),
    ("shift", HW, jnp.float32),
    ("gate", HW, jnp.float32),
    ("head_norm", HW, jnp.float32),
    ("shaped", HW, jnp.bfloat16),
    ("lifted", HW, jnp.bfloat16),
)


def head_mask(which):
    lane = lax.broadcasted_iota(jnp.int32, (1, 2 * HEAD_DIM), 1)
    inside = lane < HEAD_DIM if which == 0 else lane >= HEAD_DIM
    return jnp.where(inside, 1.0, 0.0).astype(jnp.bfloat16)


def softmax_columns(keys, queries, bias):
    scores = matmul_right(keys, queries) * HEAD_DIM ** (-0.5) + bias
    powered = jnp.exp(scores - jnp.max(scores, axis=0, keepdims=True))
    return powered / jnp.sum(powered, axis=0, keepdims=True)


def fill_bias(bias, far_row, own_row, side):
    rows = own_row.shape[-1]
    row = own_row[0:1, :]

    def column(ref):
        return jnp.broadcast_to(ref[0:1, :], (128, rows)).T[:, 0:1]

    near = column(own_row) == row
    wide = jnp.logical_and(column(far_row) == row, side == 1)
    bias[pl.ds(0, rows), :] = jnp.where(wide, 0.0, masked_fill)
    bias[pl.ds(rows, rows), :] = jnp.where(near, 0.0, masked_fill)


def pair_slices(mixed, far_pair, at):
    width = 2 * HEAD_DIM
    queries = mixed[:, span(at, width)]
    second = span(at + D // width, width)
    third = span(at + 2 * (D // width), width)
    keys = jnp.concatenate([far_pair[:, span(at, width)], mixed[:, second]], axis=0)
    values = jnp.concatenate([far_pair[:, second], mixed[:, third]], axis=0)
    return queries, keys, values


def forward_kernel(chunks, count, *refs):
    rest = list(refs)

    def take(number):
        taken = rest[:number]
        del rest[:number]
        return taken

    masters = take(8)
    tokens, head_in, head_cotangent, ids, norm_rows_own = take(5)
    fulls, sides = take(8), take(8)
    outs = dict(zip([name for name, _, _ in FORWARD_OUT], take(len(FORWARD_OUT))))
    bias_out, norms_out = take(2)
    weights = take(8)
    v = SimpleNamespace(**dict(zip([name for name, _, _ in FORWARD_OUT + FORWARD_LOCAL], take(21))))
    bias, own_row, far_row, box, norms = take(5)
    turned = take(3)
    own, slabs, joined = {}, {}, {}
    for group in range(8):
        if masters[group].shape[0] % 16 == 0:
            own[group] = rest.pop(0)
        else:
            slabs[group] = rest.pop(0)
            joined[group] = rest.pop(0)
    sends, recvs, locs, loads, moves_sem, swap_send, swap_recv, turn_sem, turn_send, turn_recv = rest

    dp, side, seq, near, far, along, _ = places()
    other = (dp, 1 - side, seq)
    greet(all_peers())
    flow = Gather(chunks, masters, fulls, own, slabs, joined, sends, recvs, locs)
    moves = Moves(moves_sem)
    swaps = Swaps(swap_send, swap_recv)
    line = LineSum(box, swaps)
    place = (dp * 2 + side) * count + seq
    width = norm_rows_own.shape[1]
    norms[...] = jnp.zeros(norms.shape, jnp.float32)
    norms[0:4, 0:width] = norm_rows_own[...].astype(jnp.bfloat16).astype(jnp.float32)
    spread = pltpu.roll(norms[...], place * width, 1)
    own_row[...] = jnp.broadcast_to(ids[...], own_row.shape).astype(jnp.float32)
    rows = tokens.shape[0]
    loading = {}
    turning = {0: [], 1: [], 2: []}
    landing = []

    def load(chunk):
        group, start, width = chunks[chunk]
        columns = pl.ds(start, width)
        if chunk in flow.inside:
            flow.inside.pop(chunk).wait()
        copy = pltpu.make_async_copy(
            fulls[group].at[:, columns], weights[group].at[:, columns], loads.at[chunk]
        )
        copy.start()
        loading[chunk] = copy

    def put(name):
        moves.start(getattr(v, name), outs[name])

    def share(group, source, which, done=False):
        depth = source.shape[0] if done else source.shape[1]
        buffer = turned[which]
        if not done:
            free(which)

            @pl.loop(0, depth // 256)
            def _(at):
                buffer[span(at, 256), :] = source[:, span(at, 256)].T

        size = depth // 8
        for place, block in enumerate(relative(dp, near, far)):
            mine = pl.multiple_of((block * 2 + side) * size, 16)
            theirs = pl.multiple_of((block * 2 + 1 - side) * size, 16)
            into = pl.ds(place * size, size)
            kept = pltpu.make_async_copy(
                buffer.at[pl.ds(mine, size), :],
                sides[group].at[into, pl.ds(0, rows)],
                turn_sem.at[group, place],
            )
            kept.start()
            turning[which].append(kept.wait)
            sent = remote(
                buffer.at[pl.ds(theirs, size), :],
                sides[group].at[into, pl.ds(rows, rows)],
                turn_send.at[group, place],
                turn_recv.at[group, place],
                other,
            )
            sent.start()
            turning[which].append(sent.wait_send)
            landing.append(sent)

    def free(which):
        for wait in turning[which]:
            wait()
        turning[which] = []

    def tiles(group, left, emit, start=0, width=None):
        width = weights[group].shape[1] if width is None else width

        @pl.loop(0, width // 256)
        def _(at):
            columns = span(at + start // 256, 256)
            emit(columns, matmul(left[...], weights[group][:, columns]))

    def stage_norm():
        norms[...] = line.land()
        moves.start(norms, norms_out)
        gain, offset = norms[0:1, :], norms[1:2, :]

        @pl.loop(0, rows // 64)
        def _(at):
            block = span(at, 64)
            values, _ = norm_rows(tokens[block, :].astype(jnp.float32))
            v.normed[block, :] = (values * gain + offset).astype(jnp.bfloat16)

        share(0, v.normed, 0)

    def stage_head_norm():
        @pl.loop(0, rows // 64)
        def _(at):
            block = span(at, 64)
            values, _ = norm_rows(head_in[block, :].astype(jnp.float32))
            v.head_norm[block, :] = values

    def stage_mixed(start, width):
        def emit(columns, total):
            v.mixed[:, columns] = total.astype(jnp.bfloat16)

        tiles(0, v.normed, emit, start, width)

    exchange = []

    def stage_swap():
        exchange.append(swaps.start(v.mixed.at[:, pl.ds(D, 2 * D)], v.far_pair, other))
        put("mixed")

    def stage_bias():
        for copy in exchange:
            copy.wait_recv()
        fill_bias(bias, far_row, own_row, side)
        moves.start(bias, bias_out)
        put("far_pair")
        free(1)

    def stage_heads(start, stop):
        @pl.loop(start, stop)
        def _(at):
            queries, keys, values = pair_slices(v.mixed, v.far_pair, at)
            total = None
            for which in range(2):
                mask = head_mask(which)
                weights_now = softmax_columns(keys, queries * mask, bias[...]).astype(jnp.bfloat16)
                part = matmul_left(values * mask, weights_now)
                total = part if total is None else total + part
            low = total.astype(jnp.bfloat16)
            turned[1][span(at, 2 * HEAD_DIM), :] = low
            v.attended[:, span(at, 2 * HEAD_DIM)] = low.T

    def stage_proj():
        share(1, turned[1].at[pl.ds(0, D), :], 1, True)

        def emit(columns, total):
            v.hidden[:, columns] = tokens[:, columns].astype(jnp.float32) + total

        tiles(1, v.attended, emit)
        put("hidden")
        gain, offset = norms[2:3, :], norms[3:4, :]

        @pl.loop(0, rows // 64)
        def _(at):
            block = span(at, 64)
            values, _ = norm_rows(v.hidden[block, :])
            v.second[block, :] = (values * gain + offset).astype(jnp.bfloat16)

        share(2, v.second, 0)

    def stage_up(start, width):
        def emit(columns, total):
            erf = lax.erf(total * 0.5**0.5)
            half = 0.5 * (1.0 + erf)
            v.activated[:, columns] = (total * half).astype(jnp.bfloat16)
            bell = jnp.exp(-0.5 * total * total) * (2.0 * 3.141592653589793) ** -0.5
            v.slope_inner[:, columns] = (half + total * bell).astype(jnp.bfloat16)

        tiles(2, v.second, emit, start, width)

    def stage_up_end():
        put("slope_inner")
        share(3, v.activated, 2)

    def stage_down(start, width):
        def emit(columns, total):
            v.block_low[:, columns] = (v.hidden[:, columns] + total).astype(jnp.bfloat16)

        tiles(3, v.activated, emit, start, width)

    def stage_down_end():
        put("block_low")
        share(4, v.block_low, 1)

    def stage_cond():
        def emit(columns, total):
            gates = jax.nn.sigmoid(total)
            v.cond_low[:, columns] = (total * gates).astype(jnp.bfloat16)
            slope = gates * (1.0 + total * (1.0 - gates))
            v.slope_cond[:, columns] = slope.astype(jnp.bfloat16)

        tiles(4, v.block_low, emit)
        put("slope_cond")
        share(5, v.cond_low, 0)

    def stage_mod(start, width):
        for at in range(start // 256, (start + width) // 256):
            total = matmul(v.cond_low[...], weights[5][:, at * 256 : (at + 1) * 256])
            part, block = divmod(at, HW // 256)
            columns = pl.ds(block * 256, 256)
            if part == 0:
                v.shift[:, columns] = total
            elif part == 1:
                scale = 1.0 + total
                v.scale[:, columns] = scale
                shaped = v.head_norm[:, columns] * scale + v.shift[:, columns]
                v.shaped[:, columns] = shaped.astype(jnp.bfloat16)
            else:
                v.gate[:, columns] = total
                grad = head_cotangent[:, columns].astype(jnp.float32) * total
                v.grad_branch[:, columns] = grad.astype(jnp.bfloat16)

    def stage_mod_end():
        put("scale")
        put("grad_branch")
        share(6, v.shaped, 1)

    def stage_inner():
        def emit(columns, total):
            gates = jax.nn.sigmoid(total)
            v.lifted[:, columns] = (total * gates).astype(jnp.bfloat16)
            slope = gates * (1.0 + total * (1.0 - gates))
            v.slope_middle[:, columns] = slope.astype(jnp.bfloat16)

        tiles(6, v.shaped, emit)
        put("slope_middle")
        share(7, v.lifted, 0)

    def stage_outer():
        def emit(columns, total):
            grown = head_in[:, columns].astype(jnp.float32) + v.gate[:, columns] * total
            v.head_out[:, columns] = grown.astype(jnp.bfloat16)
            grad = head_cotangent[:, columns].astype(jnp.float32) * total
            v.grad_gate[:, columns] = grad.astype(jnp.bfloat16)

        tiles(7, v.lifted, emit)
        put("head_out")
        put("grad_gate")

    def chunk_tasks(chunk):
        group, start, width = chunks[chunk]
        final = start + width == weights[group].shape[1]
        if group == 0:
            tasks = [lambda: stage_mixed(start, width)]
            if final:
                tasks += [stage_swap, stage_bias]
                tasks += [functools.partial(stage_heads, at, at + 2) for at in range(0, 6, 2)]
        elif group == 1:
            tasks = [stage_proj]
        elif group == 2:
            tasks = [lambda: stage_up(start, width)]
            if final:
                tasks.append(stage_up_end)
        elif group == 3:
            tasks = [lambda: stage_down(start, width)]
            if final:
                tasks.append(stage_down_end)
        elif group == 4:
            tasks = [stage_cond]
        elif group == 5:
            tasks = [lambda: stage_mod(start, width)]
            if final:
                tasks.append(stage_mod_end)
        elif group == 6:
            tasks = [stage_inner]
        else:
            tasks = [stage_outer]
        return [(chunk, task) for task in tasks]

    total = len(chunks)
    line.launch(spread)
    exchange.append(swaps.start(own_row, far_row, other))
    queue = [item for chunk in range(total) for item in chunk_tasks(chunk)]
    for step in range(-AHEAD_SEQ, total + 3):
        if step + AHEAD_SEQ < total:
            group, start, _ = chunks[step + AHEAD_SEQ]
            if start == 0:
                flow.cast(group)
            flow.first(step + AHEAD_SEQ)
        if 0 <= step + AHEAD_DP < total:
            flow.second(step + AHEAD_DP)
        if 0 <= step - 1 < total:
            flow.third(step - 1)
        if step == -2:
            stage_head_norm()
        if step == -1:
            line.launch(line.land())
        if step == 0:
            stage_norm()
        done = 0
        while queue and queue[0][0] <= step - 3 and (done < TASKS or step >= total):
            chunk, task = queue.pop(0)
            if chunk in loading:
                loading.pop(chunk).wait()
            task()
            done += 1
        if 0 <= step - 2 < total:
            flow.fourth(step - 2)
            flow.fifth(step - 2)
            load(step - 2)
    flow.finish()
    moves.finish()
    swaps.finish()
    for which in range(3):
        free(which)
    for copy in landing:
        copy.wait_recv()


def forward_all(masters, tokens, head_in, head_cotangent, image_ids, norm_params):
    devices = lax.axis_size("dp") * lax.axis_size("side") * lax.axis_size("seq")
    count = lax.axis_size("seq")
    chunks = chunk_list([master.shape for master in masters])
    total = len(chunks)
    rows = tokens.shape[0]
    low, full = jnp.bfloat16, jnp.float32
    fulls = [jax.ShapeDtypeStruct((devices * m.shape[0], m.shape[1]), low) for m in masters]
    sides = [jax.ShapeDtypeStruct((devices * m.shape[0] // 2, 2 * rows), low) for m in masters]
    outs = [jax.ShapeDtypeStruct((rows, width), kind) for _, width, kind in FORWARD_OUT]
    extra = [jax.ShapeDtypeStruct((2 * rows, rows), full), jax.ShapeDtypeStruct((8, D), full)]
    scratch = [pltpu.VMEM(item.shape, low) for item in fulls]
    scratch += [pltpu.VMEM((rows, width), kind) for _, width, kind in FORWARD_OUT + FORWARD_LOCAL]
    scratch += [
        pltpu.VMEM((2 * rows, rows), full),
        pltpu.VMEM((8, rows), full),
        pltpu.VMEM((8, rows), full),
        pltpu.VMEM((count + 8, 8, D), full),
        pltpu.VMEM((8, D), full),
        pltpu.VMEM((HW, rows), low),
        pltpu.VMEM((HW, rows), low),
        pltpu.VMEM((4 * D, rows), low),
    ]
    for master in masters:
        depth, width = master.shape
        if depth % 16 == 0:
            scratch.append(pltpu.VMEM((depth, width), low))
        else:
            scratch.append(pltpu.VMEM((count, depth, width), low))
            scratch.append(pltpu.VMEM((count * depth, width), low))
    dma = pltpu.SemaphoreType.DMA
    scratch += [
        dma((total, count + 7)),
        dma((total, count + 7)),
        dma((total,)),
        dma((total,)),
        dma((16,)),
        dma((8 + count,)),
        dma((8 + count,)),
        dma((8, 4)),
        dma((8, 4)),
        dma((8, 4)),
    ]
    vmem, hbm = pl.BlockSpec(memory_space=pltpu.VMEM), pl.BlockSpec(memory_space=pltpu.HBM)
    results = pl.pallas_call(
        lambda *refs: forward_kernel(chunks, count, *refs),
        out_shape=fulls + sides + outs + extra,
        in_specs=[vmem] * 13,
        out_specs=[hbm] * (16 + len(outs) + 2),
        scratch_shapes=scratch,
        compiler_params=pltpu.CompilerParams(
            collective_id=0, has_side_effects=True, vmem_limit_bytes=63 * 2**20
        ),
        name="forward",
    )(*masters, tokens, head_in, head_cotangent, image_ids[None, :], norm_params.T)
    named = dict(zip([name for name, _, _ in FORWARD_OUT], results[16:]))
    named["bias"], named["norms"] = results[-2:]
    return results[:8], results[8:16], named


class Scatter:
    def __init__(self, chunks, parts, inbox, after, slabs, pieces, finals, squares, sends, recvs):
        self.chunks, self.parts, self.inbox, self.after = chunks, parts, inbox, after
        self.slabs, self.pieces, self.finals, self.squares = slabs, pieces, finals, squares
        self.sends, self.recvs = sends, recvs
        self.dp, self.side, self.seq, near, far, self.along, _ = places()
        self.near, self.far = (near, self.side, self.seq), (far, self.side, self.seq)
        self.count = len(self.along) + 1
        self.started = []
        self.coming = {}

    def send(self, chunk, which, source, target, peer):
        copy = remote(source, target, self.sends.at[chunk, which], self.recvs.at[chunk, which], peer)
        copy.start()
        self.started.append(copy)
        self.coming[chunk, which] = copy

    def land(self, chunk, *which):
        for item in which:
            self.coming.pop((chunk, item)).wait_recv()

    def shape(self, chunk):
        group, start, width = self.chunks[chunk]
        size = self.parts[group].shape[1]
        return group, start, width, size, size // 2

    def first(self, chunk):
        group, start, width, size, half = self.shape(chunk)
        columns, part, inbox = pl.ds(start, width), self.parts[group], self.inbox[group]
        upper, lower = pl.ds(0, half), pl.ds(half, half)
        for item, block in enumerate((1, 3)):
            self.send(chunk, item, part.at[block, upper, columns], inbox.at[item, :, columns], self.near)
        for item, block in enumerate((2, 3)):
            self.send(
                chunk, 2 + item, part.at[block, lower, columns], inbox.at[2 + item, :, columns], self.far
            )

    def tiles(self, chunk, work):
        _, start, width, _, _ = self.shape(chunk)

        @pl.loop(0, width // 256)
        def _(at):
            work(pl.ds(pl.multiple_of(start + at * 256, 256), 256))

    def second(self, chunk):
        group, start, width, size, half = self.shape(chunk)
        columns, part, inbox = pl.ds(start, width), self.parts[group], self.inbox[group]
        upper, lower = pl.ds(0, half), pl.ds(half, half)
        self.land(chunk, 0, 1, 2, 3)

        def work(span_now):
            for block, rows, item in ((2, upper, 1), (1, lower, 3)):
                total = part[block, rows, span_now].astype(jnp.float32)
                total = total + inbox[item, :, span_now].astype(jnp.float32)
                part[block, rows, span_now] = total.astype(jnp.bfloat16)

        self.tiles(chunk, work)
        after = self.after[group]
        self.send(chunk, 4, part.at[1, lower, columns], after.at[0, :, columns], self.near)
        self.send(chunk, 5, part.at[2, upper, columns], after.at[1, :, columns], self.far)

    def third(self, chunk):
        group, start, width, size, half = self.shape(chunk)
        columns, part, inbox = pl.ds(start, width), self.parts[group], self.inbox[group]
        upper, lower = pl.ds(0, half), pl.ds(half, half)
        after = self.after[group]
        self.land(chunk, 4, 5)
        slab = self.slabs[group]
        depth = size // self.count

        def work(span_now):
            for rows, item, last, base in ((upper, 0, 1, 0), (lower, 2, 0, self.count // 2)):
                total = part[0, rows, span_now].astype(jnp.float32)
                total = total + inbox[item, :, span_now].astype(jnp.float32)
                total = total + after[last, :, span_now].astype(jnp.float32)
                for place in range(self.count // 2):
                    piece = total[place * depth : (place + 1) * depth].astype(jnp.bfloat16)
                    slab[base + place, :, span_now] = piece

        self.tiles(chunk, work)
        for step, peer in enumerate(self.along):
            self.send(
                chunk,
                6 + step,
                slab.at[peer, :, columns],
                self.pieces[group].at[step, :, columns],
                (self.dp, self.side, peer),
            )

    def fourth(self, chunk):
        group, start, width, size, half = self.shape(chunk)
        self.land(chunk, *(6 + step for step in range(self.count - 1)))
        slab, pieces, final = self.slabs[group], self.pieces[group], self.finals[group]

        def work(span_now):
            total = slab[self.seq, :, span_now].astype(jnp.float32)
            for step in range(self.count - 1):
                total = total + pieces[step, :, span_now].astype(jnp.float32)
            final[:, span_now] = total
            self.squares[0:1, :] += jnp.sum(total * total, axis=0, keepdims=True)

        self.tiles(chunk, work)

    def finish(self):
        for copy in self.started:
            copy.wait_send()


LAG = 1


BACKWARD_IN = (
    "grad_branch",
    "slope_middle",
    "head_in",
    "head_cotangent",
    "scale",
    "grad_gate",
    "slope_cond",
    "out_cotangent",
    "slope_inner",
    "hidden",
    "norms",
    "mixed",
    "far_pair",
    "bias",
    "tokens",
)


def norm_back(grads, values, scale):
    first = jnp.mean(grads, axis=-1, keepdims=True)
    second = jnp.mean(grads * values, axis=-1, keepdims=True)
    return scale * (grads - first - values * second)


def backward_kernel(chunks, count, *refs):
    rest = list(refs)

    def take(number):
        taken = rest[:number]
        del rest[:number]
        return taken

    weights, sides = take(8), take(8)
    given = dict(zip(BACKWARD_IN, take(len(BACKWARD_IN))))
    finals = take(8)
    head_in_grad, tokens_grad, norm_grads, norm_out = take(4)
    grads, parts, inbox, after, slabs, pieces = (take(8) for _ in range(6))
    small, large, tile_box = take(3)
    into = {
        "grad_branch": grads[7].at[pl.ds(0, grads[7].shape[0] // 2), :],
        "slope_middle": grads[6].at[pl.ds(0, grads[6].shape[0] // 2), :],
        "grad_gate": grads[5].at[pl.ds(0, grads[5].shape[0] // 2), pl.ds(2 * HW, HW)],
        "slope_cond": grads[4].at[pl.ds(0, grads[4].shape[0] // 2), :],
        "slope_inner": grads[2].at[pl.ds(0, grads[2].shape[0] // 2), :],
    }
    held = [name for name in BACKWARD_IN if name not in into]
    local = SimpleNamespace(**dict(zip(held, take(10))))
    spare, block_grad, attended_grad, back_pair, squares, box, square_box = take(7)
    sends, recvs, load_sem, side_sem, tile_sem, swap_send, swap_recv = rest

    dp, side, seq, near, far, along, _ = places()
    other = (dp, 1 - side, seq)
    greet(all_peers())
    rows = local.tokens.shape[0]
    own, pair = pl.ds(0, rows), pl.ds(rows, rows)
    swaps = Swaps(swap_send, swap_recv)
    flow = Scatter(chunks, parts, inbox, after, slabs, pieces, finals, squares, sends, recvs)
    loading = {}
    for item, name in enumerate(BACKWARD_IN):
        target = into[name] if name in into else getattr(local, name)
        loading[name] = pltpu.make_async_copy(given[name], target, load_sem.at[item])
    order = [group for group in range(7, -1, -1)]
    slim = [group for group in order if sides[group].shape[0] <= small.shape[1]]
    side_slot = {}
    side_copy = {}

    def side_load(group):
        depth = sides[group].shape[0]
        if group in slim:
            target = small.at[slim.index(group) % 2, pl.ds(0, depth), :]
        else:
            target = large
        side_slot[group] = target
        side_copy[group] = pltpu.make_async_copy(sides[group], target, side_sem.at[group])
        side_copy[group].start()

    def ready(*names):
        for name in names:
            loading.pop(name).wait()

    tile_list = [
        (group, at) for group in order for at in range(weights[group].shape[0] // 256)
    ]
    tile_copy = {}
    depth_box = tile_box.shape[0]

    def tile_load(item):
        if item >= len(tile_list):
            return
        group, at = tile_list[item]
        copy = pltpu.make_async_copy(
            weights[group].at[pl.ds(at * 256, 256), :],
            tile_box.at[item % depth_box, :, pl.ds(0, weights[group].shape[1])],
            tile_sem.at[item],
        )
        tile_copy[item] = copy
        copy.start()

    loading["grad_branch"].start()
    for item in range(depth_box):
        tile_load(item)
    loading["slope_middle"].start()
    side_load(slim[0])
    side_load(slim[1])
    for name in BACKWARD_IN[2:]:
        loading[name].start()
    for group in order:
        if group not in slim:
            side_load(group)
    squares[...] = jnp.zeros_like(squares)
    norm_grads[...] = jnp.zeros_like(norm_grads)
    at_tile = [0]

    def back(group, emit):
        width = weights[group].shape[1]
        for at in range(weights[group].shape[0] // 256):
            item = at_tile[0]
            at_tile[0] += 1
            tile_copy.pop(item).wait()
            total = matmul_right(
                grads[group][own, :], tile_box[item % depth_box, :, pl.ds(0, width)]
            )
            emit(pl.ds(at * 256, 256), total)
            tile_load(item + depth_box)

    coming = {}

    def share(group):
        coming[group] = swaps.start(grads[group].at[own, :], grads[group].at[pair, :], other)

    def product(chunk):
        group, start, width = chunks[chunk]
        if group in coming:
            coming.pop(group).wait_recv()
            side_copy.pop(group).wait()
        left, part = side_slot[group], parts[group]
        size = part.shape[1]
        whole = group in slim

        @pl.loop(0, width // 256)
        def _(at):
            columns = pl.ds(pl.multiple_of(start + at * 256, 256), 256)
            right = grads[group][:, columns]
            if whole:
                total = matmul(left[...], right).astype(jnp.bfloat16)
                for block in range(4):
                    part[block, :, columns] = total[block * size : (block + 1) * size]
            else:
                for block in range(4):
                    total = matmul(left[pl.ds(block * size, size), :], right)
                    part[block, :, columns] = total.astype(jnp.bfloat16)

        if start + width == weights[group].shape[1]:
            if group in slim and slim.index(group) + 2 < len(slim):
                side_load(slim[slim.index(group) + 2])

    def step(chunk):
        total = len(chunks)
        if chunk < total:
            product(chunk)
            flow.first(chunk)
        if 0 <= chunk - LAG < total:
            flow.second(chunk - LAG)
        if 0 <= chunk - LAG - 1 < total:
            flow.third(chunk - LAG - 1)
        if 0 <= chunk - LAG - 2 < total:
            flow.fourth(chunk - LAG - 2)

    def stage_outer():
        ready("grad_branch")
        share(7)
        ready("slope_middle")

        def emit(columns, total):
            slope = grads[6][own, columns].astype(jnp.float32)
            grads[6][own, columns] = (total * slope).astype(jnp.bfloat16)

        back(7, emit)
        share(6)

    def stage_inner():
        def emit(columns, total):
            spare[:, columns] = total

        back(6, emit)
        ready("head_in", "head_cotangent", "scale", "grad_gate")

        @pl.loop(0, rows // 32)
        def _(at):
            block = span(at, 32)
            values, scale = norm_rows(local.head_in[block, :].astype(jnp.float32))
            grad = spare[block, pl.ds(0, HW)]
            grads[5][block, pl.ds(0, HW)] = grad.astype(jnp.bfloat16)
            grads[5][block, pl.ds(HW, HW)] = (grad * values).astype(jnp.bfloat16)
            passed = norm_back(grad * local.scale[block, :], values, scale)
            head_in_grad[block, :] = local.head_cotangent[block, :].astype(jnp.float32) + passed

        share(5)

    def stage_mod():
        ready("slope_cond")

        def emit(columns, total):
            slope = grads[4][own, columns].astype(jnp.float32)
            grads[4][own, columns] = (total * slope).astype(jnp.bfloat16)

        back(5, emit)
        share(4)

    def stage_cond():
        ready("out_cotangent")

        def emit(columns, total):
            grad = local.out_cotangent[:, columns].astype(jnp.float32) + total
            block_grad[:, columns] = grad
            grads[3][own, columns] = grad.astype(jnp.bfloat16)

        back(4, emit)
        share(3)

    def stage_down():
        ready("slope_inner")

        def emit(columns, total):
            slope = grads[2][own, columns].astype(jnp.float32)
            grads[2][own, columns] = (total * slope).astype(jnp.bfloat16)

        back(3, emit)
        share(2)

    def norm_stage(source, base, emit):
        gain = local.norms[base : base + 1, :]

        @pl.loop(0, rows // 32)
        def _(at):
            block = span(at, 32)
            values, scale = norm_rows(source[block, :].astype(jnp.float32))
            grad = spare[block, pl.ds(0, D)]
            norm_grads[base : base + 1, :] += jnp.sum(grad * values, axis=0, keepdims=True)
            norm_grads[base + 1 : base + 2, :] += jnp.sum(grad, axis=0, keepdims=True)
            emit(block, norm_back(grad * gain, values, scale))

    def stage_up():
        def keep(columns, total):
            spare[:, columns] = total

        back(2, keep)
        ready("hidden", "norms")

        def emit(block, passed):
            grad = block_grad[block, :] + passed
            tokens_grad[block, :] = grad
            grads[1][block, :] = grad.astype(jnp.bfloat16)

        norm_stage(local.hidden, 2, emit)
        share(1)

    def stage_proj():
        def emit(columns, total):
            attended_grad[:, columns] = total.astype(jnp.bfloat16)

        back(1, emit)
        ready("mixed", "far_pair", "bias")

    def stage_heads(start, stop):
        width = 2 * HEAD_DIM
        scaling = HEAD_DIM ** (-0.5)

        @pl.loop(start, stop)
        def _(at):
            queries, keys, values = pair_slices(local.mixed, local.far_pair, at)
            outer = attended_grad[:, span(at, width)]
            query_part = key_part = value_part = None
            for which in range(2):
                mask = head_mask(which)
                query_now, outer_now = queries * mask, outer * mask
                chances = softmax_columns(keys, query_now, local.bias[...])
                slopes = matmul_right(values, outer_now)
                inner = jnp.sum(chances * slopes, axis=0, keepdims=True)
                score_grad = (chances * (slopes - inner)).astype(jnp.bfloat16)
                value_now = matmul(chances.astype(jnp.bfloat16), outer_now)
                key_now = matmul(score_grad, query_now)
                query_side = matmul_left(keys * mask, score_grad)
                if which == 0:
                    query_part, key_part, value_part = query_side, key_now, value_now
                else:
                    query_part = query_part + query_side
                    key_part = key_part + key_now
                    value_part = value_part + value_now
            grads[0][own, span(at, width)] = (query_part * scaling).astype(jnp.bfloat16).T
            key_part = key_part * scaling
            first, second = span(at, width), span(at + D // width, width)
            local.far_pair[:, first] = key_part[:rows].astype(jnp.bfloat16)
            local.far_pair[:, second] = value_part[:rows].astype(jnp.bfloat16)
            spare[:, first] = key_part[rows:]
            spare[:, second] = value_part[rows:]

    def stage_return():
        coming["back"] = swaps.start(local.far_pair, back_pair, other)

    def stage_merge():
        coming.pop("back").wait_recv()

        @pl.loop(0, 2 * D // 256)
        def _(at):
            columns = span(at, 256)
            total = spare[:, columns] + back_pair[:, columns].astype(jnp.float32)
            grads[0][own, span(at + D // 256, 256)] = total.astype(jnp.bfloat16)

        share(0)

    def stage_attend():
        def keep(columns, total):
            spare[:, columns] = total

        back(0, keep)
        ready("tokens")

        def emit(block, passed):
            tokens_grad[block, :] = tokens_grad[block, :] + passed

        norm_stage(local.tokens, 0, emit)

    stage_outer()
    stages = [
        stage_inner,
        stage_mod,
        stage_cond,
        stage_down,
        stage_up,
        stage_proj,
        lambda: stage_heads(0, 2),
        lambda: stage_heads(2, 4),
        lambda: stage_heads(4, 6),
        stage_return,
        stage_merge,
        stage_attend,
    ]
    line = LineSum(box, swaps)
    total = len(chunks)
    for chunk in range(total + LAG + 3):
        group = chunks[min(chunk, total - 1)][0]
        needed = {7: 0, 6: 0, 5: 1, 4: 2, 3: 3, 2: 4, 1: 5, 0: 11}[group]
        while stages and 12 - len(stages) < needed:
            stages.pop(0)()
        step(chunk)
        if stages:
            stages.pop(0)()
            if not stages:
                line.launch(norm_grads[...])
        elif line.level == 0:
            line.launch(line.land())
        elif line.level == 1:
            sums = line.land()
            norm_grads[...] = sums
    last = LineSum(square_box, swaps)
    last.launch(squares[...])
    last.launch(last.land())
    sums = norm_grads[...]
    flat = jnp.sum(last.land(), axis=0, keepdims=True)
    whole = jnp.sum(flat, axis=1, keepdims=True)
    extra = jnp.sum(jnp.sum(sums * sums, axis=0, keepdims=True), axis=1, keepdims=True)
    norm_out[...] = jnp.broadcast_to(jnp.sqrt(whole + extra), norm_out.shape)
    flow.finish()
    swaps.finish()


def backward_chunks(masters):
    chunks = chunk_list(masters)
    chunks = [item for group in range(7, -1, -1) for item in chunks if item[0] == group]
    group, start, width = chunks.pop()
    for size in (width - width // 2 // 256 * 256, width // 2 // 256 * 256):
        chunks.append((group, start, size)) if size else None
        start += size
    return chunks


def backward_all(masters, weights, sides, named):
    count = lax.axis_size("seq")
    shapes = [master.shape for master in masters]
    chunks = backward_chunks(shapes)
    total = len(chunks)
    rows = named["tokens"].shape[0]
    low, full = jnp.bfloat16, jnp.float32
    vmem, hbm = pl.BlockSpec(memory_space=pltpu.VMEM), pl.BlockSpec(memory_space=pltpu.HBM)
    given = [named[name] for name in BACKWARD_IN]
    outs = [jax.ShapeDtypeStruct(shape, full) for shape in shapes]
    outs += [
        jax.ShapeDtypeStruct((rows, HW), full),
        jax.ShapeDtypeStruct((rows, D), full),
        jax.ShapeDtypeStruct((8, D), full),
        jax.ShapeDtypeStruct((8, 128), full),
    ]
    scratch = [pltpu.VMEM((2 * rows, width), low) for _, width in shapes]
    scratch += [pltpu.VMEM((4, count * depth, width), low) for depth, width in shapes]
    scratch += [pltpu.VMEM((4, count * depth // 2, width), low) for depth, width in shapes]
    scratch += [pltpu.VMEM((2, count * depth // 2, width), low) for depth, width in shapes]
    scratch += [pltpu.VMEM((count, depth, width), low) for depth, width in shapes]
    scratch += [pltpu.VMEM((count - 1, depth, width), low) for depth, width in shapes]
    scratch += [
        pltpu.VMEM((2, HW // 2, 2 * rows), low),
        pltpu.VMEM((2 * D, 2 * rows), low),
        pltpu.VMEM((3, 256, 3 * HW), low),
        pltpu.VMEM((rows, HW), low),
        pltpu.VMEM((rows, HW), low),
        pltpu.VMEM((rows, HW), full),
        pltpu.VMEM((rows, D), low),
        pltpu.VMEM((rows, D), full),
        pltpu.VMEM((8, D), full),
        pltpu.VMEM((rows, 3 * D), low),
        pltpu.VMEM((rows, 2 * D), low),
        pltpu.VMEM((2 * rows, rows), full),
        pltpu.VMEM((rows, D), low),
        pltpu.VMEM((rows, 2 * D), full),
        pltpu.VMEM((rows, D), full),
        pltpu.VMEM((rows, D), low),
        pltpu.VMEM((rows, 2 * D), low),
        pltpu.VMEM((8, 256), full),
        pltpu.VMEM((count + 8, 8, D), full),
        pltpu.VMEM((count + 8, 8, 256), full),
    ]
    dma = pltpu.SemaphoreType.DMA
    scratch += [
        dma((total, 5 + count)),
        dma((total, 5 + count)),
        dma((len(BACKWARD_IN),)),
        dma((8,)),
        dma((sum(w.shape[0] // 256 for w in weights),)),
        dma((21 + 2 * count,)),
        dma((21 + 2 * count,)),
    ]
    return pl.pallas_call(
        lambda *refs: backward_kernel(chunks, count, *refs),
        out_shape=outs,
        in_specs=[hbm] * (16 + len(given)),
        out_specs=[vmem] * len(outs),
        scratch_shapes=scratch,
        compiler_params=pltpu.CompilerParams(
            collective_id=1, has_side_effects=True, vmem_limit_bytes=64 * 2**20
        ),
        name="backward",
    )(*weights, *sides, *given)


def optimizer_kernel(*refs):
    rest = list(refs)

    def take(number):
        taken = rest[:number]
        del rest[:number]
        return taken

    given = [take(5) for _ in range(8)]
    passed = take(4)
    small, grad_norm = take(5), rest.pop(0)
    results = [take(4) for _ in range(8)]
    kept = take(4)
    small_results = take(4)
    held = [take(5) for _ in range(8)]
    made = [take(4) for _ in range(8)]
    carried = take(4)
    load_sem, save_sem, pass_sem = rest
    loads, saves = [], []
    for group in range(8):
        for item in range(5):
            copy = pltpu.make_async_copy(
                given[group][item], held[group][item], load_sem.at[group, item]
            )
            copy.start()
            loads.append(copy)
    for item in range(4):
        pltpu.make_async_copy(passed[item], carried[item], pass_sem.at[0, item]).start()
    factor = jnp.minimum(1.0, clip_limit / (grad_norm[0:1, 0:1] + 1e-06))
    keep_old, take_new = average_factors()

    def update(source, target, columns, decays, rate):
        gradient, master, moment, square, average = (ref[:, columns] for ref in source)
        put(gradient, master, moment, square, average, target, columns, decays, rate)

    def put(gradient, master, moment, square, average, target, columns, decays, rate):
        fresh = adam_step(master, gradient * factor, moment, square, decays, rate)
        for item in range(3):
            target[item][:, columns] = fresh[item]
        target[3][:, columns] = keep_old * average + take_new * fresh[0]

    width = small[1].shape[1]
    total = small[0].shape[1]
    place = (lax.axis_index("dp") * 2 + lax.axis_index("side")) * lax.axis_size(
        "seq"
    ) + lax.axis_index("seq")
    turned = pltpu.roll(small[0][...], lax.rem(total - place * width, total), 1)
    own = [turned[0:4, 0:width]] + [ref[...] for ref in small[1:]]
    put(*own, small_results, slice(None), 0.0, learn_rates[8])
    for group in range(8):
        for item in range(5):
            loads[group * 5 + item].wait()

        @pl.loop(0, held[group][0].shape[1] // 256)
        def _(at):
            columns = pl.ds(pl.multiple_of(at * 256, 256), 256)
            update(held[group], made[group], columns, 1.0, learn_rates[group])

        for item in range(4):
            copy = pltpu.make_async_copy(
                made[group][item], results[group][item], save_sem.at[group, item]
            )
            copy.start()
            saves.append(copy)
        if group % 2:
            item = group // 2
            pltpu.make_async_copy(passed[item], carried[item], pass_sem.at[0, item]).wait()
            copy = pltpu.make_async_copy(carried[item], kept[item], pass_sem.at[1, item])
            copy.start()
            saves.append(copy)
    for copy in saves:
        copy.wait()


def optimizer_all(gradients, passed, norm_grads, grad_norm, masters, moments, squares, averages):
    full = jnp.float32
    vmem, hbm = pl.BlockSpec(memory_space=pltpu.VMEM), pl.BlockSpec(memory_space=pltpu.HBM)
    given = []
    for group in range(8):
        given += [
            gradients[group],
            masters[group],
            moments[group],
            squares[group],
            averages[group],
        ]
    small = [masters[8].T, moments[8].T, squares[8].T, averages[8].T]
    given += [*passed, norm_grads, *small, grad_norm]
    shapes = [master.shape for master in masters[:8]]
    outs = [jax.ShapeDtypeStruct(shape, full) for shape in shapes for _ in range(4)]
    outs += [jax.ShapeDtypeStruct(item.shape, item.dtype) for item in passed]
    outs += [jax.ShapeDtypeStruct(small[0].shape, full) for _ in range(4)]
    scratch = [pltpu.VMEM(shape, full) for shape in shapes for _ in range(5)]
    scratch += [pltpu.VMEM(shape, full) for shape in shapes for _ in range(4)]
    scratch += [pltpu.VMEM(item.shape, item.dtype) for item in passed]
    dma = pltpu.SemaphoreType.DMA
    scratch += [dma((8, 5)), dma((8, 4)), dma((2, 4))]
    results = pl.pallas_call(
        optimizer_kernel,
        out_shape=outs,
        in_specs=[hbm] * 44 + [vmem] * 6,
        out_specs=[hbm] * 36 + [vmem] * 4,
        scratch_shapes=scratch,
        compiler_params=pltpu.CompilerParams(vmem_limit_bytes=63 * 2**20),
        name="optimizer",
    )(*given)
    fresh = [results[4 * group : 4 * group + 4] for group in range(8)]
    return results[32:36], fresh + [[item.T for item in results[36:]]]


def body(*arrays):
    tokens, head_in, image_ids, out_cotangent, head_cotangent = arrays[:5]
    masters, moments, squares, averages = (arrays[at : at + 9] for at in (5, 14, 23, 32))
    sides = lax.axis_size("dp") == 4 and lax.axis_size("side") == 2
    if not sides or masters[0].shape[0] % 8 or lax.axis_size("seq") % 2:
        return plain_body(*arrays)
    weights, turned, named = forward_all(
        masters[:8], tokens, head_in, head_cotangent, image_ids, masters[8]
    )
    named = dict(
        named,
        tokens=tokens,
        head_in=head_in,
        head_cotangent=head_cotangent,
        out_cotangent=out_cotangent,
    )
    results = backward_all(masters[:8], weights, turned, named)
    gradients = results[:8]
    head_in_grad, tokens_grad, norm_grads, grad_norm = results[8:]
    passed = [named["block_low"], named["head_out"], tokens_grad, head_in_grad]
    passed, fresh = optimizer_all(
        gradients, passed, norm_grads, grad_norm, masters, moments, squares, averages
    )
    return (
        (*passed, grad_norm[0, 0])
        + tuple(item for group in fresh for item in group[:3])
        + tuple(group[3] for group in fresh)
    )


def plain_body(
    tokens,
    head_in,
    image_ids,
    out_cotangent,
    head_cotangent,
    weight_attend,
    weight_proj,
    weight_up,
    weight_down,
    weight_cond,
    weight_mod,
    weight_inner,
    weight_outer,
    norm_params,
    mean_attend,
    mean_proj,
    mean_up,
    mean_down,
    mean_cond,
    mean_mod,
    mean_inner,
    mean_outer,
    mean_norms,
    square_attend,
    square_proj,
    square_up,
    square_down,
    square_cond,
    square_mod,
    square_inner,
    square_outer,
    square_norms,
    ema_attend,
    ema_proj,
    ema_up,
    ema_down,
    ema_cond,
    ema_mod,
    ema_inner,
    ema_outer,
    ema_norms,
):
    used = (
        lax.all_gather(
            weight_attend.astype(jnp.bfloat16), AXES, axis=0, tiled=True
        ),
        lax.all_gather(weight_proj.astype(jnp.bfloat16), AXES, axis=0, tiled=True),
        lax.all_gather(weight_up.astype(jnp.bfloat16), AXES, axis=0, tiled=True),
        lax.all_gather(weight_down.astype(jnp.bfloat16), AXES, axis=0, tiled=True),
        lax.all_gather(weight_cond.astype(jnp.bfloat16), AXES, axis=0, tiled=True),
        lax.all_gather(weight_mod.astype(jnp.bfloat16), AXES, axis=0, tiled=True),
        lax.all_gather(
            weight_inner.astype(jnp.bfloat16), AXES, axis=0, tiled=True
        ),
        lax.all_gather(
            weight_outer.astype(jnp.bfloat16), AXES, axis=0, tiled=True
        ),
        lax.all_gather(norm_params.astype(jnp.bfloat16), AXES, axis=0, tiled=True),
    )
    use_attend, use_proj, use_up, use_down, use_cond, use_mod, use_inner, use_outer, use_norms = (
        used
    )
    norm_set = use_norms.astype(jnp.float32)
    inputs = tokens.astype(jnp.float32)
    row_count = tokens.shape[0]
    normed, first_back = jax.vjp(scaled_norm, inputs, norm_set[:, 0], norm_set[:, 1])
    normed_low = normed.astype(jnp.bfloat16)
    mixed_rows = matmul(normed_low, use_attend).astype(jnp.bfloat16)
    query_heads = split_heads(mixed_rows[:, :D])
    own_keys = split_heads(mixed_rows[:, D : 2 * D])
    own_values = split_heads(mixed_rows[:, 2 * D :])
    own_images = image_ids.astype(jnp.bfloat16)
    far_pair, far_images = shifted((mixed_rows[:, D:], own_images), "side", 1)
    both_keys = jnp.concatenate([split_heads(far_pair[:, :D]), own_keys], axis=1)
    both_values = jnp.concatenate([split_heads(far_pair[:, D:]), own_values], axis=1)
    near_allowed = own_images[:, None] == own_images[None, :]
    wide_allowed = own_images[:, None] == jnp.concatenate([far_images, own_images])[None, :]
    masked_side = lax.axis_index("side") == 1

    def visible_forward():
        return lax.map(
            lambda stacked: head_forward(stacked, near_allowed), (query_heads, own_keys, own_values)
        )

    def masked_forward():
        return lax.map(
            lambda stacked: head_forward(stacked, wide_allowed),
            (query_heads, both_keys, both_values),
        )

    attended_heads, log_totals = lax.cond(masked_side, masked_forward, visible_forward)
    attended = join_heads(attended_heads)
    hidden = inputs + matmul(attended, use_proj)
    second, second_back = jax.vjp(scaled_norm, hidden, norm_set[:, 2], norm_set[:, 3])
    second_low = second.astype(jnp.bfloat16)
    inner_pre = matmul(second_low, use_up)
    activated_full, gelu_back = jax.vjp(gelu_exact, inner_pre)
    activated = activated_full.astype(jnp.bfloat16)
    block_low = (hidden + matmul(activated, use_down)).astype(jnp.bfloat16)
    condition = matmul(block_low, use_cond)
    lifted_cond, cond_back = jax.vjp(jax.nn.silu, condition)
    cond_low = lifted_cond.astype(jnp.bfloat16)
    modulation = matmul(cond_low, use_mod)
    head_shift = modulation[:, :HW]
    head_scale = modulation[:, HW : 2 * HW]
    head_gate = modulation[:, 2 * HW :]
    head_rows = head_in.astype(jnp.float32)
    shaped, shaped_back = jax.vjp(modulated, head_rows, head_shift, head_scale)
    shaped_low = shaped.astype(jnp.bfloat16)
    middle = matmul(shaped_low, use_inner)
    lifted_full, middle_back = jax.vjp(jax.nn.silu, middle)
    lifted_rows = lifted_full.astype(jnp.bfloat16)
    branch = matmul(lifted_rows, use_outer)
    head_out = (head_rows + head_gate * branch).astype(jnp.bfloat16)
    head_grad = head_cotangent.astype(jnp.float32)
    grad_branch = (head_grad * head_gate).astype(jnp.bfloat16)
    grad_outer = matmul_left(lifted_rows, grad_branch)
    grad_middle = middle_back(matmul_right(grad_branch, use_outer))[0].astype(jnp.bfloat16)
    grad_inner = matmul_left(shaped_low, grad_middle)
    head_part, grad_shift, grad_scale = shaped_back(matmul_right(grad_middle, use_inner))
    head_in_grad = head_grad + head_part
    grad_modulation = jnp.concatenate([grad_shift, grad_scale, head_grad * branch], axis=1).astype(
        jnp.bfloat16
    )
    grad_mod = matmul_left(cond_low, grad_modulation)
    grad_condition = cond_back(matmul_right(grad_modulation, use_mod))[0].astype(jnp.bfloat16)
    grad_cond = matmul_left(block_low, grad_condition)
    grad_block = out_cotangent.astype(jnp.float32) + matmul_right(grad_condition, use_cond)
    grad_feed = grad_block.astype(jnp.bfloat16)
    grad_down = matmul_left(activated, grad_feed)
    grad_inner_pre = gelu_back(matmul_right(grad_feed, use_down))[0].astype(jnp.bfloat16)
    grad_up = matmul_left(second_low, grad_inner_pre)
    hidden_part, grad_gain_two, grad_bias_two = second_back(matmul_right(grad_inner_pre, use_up))
    grad_hidden = grad_block + hidden_part
    grad_proj_out = grad_hidden.astype(jnp.bfloat16)
    grad_proj = matmul_left(attended, grad_proj_out)
    grad_attended = split_heads(matmul_right(grad_proj_out, use_proj).astype(jnp.bfloat16))

    def visible_backward():
        grad_query, grad_keys, grad_values = lax.map(
            lambda stacked: head_backward(stacked, near_allowed),
            (query_heads, own_keys, own_values, log_totals, grad_attended),
        )
        zero_fill = jnp.zeros_like(grad_keys)
        return (
            grad_query,
            jnp.concatenate([zero_fill, grad_keys], axis=1),
            jnp.concatenate([zero_fill, grad_values], axis=1),
        )

    def masked_backward():
        return lax.map(
            lambda stacked: head_backward(stacked, wide_allowed),
            (query_heads, both_keys, both_values, log_totals, grad_attended),
        )

    grad_query, grad_keys, grad_values = lax.cond(masked_side, masked_backward, visible_backward)
    far_grad = jnp.concatenate(
        [join_heads(grad_keys[:, :row_count]), join_heads(grad_values[:, :row_count])], axis=1
    )
    returned = shifted(far_grad.astype(jnp.bfloat16), "side", -1).astype(far_grad.dtype)
    near_grad = (
        jnp.concatenate(
            [join_heads(grad_keys[:, row_count:]), join_heads(grad_values[:, row_count:])], axis=1
        )
        + returned
    )
    grad_mixed = jnp.concatenate([join_heads(grad_query), near_grad], axis=1).astype(jnp.bfloat16)
    grad_attend = matmul_left(normed_low, grad_mixed)
    tokens_part, grad_gain_one, grad_bias_one = first_back(matmul_right(grad_mixed, use_attend))
    tokens_grad = grad_hidden + tokens_part
    grad_norms = jnp.stack([grad_gain_one, grad_bias_one, grad_gain_two, grad_bias_two], axis=1)
    owned = (
        lax.psum_scatter(grad_attend, AXES, scatter_dimension=0, tiled=True),
        lax.psum_scatter(grad_proj, AXES, scatter_dimension=0, tiled=True),
        lax.psum_scatter(grad_up, AXES, scatter_dimension=0, tiled=True),
        lax.psum_scatter(grad_down, AXES, scatter_dimension=0, tiled=True),
        lax.psum_scatter(grad_cond, AXES, scatter_dimension=0, tiled=True),
        lax.psum_scatter(grad_mod, AXES, scatter_dimension=0, tiled=True),
        lax.psum_scatter(grad_inner, AXES, scatter_dimension=0, tiled=True),
        lax.psum_scatter(grad_outer, AXES, scatter_dimension=0, tiled=True),
        lax.psum_scatter(grad_norms, AXES, scatter_dimension=0, tiled=True),
    )
    local_squares = sum((jnp.sum(gradient * gradient) for gradient in owned))
    grad_norm = jnp.sqrt(lax.psum(local_squares, AXES))
    factor = jnp.minimum(1.0, clip_limit / (grad_norm + 1e-06))
    masters = [
        weight_attend,
        weight_proj,
        weight_up,
        weight_down,
        weight_cond,
        weight_mod,
        weight_inner,
        weight_outer,
        norm_params,
    ]
    moments = [
        mean_attend,
        mean_proj,
        mean_up,
        mean_down,
        mean_cond,
        mean_mod,
        mean_inner,
        mean_outer,
        mean_norms,
    ]
    squares = [
        square_attend,
        square_proj,
        square_up,
        square_down,
        square_cond,
        square_mod,
        square_inner,
        square_outer,
        square_norms,
    ]
    averages = [
        ema_attend,
        ema_proj,
        ema_up,
        ema_down,
        ema_cond,
        ema_mod,
        ema_inner,
        ema_outer,
        ema_norms,
    ]
    keep_old, take_new = average_factors()
    results = []
    smoothed = []
    for position in range(9):
        decays = 1.0 if position < 8 else 0.0
        fresh = adam_step(
            masters[position],
            owned[position] * factor,
            moments[position],
            squares[position],
            decays,
            learn_rates[position],
        )
        results.extend(fresh)
        smoothed.append(keep_old * averages[position] + take_new * fresh[0])
    return (
        (block_low, head_out, tokens_grad, head_in_grad, grad_norm)
        + tuple(results)
        + tuple(smoothed)
    )


def solution(mesh):
    rows, line = P(AXES, None), P(AXES)
    in_specs = (rows, rows, line) + (rows,) * 38
    out_specs = (rows,) * 4 + (P(),) + (rows,) * 36
    return jax.shard_map(body, mesh=mesh, in_specs=in_specs, out_specs=out_specs, check_vma=False)
```

```python
import functools
from types import SimpleNamespace

import jax
import jax.numpy as jnp
from jax import lax
from jax.experimental import pallas as pl
from jax.experimental.pallas import tpu as pltpu
from jax.sharding import PartitionSpec as P

D = 768
HEADS = 12
HEAD_DIM = 64
HW = 1024
STEP = 5


norm_eps = 1e-06
clip_limit = 2048.0
learn_rates = (0.03, 0.24, 0.03, 0.03, 0.03, 0.03, 0.03, 0.03, 0.4)
beta_first = 0.9
beta_second = 0.95
weight_decay = 0.02
adam_eps = 1e-08
ema_decay = 0.9999
masked_fill = -1e30

MESH = pl.DeviceIdType.MESH
AXES = ("dp", "side", "seq")


def places():
    dp, side, seq = (lax.axis_index(name) for name in AXES)
    count = lax.axis_size("seq")
    near = dp + 1 - 2 * lax.rem(dp, 2)
    far = dp + 2 - 4 * (dp // 2)
    along = [lax.rem(seq + step, count) for step in range(1, count)]
    before = [lax.rem(seq + count - step, count) for step in range(1, count)]
    return dp, side, seq, near, far, along, before


def greet(peers):
    barrier = pltpu.get_barrier_semaphore()
    for peer in peers:
        pl.semaphore_signal(barrier, inc=1, device_id=peer, device_id_type=MESH)
    pl.semaphore_wait(barrier, len(peers))


def remote(source, target, send_sem, recv_sem, peer):
    return pltpu.make_async_remote_copy(
        src_ref=source,
        dst_ref=target,
        send_sem=send_sem,
        recv_sem=recv_sem,
        device_id=peer,
        device_id_type=MESH,
    )


class Line:
    def __init__(self):
        self.dp, self.side, self.seq, self.near, self.far, self.along, self.before = places()
        self.count = len(self.along) + 1
        self.started = {}

    def at(self, dp, side, seq=None):
        return dp, side, self.seq if seq is None else seq

    def start(self, chunk, copy, go=None):
        if go is None:
            copy.start()
        else:
            pl.when(go)(copy.start)
        self.started.setdefault(chunk, []).append((copy, go))

    def sent(self, chunk):
        for copy, go in self.started.pop(chunk):
            if go is None:
                copy.wait_send()
            else:
                pl.when(go)(copy.wait_send)

    def goes(self, step):
        if self.count != 4 or step == 1:
            return None
        return self.seq != (3 if step == 0 else 0)

    def inner(self):
        return jnp.logical_and(self.seq > 0, self.seq < self.count - 1)

    def finish(self):
        for chunk in list(self.started):
            self.sent(chunk)


class Gather(Line):
    def __init__(self, chunks, entering, masters, fulls, own, slabs, joined, plain, sems, locs):
        super().__init__()
        self.chunks, self.masters, self.fulls = chunks, masters, fulls
        self.entering = entering
        self.own, self.slabs, self.joined = own, slabs, joined
        self.plain, self.sems, self.locs = plain, sems, locs
        self.inside = {}
        self.ready = set()
        self.crossing = [at for at in range(len(chunks)) if at not in plain]
        self.places = relative(self.dp, self.near, self.far)

    def rows(self, group, dp, side):
        size = self.count * self.masters[group].shape[0]
        return pl.multiple_of((dp * 2 + side) * size, 16), size

    def packed(self, group):
        return self.masters[group].shape[0] % 16 == 0

    def part(self, chunk, start, size):
        group, first, width = self.chunks[chunk]
        return self.fulls[group].at[pl.ds(pl.multiple_of(start, 16), size), pl.ds(first, width)]

    def send(self, chunk, which, source, target, peer, go=None, into=None):
        into = which if into is None else into
        copy = remote(source, target, self.sem(0, chunk, which), self.sem(1, chunk, into), peer)
        self.start(chunk, copy, go)

    def sem(self, kind, chunk, which):
        if chunk in self.plain:
            return self.sems[kind].at[self.plain.index(chunk) % RING, which]
        return self.sems[2 + kind].at[self.crossing.index(chunk), which]

    def arrived(self, chunk, which, target):
        peer = (self.near, self.side, self.seq)
        sems = self.sem(0, chunk, which), self.sem(1, chunk, which)
        remote(target, target, *sems, peer).wait_recv()

    def local(self, chunk, source, target):
        copy = pltpu.make_async_copy(source, target, self.locs.at[chunk])
        copy.start()
        self.inside[chunk] = copy

    def cast(self, group):
        if group in self.ready:
            return
        self.ready.add(group)
        self.entering[group].wait()
        rounded = self.masters[group][...].astype(jnp.bfloat16)
        if self.packed(group):
            self.own[group][...] = rounded
        else:
            self.slabs[group][self.seq] = rounded

    def piece(self, chunk, dp, seq):
        group, start, width = self.chunks[chunk]
        if not self.packed(group):
            return self.slabs[group].at[seq, :, pl.ds(start, width)]
        rows = self.masters[group].shape[0]
        return self.part(chunk, self.rows(group, dp, self.side)[0] + seq * rows, rows)

    def line(self, chunk, base, source, dp):
        target = self.piece(chunk, dp, self.seq)
        for step, peer in enumerate(self.along):
            self.send(
                chunk, base + step, source, target, self.at(self.dp, self.side, peer), self.goes(step)
            )

    def pass_on(self, chunk, base, spare, dp):
        self.arrived(chunk, base + 1, self.piece(chunk, dp, self.before[1]))
        if self.count == 4:
            half = self.seq // 2
            origin = 3 - 3 * half
            piece = self.piece(chunk, dp, origin)
            peer = self.at(self.dp, self.side, 3 - origin)
            self.send(chunk, spare, piece, piece, peer, self.inner(), base + 2 * half)

    def line_end(self, chunk, base, dp):
        for step, peer in enumerate(self.before):
            if step != 1:
                self.arrived(chunk, base + step, self.piece(chunk, dp, peer))

    def first(self, chunk):
        group, start, width = self.chunks[chunk]
        at = self.plain.index(chunk)
        if at >= RING:
            self.sent(self.plain[at - RING])
        self.cast(group)
        target = source = self.piece(chunk, self.dp, self.seq)
        if self.packed(group):
            source = self.own[group].at[:, pl.ds(start, width)]
            self.local(chunk, source, target)
        self.line(chunk, 0, source, self.dp)

    def relay(self, chunk):
        self.pass_on(chunk, 0, self.count + 7, self.dp)

    def second(self, chunk):
        group, start, width = self.chunks[chunk]
        columns = pl.ds(start, width)
        base, size = self.rows(group, self.dp, self.side)
        self.line_end(chunk, 0, self.dp)
        block = self.part(chunk, base, size)
        if self.packed(group):
            self.inside.pop(chunk).wait()
            source = block
        else:
            tile = 256
            joined, slab = self.joined[group], self.slabs[group]

            @pl.loop(0, width // tile)
            def _(at):
                span = pl.ds(pl.multiple_of(start + at * tile, tile), tile)
                stacked = [slab[place, :, span].astype(jnp.float32) for place in range(self.count)]
                joined[:, span] = jnp.concatenate(stacked, axis=0).astype(jnp.bfloat16)

            source = joined.at[:, columns]
            self.local(chunk, source, block)
        last = self.count - 1
        self.send(chunk, last, source, block, self.at(self.near, self.side))
        self.send(chunk, last + 1, source, block, self.at(self.far, self.side))
        self.send(chunk, last + 4, source, block, self.at(self.dp, 1 - self.side))

    def third(self, chunk):
        last = self.count - 1
        size = self.rows(self.chunks[chunk][0], self.dp, self.side)[1]
        self.exchange(chunk, last, last + 1, last + 2, last + 3, 0, size, (last + 5, last + 6))

    def exchange(self, chunk, one, two, three, four, offset, size, sides):
        group = self.chunks[chunk][0]
        half = size // 2
        other = self.at(self.dp, 1 - self.side)
        for place, which, onward, shift, peer, item in (
            (self.near, one, four, 0, self.far, 0),
            (self.far, two, three, half, self.near, 1),
        ):
            base = self.rows(group, place, self.side)[0] + offset
            block = self.part(chunk, base, size)
            self.arrived(chunk, which, block)
            piece = self.part(chunk, base + shift, half)
            self.send(chunk, onward, piece, piece, self.at(peer, self.side))
            if sides:
                self.send(chunk, sides[item], block, block, other)

    def diagonal(self, chunk, three, four, offset, size):
        base = self.rows(self.chunks[chunk][0], 3 - self.dp, self.side)[0] + offset
        half = size // 2
        self.arrived(chunk, four, self.part(chunk, base, half))
        self.arrived(chunk, three, self.part(chunk, base + half, half))

    def fourth(self, chunk):
        last = self.count - 1
        base, size = self.rows(self.chunks[chunk][0], 3 - self.dp, self.side)
        self.diagonal(chunk, last + 2, last + 3, 0, size)
        block = self.part(chunk, base, size)
        self.send(chunk, last + 7, block, block, self.at(self.dp, 1 - self.side))

    def fifth(self, chunk, first=None):
        first = self.count + 3 if first is None else first
        for which, place in enumerate(self.places):
            base, size = self.rows(self.chunks[chunk][0], place, 1 - self.side)
            self.arrived(chunk, first + which, self.part(chunk, base, size))

    def cross(self, chunk, phase):
        group, start, width = self.chunks[chunk]
        rows = self.masters[group].shape[0]
        mine = self.seq * rows
        hops = self.count - 1
        spare = 4 + 4 * hops
        if phase == 0:
            self.cast(group)
            source = self.own[group].at[:, pl.ds(start, width)]
            target = self.piece(chunk, self.dp, self.seq)
            self.local(chunk, source, target)
            self.send(chunk, 0, source, target, self.at(self.near, self.side))
            self.send(chunk, 1, source, target, self.at(self.far, self.side))
        if phase == 1:
            self.exchange(chunk, 0, 1, 2, 3, mine, rows, ())
            self.inside.pop(chunk).wait()
        if phase == 2:
            self.diagonal(chunk, 2, 3, mine, rows)
        for item, place in enumerate(self.places):
            base = 4 + item * hops
            if phase == 2 + item:
                piece = self.piece(chunk, place, self.seq)
                self.line(chunk, base, piece, place)
            if phase == 4 + item:
                self.pass_on(chunk, base, spare + item, place)
            if phase == 5 + item:
                self.line_end(chunk, base, place)
                start, size = self.rows(group, place, self.side)
                block = self.part(chunk, start, size)
                self.send(chunk, spare + 4 + item, block, block, self.at(self.dp, 1 - self.side))
        if phase == CROSS_PHASES - 1:
            self.fifth(chunk, spare + 4)


RING = 6
CROSS_PHASES = 10


def relative(dp, near, far):
    return (dp, near, far, 3 - dp)


def chunk_list(masters):
    chunks = []
    for group, shape in enumerate(masters):
        rows, width = shape
        step = width
        while rows * step > 32 * 1024 and step % 512 == 0:
            step //= 2
        if rows * step > 32 * 1024 and step % 384 == 0:
            step //= 3
        chunks += [(group, start, step) for start in range(0, width, step)]
    return chunks


def cross_chunks(masters, chunks, count):
    if count != 4 or masters[5][0] % 32 or masters[6][0] % 32:
        return []
    inner = [at for at, item in enumerate(chunks) if item[0] == 5]
    return inner[1:2] + [at for at, item in enumerate(chunks) if item[0] > 5]


def shifted(value, axis, steps):
    count = lax.axis_size(axis)
    first, last = (max(0, -steps), min(count, count - steps))
    return lax.ppermute(value, axis, [(source, source + steps) for source in range(first, last)])


def layer_norm(values):
    centre = values - jnp.mean(values, axis=-1, keepdims=True)
    spread = jnp.mean(centre * centre, axis=-1, keepdims=True)
    return centre * lax.rsqrt(spread + norm_eps)


def scaled_norm(values, norm_gain, norm_bias):
    return layer_norm(values) * norm_gain + norm_bias


def modulated(values, head_shift, head_scale):
    return layer_norm(values) * (1.0 + head_scale) + head_shift


def gelu_exact(values):
    return jax.nn.gelu(values, approximate=False)


def matmul(left_side, right_side):
    return jnp.dot(left_side, right_side, preferred_element_type=jnp.float32)


def matmul_left(left_side, right_side):
    return lax.dot_general(
        left_side, right_side, (((0,), (0,)), ((), ())), preferred_element_type=jnp.float32
    )


def matmul_right(left_side, right_side):
    return lax.dot_general(
        left_side, right_side, (((1,), (1,)), ((), ())), preferred_element_type=jnp.float32
    )


def split_heads(tensor):
    return tensor.reshape(tensor.shape[0], HEADS, HEAD_DIM).transpose(1, 0, 2)


def join_heads(tensor):
    return tensor.transpose(1, 0, 2).reshape(tensor.shape[1], HEADS * HEAD_DIM)


def head_forward(stacked, allowed):
    query_rows, key_rows, value_rows = stacked
    scores = jnp.where(
        allowed, matmul_right(query_rows, key_rows) * HEAD_DIM ** (-0.5), masked_fill
    )
    largest = jnp.max(scores, axis=1, keepdims=True)
    powered = jnp.exp(scores - largest)
    totals = jnp.sum(powered, axis=1, keepdims=True)
    weights = (powered / totals).astype(jnp.bfloat16)
    attended = matmul(weights, value_rows).astype(jnp.bfloat16)
    return (attended, (largest + jnp.log(totals))[:, 0])


def head_backward(stacked, allowed):
    query_rows, key_rows, value_rows, log_total, grad_rows = stacked
    scores = jnp.where(
        allowed, matmul_right(query_rows, key_rows) * HEAD_DIM ** (-0.5), masked_fill
    )
    weights = jnp.exp(scores - log_total[:, None])
    grad_weights = matmul_right(grad_rows, value_rows)
    row_inner = jnp.sum(weights * grad_weights, axis=1, keepdims=True)
    grad_scores = (weights * (grad_weights - row_inner)).astype(jnp.bfloat16)
    grad_query = matmul(grad_scores, key_rows) * HEAD_DIM ** (-0.5)
    grad_keys = matmul_left(grad_scores, query_rows) * HEAD_DIM ** (-0.5)
    grad_values = matmul_left(weights.astype(jnp.bfloat16), grad_rows)
    return (grad_query, grad_keys, grad_values)


def adam_step(master, gradient, moment, square, decays, rate):
    new_moment = beta_first * moment + (1.0 - beta_first) * gradient
    new_square = beta_second * square + (1.0 - beta_second) * gradient * gradient
    moment_hat = new_moment / (1.0 - beta_first**STEP)
    square_hat = new_square / (1.0 - beta_second**STEP)
    shrunk = master * (1.0 - rate * weight_decay * decays)
    return (shrunk - rate * moment_hat / (jnp.sqrt(square_hat) + adam_eps), new_moment, new_square)


def average_factors():
    total = 1.0 - ema_decay**STEP
    return (ema_decay * (1.0 - ema_decay ** (STEP - 1)) / total, (1.0 - ema_decay) / total)


def norm_rows(values):
    centre = values - jnp.mean(values, axis=-1, keepdims=True)
    spread = jnp.mean(centre * centre, axis=-1, keepdims=True)
    scale = lax.rsqrt(spread + norm_eps)
    return centre * scale, scale


def span(at, size):
    return pl.ds(pl.multiple_of(at * size, size), size)


class Moves:
    def __init__(self, sems):
        self.sems, self.used, self.open = sems, 0, []

    def start(self, source, target):
        copy = pltpu.make_async_copy(source, target, self.sems.at[self.used])
        self.used += 1
        copy.start()
        self.open.append(copy)
        return copy

    def finish(self):
        for copy in self.open:
            copy.wait()
        self.open = []


class Swaps:
    def __init__(self, sends, recvs):
        self.sends, self.recvs, self.used, self.open = sends, recvs, 0, []

    def start(self, source, target, peer):
        copy = remote(source, target, self.sends.at[self.used], self.recvs.at[self.used], peer)
        self.used += 1
        copy.start()
        self.open.append(copy)
        return copy

    def finish(self):
        for copy in self.open:
            copy.wait_send()
        self.open = []


class LineSum:
    def __init__(self, box, swaps):
        self.box, self.swaps = box, swaps
        dp, side, seq, near, far, along, _ = places()
        self.count = len(along) + 1
        self.spots = (seq, self.count + dp * 2 + side)
        self.hops = (
            [(dp, side, place) for place in along],
            [(place, side, seq) for place in (near, far, 3 - dp)]
            + [(place, 1 - side, seq) for place in (dp, near, far, 3 - dp)],
        )
        self.waiting = []
        self.level = 0

    def launch(self, value):
        spot = self.spots[self.level]
        self.box[spot] = value
        for peer in self.hops[self.level]:
            self.waiting.append(self.swaps.start(self.box.at[spot], self.box.at[spot], peer))

    def land(self):
        for copy in self.waiting:
            copy.wait_recv()
        first, size = ((0, self.count), (self.count, 8))[self.level]
        total = self.box[first]
        for place in range(first + 1, first + size):
            total = total + self.box[place]
        self.waiting = []
        self.level += 1
        return total


def all_peers():
    dp, side, seq, near, far, along, _ = places()
    peers = [(place, side, seq) for place in (near, far, 3 - dp)]
    peers += [(place, 1 - side, seq) for place in (dp, near, far, 3 - dp)]
    return peers + [(dp, side, place) for place in along]


AHEAD_SEQ = 2
AHEAD_DP = 0
TASKS = 3
CROSS_GAP = 5
NORM_STEP = 1


FORWARD_OUT = (
    ("block_low", D, jnp.bfloat16),
    ("head_out", HW, jnp.bfloat16),
    ("grad_branch", HW, jnp.bfloat16),
    ("grad_gate", HW, jnp.bfloat16),
    ("scale", HW, jnp.float32),
    ("slope_middle", HW, jnp.bfloat16),
    ("slope_cond", HW, jnp.bfloat16),
    ("slope_inner", 4 * D, jnp.bfloat16),
    ("hidden", D, jnp.float32),
    ("mixed", 3 * D, jnp.bfloat16),
    ("far_pair", 2 * D, jnp.bfloat16),
)
FORWARD_LOCAL = (
    ("normed", D, jnp.bfloat16),
    ("attended", D, jnp.bfloat16),
    ("second", D, jnp.bfloat16),
    ("activated", 4 * D, jnp.bfloat16),
    ("cond_low", HW, jnp.bfloat16),
    ("shift", HW, jnp.float32),
    ("gate", HW, jnp.float32),
    ("head_norm", HW, jnp.float32),
    ("shaped", HW, jnp.bfloat16),
    ("lifted", HW, jnp.bfloat16),
)


def head_mask(which):
    lane = lax.broadcasted_iota(jnp.int32, (1, 2 * HEAD_DIM), 1)
    inside = lane < HEAD_DIM if which == 0 else lane >= HEAD_DIM
    return jnp.where(inside, 1.0, 0.0).astype(jnp.bfloat16)


def softmax_columns(keys, queries, bias):
    scores = matmul_right(keys, queries) * HEAD_DIM ** (-0.5) + bias
    powered = jnp.exp(scores - jnp.max(scores, axis=0, keepdims=True))
    return powered / jnp.sum(powered, axis=0, keepdims=True)


def fill_bias(bias, far_row, own_row, side):
    rows = own_row.shape[-1]
    row = own_row[0:1, :]

    def column(ref):
        return jnp.broadcast_to(ref[0:1, :], (128, rows)).T[:, 0:1]

    near = column(own_row) == row
    wide = jnp.logical_and(column(far_row) == row, side == 1)
    bias[pl.ds(0, rows), :] = jnp.where(wide, 0.0, masked_fill)
    bias[pl.ds(rows, rows), :] = jnp.where(near, 0.0, masked_fill)


def pair_slices(mixed, far_pair, at):
    width = 2 * HEAD_DIM
    queries = mixed[:, span(at, width)]
    second = span(at + D // width, width)
    third = span(at + 2 * (D // width), width)
    keys = jnp.concatenate([far_pair[:, span(at, width)], mixed[:, second]], axis=0)
    values = jnp.concatenate([far_pair[:, second], mixed[:, third]], axis=0)
    return queries, keys, values


def forward_kernel(chunks, crossing, count, *refs):
    rest = list(refs)

    def take(number):
        taken = rest[:number]
        del rest[:number]
        return taken

    given = take(13)
    fulls, sides = take(8), take(8)
    outs = dict(zip([name for name, _, _ in FORWARD_OUT], take(len(FORWARD_OUT))))
    bias_out, norms_out = take(2)
    held = take(13)
    masters = held[:8]
    tokens, head_in, head_cotangent, ids, norm_rows_own = held[8:]
    weights = take(8)
    v = SimpleNamespace(**dict(zip([name for name, _, _ in FORWARD_OUT + FORWARD_LOCAL], take(21))))
    bias, own_row, far_row, box, norms = take(5)
    turned = take(3)
    own, slabs, joined = {}, {}, {}
    for group in range(8):
        if masters[group].shape[0] % 16 == 0:
            own[group] = rest.pop(0)
        else:
            slabs[group] = rest.pop(0)
            joined[group] = rest.pop(0)
    entry, *sems, locs, loads, moves_sem, swap_send, swap_recv, turn_sem, turn_send, turn_recv = rest

    dp, side, seq, near, far, along, _ = places()
    other = (dp, 1 - side, seq)
    entering = [
        pltpu.make_async_copy(source, target, entry.at[item])
        for item, (source, target) in enumerate(zip(given, held))
    ]
    for item in (0, 11, 12, 5, 8, 9, 6, 7, 1, 2, 3, 4, 10):
        entering[item].start()
    greet(all_peers())
    late = [at for at, item in enumerate(chunks) if item[0] == 5 and item[1] >= 2 * HW]
    plain = [at for at in range(len(chunks)) if at not in crossing + late] + late
    flow = Gather(chunks, entering, masters, fulls, own, slabs, joined, plain, sems, locs)
    moves = Moves(moves_sem)
    swaps = Swaps(swap_send, swap_recv)
    line = LineSum(box, swaps)
    place = (dp * 2 + side) * count + seq
    width = norm_rows_own.shape[1]
    norms[...] = jnp.zeros(norms.shape, jnp.float32)
    for item in (11, 12):
        entering[item].wait()
    norms[0:4, 0:width] = norm_rows_own[...].astype(jnp.bfloat16).astype(jnp.float32)
    spread = pltpu.roll(norms[...], place * width, 1)
    own_row[...] = jnp.broadcast_to(ids[...], own_row.shape).astype(jnp.float32)
    rows = tokens.shape[0]
    loading = {}
    turning = {0: [], 1: [], 2: []}
    landing = []

    def load(chunk):
        group, start, width = chunks[chunk]
        columns = pl.ds(start, width)
        if chunk in flow.inside:
            flow.inside.pop(chunk).wait()
        copy = pltpu.make_async_copy(
            fulls[group].at[:, columns], weights[group].at[:, columns], loads.at[chunk]
        )
        copy.start()
        loading[chunk] = copy

    def put(name):
        moves.start(getattr(v, name), outs[name])

    def share(group, source, which, done=False):
        depth = source.shape[0] if done else source.shape[1]
        buffer = turned[which]
        if not done:
            free(which)

            @pl.loop(0, depth // 256)
            def _(at):
                buffer[span(at, 256), :] = source[:, span(at, 256)].T

        size = depth // 8
        for place, block in enumerate(relative(dp, near, far)):
            mine = pl.multiple_of((block * 2 + side) * size, 16)
            theirs = pl.multiple_of((block * 2 + 1 - side) * size, 16)
            into = pl.ds(place * size, size)
            kept = pltpu.make_async_copy(
                buffer.at[pl.ds(mine, size), :],
                sides[group].at[into, pl.ds(0, rows)],
                turn_sem.at[group, place],
            )
            kept.start()
            turning[which].append(kept.wait)
            sent = remote(
                buffer.at[pl.ds(theirs, size), :],
                sides[group].at[into, pl.ds(rows, rows)],
                turn_send.at[group, place],
                turn_recv.at[group, place],
                other,
            )
            sent.start()
            turning[which].append(sent.wait_send)
            landing.append(sent)

    def free(which):
        for wait in turning[which]:
            wait()
        turning[which] = []

    def tiles(group, left, emit, start=0, width=None):
        width = weights[group].shape[1] if width is None else width

        @pl.loop(0, width // 256)
        def _(at):
            columns = span(at + start // 256, 256)
            emit(columns, matmul(left[...], weights[group][:, columns]))

    def stage_norm():
        norms[...] = line.land()
        moves.start(norms, norms_out)
        gain, offset = norms[0:1, :], norms[1:2, :]

        @pl.loop(0, rows // 64)
        def _(at):
            block = span(at, 64)
            values, _ = norm_rows(tokens[block, :].astype(jnp.float32))
            v.normed[block, :] = (values * gain + offset).astype(jnp.bfloat16)

        share(0, v.normed, 0)

    def stage_head_norm():
        @pl.loop(0, rows // 64)
        def _(at):
            block = span(at, 64)
            values, _ = norm_rows(head_in[block, :].astype(jnp.float32))
            v.head_norm[block, :] = values

    def stage_mixed(start, width):
        def emit(columns, total):
            v.mixed[:, columns] = total.astype(jnp.bfloat16)

        tiles(0, v.normed, emit, start, width)

    exchange = []

    def stage_swap():
        exchange.append(swaps.start(v.mixed.at[:, pl.ds(D, 2 * D)], v.far_pair, other))
        put("mixed")

    def stage_bias():
        for copy in exchange:
            copy.wait_recv()
        fill_bias(bias, far_row, own_row, side)
        moves.start(bias, bias_out)
        put("far_pair")
        free(1)

    def stage_heads(start, stop):
        @pl.loop(start, stop)
        def _(at):
            queries, keys, values = pair_slices(v.mixed, v.far_pair, at)
            total = None
            for which in range(2):
                mask = head_mask(which)
                weights_now = softmax_columns(keys, queries * mask, bias[...]).astype(jnp.bfloat16)
                part = matmul_left(values * mask, weights_now)
                total = part if total is None else total + part
            low = total.astype(jnp.bfloat16)
            turned[1][span(at, 2 * HEAD_DIM), :] = low
            v.attended[:, span(at, 2 * HEAD_DIM)] = low.T

    def stage_proj():
        share(1, turned[1].at[pl.ds(0, D), :], 1, True)

        def emit(columns, total):
            v.hidden[:, columns] = tokens[:, columns].astype(jnp.float32) + total

        tiles(1, v.attended, emit)
        put("hidden")
        gain, offset = norms[2:3, :], norms[3:4, :]

        @pl.loop(0, rows // 64)
        def _(at):
            block = span(at, 64)
            values, _ = norm_rows(v.hidden[block, :])
            v.second[block, :] = (values * gain + offset).astype(jnp.bfloat16)

        share(2, v.second, 0)

    def stage_up(start, width):
        def emit(columns, total):
            erf = lax.erf(total * 0.5**0.5)
            half = 0.5 * (1.0 + erf)
            v.activated[:, columns] = (total * half).astype(jnp.bfloat16)
            bell = jnp.exp(-0.5 * total * total) * (2.0 * 3.141592653589793) ** -0.5
            v.slope_inner[:, columns] = (half + total * bell).astype(jnp.bfloat16)

        tiles(2, v.second, emit, start, width)

    def stage_up_end():
        put("slope_inner")
        share(3, v.activated, 2)

    def stage_down(start, width):
        def emit(columns, total):
            v.block_low[:, columns] = (v.hidden[:, columns] + total).astype(jnp.bfloat16)

        tiles(3, v.activated, emit, start, width)

    def stage_down_end():
        put("block_low")
        share(4, v.block_low, 1)

    def stage_cond():
        def emit(columns, total):
            gates = jax.nn.sigmoid(total)
            v.cond_low[:, columns] = (total * gates).astype(jnp.bfloat16)
            slope = gates * (1.0 + total * (1.0 - gates))
            v.slope_cond[:, columns] = slope.astype(jnp.bfloat16)

        tiles(4, v.block_low, emit)
        put("slope_cond")
        share(5, v.cond_low, 0)

    def stage_mod(start, width):
        for at in range(start // 256, (start + width) // 256):
            total = matmul(v.cond_low[...], weights[5][:, at * 256 : (at + 1) * 256])
            part, block = divmod(at, HW // 256)
            columns = pl.ds(block * 256, 256)
            if part == 0:
                v.shift[:, columns] = total
            elif part == 1:
                scale = 1.0 + total
                v.scale[:, columns] = scale
                shaped = v.head_norm[:, columns] * scale + v.shift[:, columns]
                v.shaped[:, columns] = shaped.astype(jnp.bfloat16)
            else:
                v.gate[:, columns] = total
                grad = head_cotangent[:, columns].astype(jnp.float32) * total
                v.grad_branch[:, columns] = grad.astype(jnp.bfloat16)

    def stage_shaped():
        put("scale")
        share(6, v.shaped, 1)

    def stage_inner():
        def emit(columns, total):
            gates = jax.nn.sigmoid(total)
            v.lifted[:, columns] = (total * gates).astype(jnp.bfloat16)
            slope = gates * (1.0 + total * (1.0 - gates))
            v.slope_middle[:, columns] = slope.astype(jnp.bfloat16)

        tiles(6, v.shaped, emit)
        put("slope_middle")
        share(7, v.lifted, 0)

    def stage_outer():
        def emit(columns, total):
            v.shift[:, columns] = total
            grad = head_cotangent[:, columns].astype(jnp.float32) * total
            v.grad_gate[:, columns] = grad.astype(jnp.bfloat16)

        tiles(7, v.lifted, emit)
        put("grad_gate")

    def stage_gate():
        put("grad_branch")

        @pl.loop(0, HW // 256)
        def _(at):
            columns = span(at, 256)
            grown = head_in[:, columns].astype(jnp.float32) + v.gate[:, columns] * v.shift[:, columns]
            v.head_out[:, columns] = grown.astype(jnp.bfloat16)

        put("head_out")

    def chunk_tasks(chunk):
        group, start, width = chunks[chunk]
        final = start + width == weights[group].shape[1]
        if group == 0:
            tasks = [lambda: stage_mixed(start, width)]
            if final:
                tasks += [stage_swap, stage_bias]
                tasks += [functools.partial(stage_heads, at, at + 2) for at in range(0, 6, 2)]
        elif group == 1:
            tasks = [stage_proj]
        elif group == 2:
            tasks = [lambda: stage_up(start, width)]
            if final:
                tasks.append(stage_up_end)
        elif group == 3:
            tasks = [lambda: stage_down(start, width)]
            if final:
                tasks.append(stage_down_end)
        elif group == 4:
            tasks = [stage_cond]
        elif group == 5:
            tasks = [lambda: stage_mod(start, width)]
        elif group == 6:
            tasks = [stage_inner]
        else:
            tasks = [stage_outer]
        return [(chunk, task) for task in tasks]

    line.launch(spread)
    exchange.append(swaps.start(own_row, far_row, other))
    queue = [item for at in range(len(chunks)) if at not in late for item in chunk_tasks(at)]
    place = next(at for at, item in enumerate(queue) if chunks[item[0]][0] == 6)
    queue.insert(place, (queue[place - 1][0], stage_shaped))
    queue += [item for at in late for item in chunk_tasks(at)]
    queue.append((queue[-1][0], stage_gate))
    total = len(plain)
    arrived = set()
    pending = []
    for step in range(-AHEAD_SEQ, total + 4):
        if step + AHEAD_SEQ < total:
            flow.first(plain[step + AHEAD_SEQ])
        for item, chunk in enumerate(crossing):
            phase = step + AHEAD_SEQ - CROSS_GAP * item
            if 0 <= phase < CROSS_PHASES:
                flow.cross(chunk, phase)
                if phase == CROSS_PHASES - 1:
                    pending.append(chunk)
        if 0 <= step + AHEAD_DP + 1 < total:
            flow.relay(plain[step + AHEAD_DP + 1])
        if 0 <= step + AHEAD_DP < total:
            flow.second(plain[step + AHEAD_DP])
        if 0 <= step - 1 < total:
            flow.third(plain[step - 1])
        if step == -2:
            for item in (8, 9, 10):
                entering[item].wait()
            stage_head_norm()
        if step == NORM_STEP:
            line.launch(line.land())
        if step == NORM_STEP + 1:
            stage_norm()
        done = 0
        while queue and queue[0][0] in arrived and (done < TASKS or step >= total):
            chunk, task = queue.pop(0)
            if chunk in loading:
                loading.pop(chunk).wait()
            task()
            done += 1
        if 0 <= step - 2 < total:
            flow.fourth(plain[step - 2])
            flow.fifth(plain[step - 2])
            pending.append(plain[step - 2])
        for chunk in pending:
            load(chunk)
            arrived.add(chunk)
        pending = []
    flow.finish()
    moves.finish()
    swaps.finish()
    for which in range(3):
        free(which)
    for copy in landing:
        copy.wait_recv()


def forward_all(masters, tokens, head_in, head_cotangent, image_ids, norm_params):
    devices = lax.axis_size("dp") * lax.axis_size("side") * lax.axis_size("seq")
    count = lax.axis_size("seq")
    chunks = chunk_list([master.shape for master in masters])
    total = len(chunks)
    crossing = cross_chunks([master.shape for master in masters], chunks, count)
    rows = tokens.shape[0]
    low, full = jnp.bfloat16, jnp.float32
    fulls = [jax.ShapeDtypeStruct((devices * m.shape[0], m.shape[1]), low) for m in masters]
    sides = [jax.ShapeDtypeStruct((devices * m.shape[0] // 2, 2 * rows), low) for m in masters]
    outs = [jax.ShapeDtypeStruct((rows, width), kind) for _, width, kind in FORWARD_OUT]
    extra = [jax.ShapeDtypeStruct((2 * rows, rows), full), jax.ShapeDtypeStruct((8, D), full)]
    given = [*masters, tokens, head_in, head_cotangent, image_ids[None, :], norm_params.T]
    scratch = [pltpu.VMEM(item.shape, item.dtype) for item in given]
    scratch += [pltpu.VMEM(item.shape, low) for item in fulls]
    scratch += [pltpu.VMEM((rows, width), kind) for _, width, kind in FORWARD_OUT + FORWARD_LOCAL]
    scratch += [
        pltpu.VMEM((2 * rows, rows), full),
        pltpu.VMEM((8, rows), full),
        pltpu.VMEM((8, rows), full),
        pltpu.VMEM((count + 8, 8, D), full),
        pltpu.VMEM((8, D), full),
        pltpu.VMEM((HW, rows), low),
        pltpu.VMEM((HW, rows), low),
        pltpu.VMEM((4 * D, rows), low),
    ]
    for master in masters:
        depth, width = master.shape
        if depth % 16 == 0:
            scratch.append(pltpu.VMEM((depth, width), low))
        else:
            scratch.append(pltpu.VMEM((count, depth, width), low))
            scratch.append(pltpu.VMEM((count * depth, width), low))
    dma = pltpu.SemaphoreType.DMA
    scratch += [
        dma((13,)),
        dma((RING, count + 8)),
        dma((RING, count + 8)),
        dma((max(1, len(crossing)), 4 * count + 8)),
        dma((max(1, len(crossing)), 4 * count + 8)),
        dma((total,)),
        dma((total,)),
        dma((16,)),
        dma((8 + count,)),
        dma((8 + count,)),
        dma((8, 4)),
        dma((8, 4)),
        dma((8, 4)),
    ]
    hbm = pl.BlockSpec(memory_space=pltpu.HBM)
    results = pl.pallas_call(
        lambda *refs: forward_kernel(chunks, crossing, count, *refs),
        out_shape=fulls + sides + outs + extra,
        in_specs=[hbm] * 13,
        out_specs=[hbm] * (16 + len(outs) + 2),
        scratch_shapes=scratch,
        compiler_params=pltpu.CompilerParams(
            collective_id=0, has_side_effects=True, vmem_limit_bytes=63 * 2**20
        ),
        name="forward",
    )(*given)
    named = dict(zip([name for name, _, _ in FORWARD_OUT], results[16:]))
    named["bias"], named["norms"] = results[-2:]
    return results[:8], results[8:16], named


class Scatter:
    def __init__(self, chunks, parts, inbox, after, slabs, pieces, finals, squares, sends, recvs):
        self.chunks, self.parts, self.inbox, self.after = chunks, parts, inbox, after
        self.slabs, self.pieces, self.finals, self.squares = slabs, pieces, finals, squares
        self.sends, self.recvs = sends, recvs
        self.dp, self.side, self.seq, near, far, self.along, _ = places()
        self.near, self.far = (near, self.side, self.seq), (far, self.side, self.seq)
        self.count = len(self.along) + 1
        self.started = {}
        self.coming = {}

    def send(self, chunk, which, source, target, peer):
        slot = chunk % RING
        copy = remote(source, target, self.sends.at[slot, which], self.recvs.at[slot, which], peer)
        copy.start()
        self.started.setdefault(chunk, []).append(copy)
        self.coming[chunk, which] = copy

    def land(self, chunk, *which):
        for item in which:
            self.coming.pop((chunk, item)).wait_recv()

    def shape(self, chunk):
        group, start, width = self.chunks[chunk]
        size = self.parts[group].shape[1]
        return group, start, width, size, size // 2

    def first(self, chunk):
        group, start, width, size, half = self.shape(chunk)
        columns, part, inbox = pl.ds(start, width), self.parts[group], self.inbox[group]
        upper, lower = pl.ds(0, half), pl.ds(half, half)
        self.sent(chunk - RING)
        for item, block in enumerate((1, 3)):
            self.send(chunk, item, part.at[block, upper, columns], inbox.at[item, :, columns], self.near)
        for item, block in enumerate((2, 3)):
            self.send(
                chunk, 2 + item, part.at[block, lower, columns], inbox.at[2 + item, :, columns], self.far
            )

    def tiles(self, chunk, work):
        _, start, width, _, _ = self.shape(chunk)

        @pl.loop(0, width // 256)
        def _(at):
            work(pl.ds(pl.multiple_of(start + at * 256, 256), 256))

    def second(self, chunk):
        group, start, width, size, half = self.shape(chunk)
        columns, part, inbox = pl.ds(start, width), self.parts[group], self.inbox[group]
        upper, lower = pl.ds(0, half), pl.ds(half, half)
        self.land(chunk, 0, 1, 2, 3)

        def work(span_now):
            for block, rows, item in ((2, upper, 1), (1, lower, 3)):
                total = part[block, rows, span_now].astype(jnp.float32)
                total = total + inbox[item, :, span_now].astype(jnp.float32)
                part[block, rows, span_now] = total.astype(jnp.bfloat16)

        self.tiles(chunk, work)
        after = self.after[group]
        self.send(chunk, 4, part.at[1, lower, columns], after.at[0, :, columns], self.near)
        self.send(chunk, 5, part.at[2, upper, columns], after.at[1, :, columns], self.far)

    def third(self, chunk):
        group, start, width, size, half = self.shape(chunk)
        columns, part, inbox = pl.ds(start, width), self.parts[group], self.inbox[group]
        upper, lower = pl.ds(0, half), pl.ds(half, half)
        after = self.after[group]
        self.land(chunk, 4, 5)
        slab = self.slabs[group]
        depth = size // self.count

        def work(span_now):
            for rows, item, last, base in ((upper, 0, 1, 0), (lower, 2, 0, self.count // 2)):
                total = part[0, rows, span_now].astype(jnp.float32)
                total = total + inbox[item, :, span_now].astype(jnp.float32)
                total = total + after[last, :, span_now].astype(jnp.float32)
                for place in range(self.count // 2):
                    piece = total[place * depth : (place + 1) * depth].astype(jnp.bfloat16)
                    slab[base + place, :, span_now] = piece

        self.tiles(chunk, work)
        for step, peer in enumerate(self.along):
            self.send(
                chunk,
                6 + step,
                slab.at[peer, :, columns],
                self.pieces[group].at[step, :, columns],
                (self.dp, self.side, peer),
            )

    def fourth(self, chunk):
        group, start, width, size, half = self.shape(chunk)
        self.land(chunk, *(6 + step for step in range(self.count - 1)))
        slab, pieces, final = self.slabs[group], self.pieces[group], self.finals[group]

        def work(span_now):
            total = slab[self.seq, :, span_now].astype(jnp.float32)
            for step in range(self.count - 1):
                total = total + pieces[step, :, span_now].astype(jnp.float32)
            final[:, span_now] = total
            self.squares[0:1, :] += jnp.sum(total * total, axis=0, keepdims=True)

        self.tiles(chunk, work)

    def sent(self, chunk):
        for copy in self.started.pop(chunk, ()):
            copy.wait_send()

    def finish(self):
        for chunk in list(self.started):
            self.sent(chunk)


LAG = 1


BACKWARD_IN = (
    "grad_branch",
    "slope_middle",
    "head_in",
    "head_cotangent",
    "scale",
    "grad_gate",
    "slope_cond",
    "out_cotangent",
    "slope_inner",
    "hidden",
    "norms",
    "mixed",
    "far_pair",
    "bias",
    "tokens",
)


def norm_back(grads, values, scale):
    first = jnp.mean(grads, axis=-1, keepdims=True)
    second = jnp.mean(grads * values, axis=-1, keepdims=True)
    return scale * (grads - first - values * second)


def backward_kernel(chunks, count, *refs):
    rest = list(refs)

    def take(number):
        taken = rest[:number]
        del rest[:number]
        return taken

    weights, sides = take(8), take(8)
    given = dict(zip(BACKWARD_IN, take(len(BACKWARD_IN))))
    outs = take(12)
    finals = take(8)
    head_in_grad, tokens_grad, norm_grads, norm_out = take(4)
    grads, parts, inbox, after, slabs, pieces = (take(8) for _ in range(6))
    small, large, tile_box = take(3)
    into = {
        "grad_branch": grads[7].at[pl.ds(0, grads[7].shape[0] // 2), :],
        "slope_middle": grads[6].at[pl.ds(0, grads[6].shape[0] // 2), :],
        "grad_gate": grads[5].at[pl.ds(0, grads[5].shape[0] // 2), pl.ds(2 * HW, HW)],
        "slope_cond": grads[4].at[pl.ds(0, grads[4].shape[0] // 2), :],
        "slope_inner": grads[2].at[pl.ds(0, grads[2].shape[0] // 2), :],
    }
    held = [name for name in BACKWARD_IN if name not in into]
    local = SimpleNamespace(**dict(zip(held, take(10))))
    spare, block_grad, attended_grad, back_pair, squares, box, square_box = take(7)
    sends, recvs, load_sem, side_sem, tile_sem, swap_send, swap_recv, out_sem = rest

    dp, side, seq, near, far, along, _ = places()
    other = (dp, 1 - side, seq)
    greet(all_peers())
    rows = local.tokens.shape[0]
    own, pair = pl.ds(0, rows), pl.ds(rows, rows)
    swaps = Swaps(swap_send, swap_recv)
    moves = Moves(out_sem)
    flow = Scatter(chunks, parts, inbox, after, slabs, pieces, finals, squares, sends, recvs)
    loading = {}
    for item, name in enumerate(BACKWARD_IN):
        target = into[name] if name in into else getattr(local, name)
        loading[name] = pltpu.make_async_copy(given[name], target, load_sem.at[item])
    order = [group for group in range(7, -1, -1)]
    slim = [group for group in order if sides[group].shape[0] <= small.shape[1]]
    side_slot = {}
    side_copy = {}

    def side_load(group):
        depth = sides[group].shape[0]
        if group in slim:
            target = small.at[slim.index(group) % 2, pl.ds(0, depth), :]
        else:
            target = large
        side_slot[group] = target
        side_copy[group] = pltpu.make_async_copy(sides[group], target, side_sem.at[group])
        side_copy[group].start()

    def ready(*names):
        for name in names:
            loading.pop(name).wait()

    tile_list = [
        (group, at) for group in order for at in range(weights[group].shape[0] // 256)
    ]
    tile_copy = {}
    depth_box = tile_box.shape[0]

    def tile_load(item):
        if item >= len(tile_list):
            return
        group, at = tile_list[item]
        copy = pltpu.make_async_copy(
            weights[group].at[pl.ds(at * 256, 256), :],
            tile_box.at[item % depth_box, :, pl.ds(0, weights[group].shape[1])],
            tile_sem.at[item % depth_box],
        )
        tile_copy[item] = copy
        copy.start()

    loading["grad_branch"].start()
    for item in range(depth_box):
        tile_load(item)
    loading["slope_middle"].start()
    side_load(slim[0])
    side_load(slim[1])
    for name in BACKWARD_IN[2:]:
        loading[name].start()
    for group in order:
        if group not in slim:
            side_load(group)
    squares[...] = jnp.zeros_like(squares)
    norm_grads[...] = jnp.zeros_like(norm_grads)
    at_tile = [0]

    def back(group, emit):
        width = weights[group].shape[1]
        for at in range(weights[group].shape[0] // 256):
            item = at_tile[0]
            at_tile[0] += 1
            tile_copy.pop(item).wait()
            total = matmul_right(
                grads[group][own, :], tile_box[item % depth_box, :, pl.ds(0, width)]
            )
            emit(pl.ds(at * 256, 256), total)
            tile_load(item + depth_box)

    coming = {}

    def share(group):
        coming[group] = swaps.start(grads[group].at[own, :], grads[group].at[pair, :], other)

    def product(chunk):
        group, start, width = chunks[chunk]
        if group in coming:
            coming.pop(group).wait_recv()
            side_copy.pop(group).wait()
        left, part = side_slot[group], parts[group]
        size = part.shape[1]
        whole = group in slim

        @pl.loop(0, width // 256)
        def _(at):
            columns = pl.ds(pl.multiple_of(start + at * 256, 256), 256)
            right = grads[group][:, columns]
            if whole:
                total = matmul(left[...], right).astype(jnp.bfloat16)
                for block in range(4):
                    part[block, :, columns] = total[block * size : (block + 1) * size]
            else:
                for block in range(4):
                    total = matmul(left[pl.ds(block * size, size), :], right)
                    part[block, :, columns] = total.astype(jnp.bfloat16)

        if start + width == weights[group].shape[1]:
            if group in slim and slim.index(group) + 2 < len(slim):
                side_load(slim[slim.index(group) + 2])

    def step(chunk):
        total = len(chunks)
        if chunk < total:
            product(chunk)
            flow.first(chunk)
        if 0 <= chunk - LAG < total:
            flow.second(chunk - LAG)
        if 0 <= chunk - LAG - 1 < total:
            flow.third(chunk - LAG - 1)
        if 0 <= chunk - LAG - 2 < total:
            flow.fourth(chunk - LAG - 2)
            group, start, width = chunks[chunk - LAG - 2]
            columns = pl.ds(start, width)
            moves.start(finals[group].at[:, columns], outs[group].at[:, columns])

    def stage_outer():
        ready("grad_branch")
        share(7)
        ready("slope_middle")

        def emit(columns, total):
            slope = grads[6][own, columns].astype(jnp.float32)
            grads[6][own, columns] = (total * slope).astype(jnp.bfloat16)

        back(7, emit)
        share(6)

    def stage_inner():
        def emit(columns, total):
            spare[:, columns] = total

        back(6, emit)
        ready("head_in", "head_cotangent", "scale", "grad_gate")

        @pl.loop(0, rows // 32)
        def _(at):
            block = span(at, 32)
            values, scale = norm_rows(local.head_in[block, :].astype(jnp.float32))
            grad = spare[block, pl.ds(0, HW)]
            grads[5][block, pl.ds(0, HW)] = grad.astype(jnp.bfloat16)
            grads[5][block, pl.ds(HW, HW)] = (grad * values).astype(jnp.bfloat16)
            passed = norm_back(grad * local.scale[block, :], values, scale)
            head_in_grad[block, :] = local.head_cotangent[block, :].astype(jnp.float32) + passed

        share(5)
        moves.start(head_in_grad, outs[8])

    def stage_mod():
        ready("slope_cond")

        def emit(columns, total):
            slope = grads[4][own, columns].astype(jnp.float32)
            grads[4][own, columns] = (total * slope).astype(jnp.bfloat16)

        back(5, emit)
        share(4)

    def stage_cond():
        ready("out_cotangent")

        def emit(columns, total):
            grad = local.out_cotangent[:, columns].astype(jnp.float32) + total
            block_grad[:, columns] = grad
            grads[3][own, columns] = grad.astype(jnp.bfloat16)

        back(4, emit)
        share(3)

    def stage_down():
        ready("slope_inner")

        def emit(columns, total):
            slope = grads[2][own, columns].astype(jnp.float32)
            grads[2][own, columns] = (total * slope).astype(jnp.bfloat16)

        back(3, emit)
        share(2)

    def norm_stage(source, base, emit):
        gain = local.norms[base : base + 1, :]

        @pl.loop(0, rows // 32)
        def _(at):
            block = span(at, 32)
            values, scale = norm_rows(source[block, :].astype(jnp.float32))
            grad = spare[block, pl.ds(0, D)]
            norm_grads[base : base + 1, :] += jnp.sum(grad * values, axis=0, keepdims=True)
            norm_grads[base + 1 : base + 2, :] += jnp.sum(grad, axis=0, keepdims=True)
            emit(block, norm_back(grad * gain, values, scale))

    def stage_up():
        def keep(columns, total):
            spare[:, columns] = total

        back(2, keep)
        ready("hidden", "norms")

        def emit(block, passed):
            grad = block_grad[block, :] + passed
            tokens_grad[block, :] = grad
            grads[1][block, :] = grad.astype(jnp.bfloat16)

        norm_stage(local.hidden, 2, emit)
        share(1)

    def stage_proj():
        def emit(columns, total):
            attended_grad[:, columns] = total.astype(jnp.bfloat16)

        back(1, emit)
        ready("mixed", "far_pair", "bias")

    def stage_heads(start, stop):
        width = 2 * HEAD_DIM
        scaling = HEAD_DIM ** (-0.5)

        @pl.loop(start, stop)
        def _(at):
            queries, keys, values = pair_slices(local.mixed, local.far_pair, at)
            outer = attended_grad[:, span(at, width)]
            query_part = key_part = value_part = None
            for which in range(2):
                mask = head_mask(which)
                query_now, outer_now = queries * mask, outer * mask
                chances = softmax_columns(keys, query_now, local.bias[...])
                slopes = matmul_right(values, outer_now)
                inner = jnp.sum(chances * slopes, axis=0, keepdims=True)
                score_grad = (chances * (slopes - inner)).astype(jnp.bfloat16)
                value_now = matmul(chances.astype(jnp.bfloat16), outer_now)
                key_now = matmul(score_grad, query_now)
                query_side = matmul_left(keys * mask, score_grad)
                if which == 0:
                    query_part, key_part, value_part = query_side, key_now, value_now
                else:
                    query_part = query_part + query_side
                    key_part = key_part + key_now
                    value_part = value_part + value_now
            grads[0][own, span(at, width)] = (query_part * scaling).astype(jnp.bfloat16).T
            key_part = key_part * scaling
            first, second = span(at, width), span(at + D // width, width)
            local.far_pair[:, first] = key_part[:rows].astype(jnp.bfloat16)
            local.far_pair[:, second] = value_part[:rows].astype(jnp.bfloat16)
            spare[:, first] = key_part[rows:]
            spare[:, second] = value_part[rows:]

    def stage_return():
        coming["back"] = swaps.start(local.far_pair, back_pair, other)

    def stage_merge():
        coming.pop("back").wait_recv()

        @pl.loop(0, 2 * D // 256)
        def _(at):
            columns = span(at, 256)
            total = spare[:, columns] + back_pair[:, columns].astype(jnp.float32)
            grads[0][own, span(at + D // 256, 256)] = total.astype(jnp.bfloat16)

        share(0)

    def stage_attend():
        def keep(columns, total):
            spare[:, columns] = total

        back(0, keep)
        ready("tokens")

        def emit(block, passed):
            tokens_grad[block, :] = tokens_grad[block, :] + passed

        norm_stage(local.tokens, 0, emit)
        moves.start(tokens_grad, outs[9])

    stage_outer()
    stages = [
        stage_inner,
        stage_mod,
        stage_cond,
        stage_down,
        stage_up,
        stage_proj,
        lambda: stage_heads(0, 2),
        lambda: stage_heads(2, 4),
        lambda: stage_heads(4, 6),
        stage_return,
        stage_merge,
        stage_attend,
    ]
    line = LineSum(box, swaps)
    total = len(chunks)
    for chunk in range(total + LAG + 3):
        group = chunks[min(chunk, total - 1)][0]
        needed = {7: 0, 6: 0, 5: 1, 4: 2, 3: 3, 2: 4, 1: 5, 0: 11}[group]
        while stages and 12 - len(stages) < needed:
            stages.pop(0)()
        step(chunk)
        if stages:
            stages.pop(0)()
            if not stages:
                line.launch(norm_grads[...])
        elif line.level == 0:
            line.launch(line.land())
        elif line.level == 1:
            sums = line.land()
            norm_grads[...] = sums
            moves.start(norm_grads, outs[10])
    last = LineSum(square_box, swaps)
    last.launch(squares[...])
    last.launch(last.land())
    sums = norm_grads[...]
    flat = jnp.sum(last.land(), axis=0, keepdims=True)
    whole = jnp.sum(flat, axis=1, keepdims=True)
    extra = jnp.sum(jnp.sum(sums * sums, axis=0, keepdims=True), axis=1, keepdims=True)
    norm_out[...] = jnp.broadcast_to(jnp.sqrt(whole + extra), norm_out.shape)
    moves.start(norm_out, outs[11])
    flow.finish()
    swaps.finish()
    moves.finish()


def backward_chunks(masters):
    chunks = chunk_list(masters)
    chunks = [item for group in range(7, -1, -1) for item in chunks if item[0] == group]
    group, start, width = chunks.pop()
    for size in (width - width // 2 // 256 * 256, width // 2 // 256 * 256):
        chunks.append((group, start, size)) if size else None
        start += size
    return chunks


def backward_all(masters, weights, sides, named):
    count = lax.axis_size("seq")
    shapes = [master.shape for master in masters]
    chunks = backward_chunks(shapes)
    total = len(chunks)
    rows = named["tokens"].shape[0]
    low, full = jnp.bfloat16, jnp.float32
    hbm = pl.BlockSpec(memory_space=pltpu.HBM)
    given = [named[name] for name in BACKWARD_IN]
    outs = [jax.ShapeDtypeStruct(shape, full) for shape in shapes]
    outs += [
        jax.ShapeDtypeStruct((rows, HW), full),
        jax.ShapeDtypeStruct((rows, D), full),
        jax.ShapeDtypeStruct((8, D), full),
        jax.ShapeDtypeStruct((8, 128), full),
    ]
    scratch = [pltpu.VMEM(item.shape, full) for item in outs]
    scratch += [pltpu.VMEM((2 * rows, width), low) for _, width in shapes]
    scratch += [pltpu.VMEM((4, count * depth, width), low) for depth, width in shapes]
    scratch += [pltpu.VMEM((4, count * depth // 2, width), low) for depth, width in shapes]
    scratch += [pltpu.VMEM((2, count * depth // 2, width), low) for depth, width in shapes]
    scratch += [pltpu.VMEM((count, depth, width), low) for depth, width in shapes]
    scratch += [pltpu.VMEM((count - 1, depth, width), low) for depth, width in shapes]
    scratch += [
        pltpu.VMEM((2, HW // 2, 2 * rows), low),
        pltpu.VMEM((2 * D, 2 * rows), low),
        pltpu.VMEM((3, 256, 3 * HW), low),
        pltpu.VMEM((rows, HW), low),
        pltpu.VMEM((rows, HW), low),
        pltpu.VMEM((rows, HW), full),
        pltpu.VMEM((rows, D), low),
        pltpu.VMEM((rows, D), full),
        pltpu.VMEM((8, D), full),
        pltpu.VMEM((rows, 3 * D), low),
        pltpu.VMEM((rows, 2 * D), low),
        pltpu.VMEM((2 * rows, rows), full),
        pltpu.VMEM((rows, D), low),
        pltpu.VMEM((rows, 2 * D), full),
        pltpu.VMEM((rows, D), full),
        pltpu.VMEM((rows, D), low),
        pltpu.VMEM((rows, 2 * D), low),
        pltpu.VMEM((8, 256), full),
        pltpu.VMEM((count + 8, 8, D), full),
        pltpu.VMEM((count + 8, 8, 256), full),
    ]
    dma = pltpu.SemaphoreType.DMA
    scratch += [
        dma((RING, 5 + count)),
        dma((RING, 5 + count)),
        dma((len(BACKWARD_IN),)),
        dma((8,)),
        dma((3,)),
        dma((21 + 2 * count,)),
        dma((21 + 2 * count,)),
        dma((total + 4,)),
    ]
    return pl.pallas_call(
        lambda *refs: backward_kernel(chunks, count, *refs),
        out_shape=outs,
        in_specs=[hbm] * (16 + len(given)),
        out_specs=[hbm] * len(outs),
        scratch_shapes=scratch,
        compiler_params=pltpu.CompilerParams(
            collective_id=1, has_side_effects=True, vmem_limit_bytes=64 * 2**20
        ),
        name="backward",
    )(*weights, *sides, *given)


def optimizer_kernel(*refs):
    rest = list(refs)

    def take(number):
        taken = rest[:number]
        del rest[:number]
        return taken

    given = [take(5) for _ in range(8)]
    passed = take(4)
    small_given = take(6)
    results = [take(4) for _ in range(8)]
    kept = take(4)
    small_outs = take(4)
    small_held, small_results = take(6), take(4)
    small, grad_norm = small_held[:5], small_held[5]
    held = [take(5) for _ in range(8)]
    made = [take(4) for _ in range(8)]
    carried = take(4)
    load_sem, save_sem, pass_sem, small_sem = rest
    loads, saves, first = [], [], []
    for item in range(6):
        copy = pltpu.make_async_copy(small_given[item], small_held[item], small_sem.at[item])
        copy.start()
        first.append(copy)
    for group in range(8):
        for item in range(5):
            copy = pltpu.make_async_copy(
                given[group][item], held[group][item], load_sem.at[group, item]
            )
            copy.start()
            loads.append(copy)
    for item in range(4):
        pltpu.make_async_copy(passed[item], carried[item], pass_sem.at[0, item]).start()
    for copy in first:
        copy.wait()
    factor = jnp.minimum(1.0, clip_limit / (grad_norm[0:1, 0:1] + 1e-06))
    keep_old, take_new = average_factors()

    def update(source, target, columns, decays, rate):
        gradient, master, moment, square, average = (ref[:, columns] for ref in source)
        put(gradient, master, moment, square, average, target, columns, decays, rate)

    def put(gradient, master, moment, square, average, target, columns, decays, rate):
        fresh = adam_step(master, gradient * factor, moment, square, decays, rate)
        for item in range(3):
            target[item][:, columns] = fresh[item]
        target[3][:, columns] = keep_old * average + take_new * fresh[0]

    width = small[1].shape[1]
    total = small[0].shape[1]
    place = (lax.axis_index("dp") * 2 + lax.axis_index("side")) * lax.axis_size(
        "seq"
    ) + lax.axis_index("seq")
    turned = pltpu.roll(small[0][...], lax.rem(total - place * width, total), 1)
    own = [turned[0:4, 0:width]] + [ref[...] for ref in small[1:]]
    put(*own, small_results, slice(None), 0.0, learn_rates[8])
    for item in range(4):
        copy = pltpu.make_async_copy(
            small_results[item], small_outs[item], small_sem.at[6 + item]
        )
        copy.start()
        saves.append(copy)
    for group in range(8):
        for item in range(5):
            loads[group * 5 + item].wait()

        @pl.loop(0, held[group][0].shape[1] // 256)
        def _(at):
            columns = pl.ds(pl.multiple_of(at * 256, 256), 256)
            update(held[group], made[group], columns, 1.0, learn_rates[group])

        for item in range(4):
            copy = pltpu.make_async_copy(
                made[group][item], results[group][item], save_sem.at[group, item]
            )
            copy.start()
            saves.append(copy)
        if group % 2:
            item = group // 2
            pltpu.make_async_copy(passed[item], carried[item], pass_sem.at[0, item]).wait()
            copy = pltpu.make_async_copy(carried[item], kept[item], pass_sem.at[1, item])
            copy.start()
            saves.append(copy)
    for copy in saves:
        copy.wait()


def optimizer_all(gradients, passed, norm_grads, grad_norm, masters, moments, squares, averages):
    full = jnp.float32
    hbm = pl.BlockSpec(memory_space=pltpu.HBM)
    given = []
    for group in range(8):
        given += [
            gradients[group],
            masters[group],
            moments[group],
            squares[group],
            averages[group],
        ]
    small = [masters[8].T, moments[8].T, squares[8].T, averages[8].T]
    given += [*passed, norm_grads, *small, grad_norm]
    shapes = [master.shape for master in masters[:8]]
    outs = [jax.ShapeDtypeStruct(shape, full) for shape in shapes for _ in range(4)]
    outs += [jax.ShapeDtypeStruct(item.shape, item.dtype) for item in passed]
    outs += [jax.ShapeDtypeStruct(small[0].shape, full) for _ in range(4)]
    scratch = [pltpu.VMEM(item.shape, full) for item in given[44:] + outs[36:]]
    scratch += [pltpu.VMEM(shape, full) for shape in shapes for _ in range(5)]
    scratch += [pltpu.VMEM(shape, full) for shape in shapes for _ in range(4)]
    scratch += [pltpu.VMEM(item.shape, item.dtype) for item in passed]
    dma = pltpu.SemaphoreType.DMA
    scratch += [dma((8, 5)), dma((8, 4)), dma((2, 4)), dma((10,))]
    results = pl.pallas_call(
        optimizer_kernel,
        out_shape=outs,
        in_specs=[hbm] * len(given),
        out_specs=[hbm] * len(outs),
        scratch_shapes=scratch,
        compiler_params=pltpu.CompilerParams(vmem_limit_bytes=63 * 2**20),
        name="optimizer",
    )(*given)
    fresh = [results[4 * group : 4 * group + 4] for group in range(8)]
    return results[32:36], fresh + [[item.T for item in results[36:]]]


def body(*arrays):
    tokens, head_in, image_ids, out_cotangent, head_cotangent = arrays[:5]
    masters, moments, squares, averages = (arrays[at : at + 9] for at in (5, 14, 23, 32))
    sides = lax.axis_size("dp") == 4 and lax.axis_size("side") == 2
    if not sides or masters[0].shape[0] % 8 or lax.axis_size("seq") != 4:
        return plain_body(*arrays)
    weights, turned, named = forward_all(
        masters[:8], tokens, head_in, head_cotangent, image_ids, masters[8]
    )
    named = dict(
        named,
        tokens=tokens,
        head_in=head_in,
        head_cotangent=head_cotangent,
        out_cotangent=out_cotangent,
    )
    results = backward_all(masters[:8], weights, turned, named)
    gradients = results[:8]
    head_in_grad, tokens_grad, norm_grads, grad_norm = results[8:]
    passed = [named["block_low"], named["head_out"], tokens_grad, head_in_grad]
    passed, fresh = optimizer_all(
        gradients, passed, norm_grads, grad_norm, masters, moments, squares, averages
    )
    return (
        (*passed, grad_norm[0, 0])
        + tuple(item for group in fresh for item in group[:3])
        + tuple(group[3] for group in fresh)
    )


def plain_body(
    tokens,
    head_in,
    image_ids,
    out_cotangent,
    head_cotangent,
    weight_attend,
    weight_proj,
    weight_up,
    weight_down,
    weight_cond,
    weight_mod,
    weight_inner,
    weight_outer,
    norm_params,
    mean_attend,
    mean_proj,
    mean_up,
    mean_down,
    mean_cond,
    mean_mod,
    mean_inner,
    mean_outer,
    mean_norms,
    square_attend,
    square_proj,
    square_up,
    square_down,
    square_cond,
    square_mod,
    square_inner,
    square_outer,
    square_norms,
    ema_attend,
    ema_proj,
    ema_up,
    ema_down,
    ema_cond,
    ema_mod,
    ema_inner,
    ema_outer,
    ema_norms,
):
    used = (
        lax.all_gather(
            weight_attend.astype(jnp.bfloat16), AXES, axis=0, tiled=True
        ),
        lax.all_gather(weight_proj.astype(jnp.bfloat16), AXES, axis=0, tiled=True),
        lax.all_gather(weight_up.astype(jnp.bfloat16), AXES, axis=0, tiled=True),
        lax.all_gather(weight_down.astype(jnp.bfloat16), AXES, axis=0, tiled=True),
        lax.all_gather(weight_cond.astype(jnp.bfloat16), AXES, axis=0, tiled=True),
        lax.all_gather(weight_mod.astype(jnp.bfloat16), AXES, axis=0, tiled=True),
        lax.all_gather(
            weight_inner.astype(jnp.bfloat16), AXES, axis=0, tiled=True
        ),
        lax.all_gather(
            weight_outer.astype(jnp.bfloat16), AXES, axis=0, tiled=True
        ),
        lax.all_gather(norm_params.astype(jnp.bfloat16), AXES, axis=0, tiled=True),
    )
    use_attend, use_proj, use_up, use_down, use_cond, use_mod, use_inner, use_outer, use_norms = (
        used
    )
    norm_set = use_norms.astype(jnp.float32)
    inputs = tokens.astype(jnp.float32)
    row_count = tokens.shape[0]
    normed, first_back = jax.vjp(scaled_norm, inputs, norm_set[:, 0], norm_set[:, 1])
    normed_low = normed.astype(jnp.bfloat16)
    mixed_rows = matmul(normed_low, use_attend).astype(jnp.bfloat16)
    query_heads = split_heads(mixed_rows[:, :D])
    own_keys = split_heads(mixed_rows[:, D : 2 * D])
    own_values = split_heads(mixed_rows[:, 2 * D :])
    own_images = image_ids.astype(jnp.bfloat16)
    far_pair, far_images = shifted((mixed_rows[:, D:], own_images), "side", 1)
    both_keys = jnp.concatenate([split_heads(far_pair[:, :D]), own_keys], axis=1)
    both_values = jnp.concatenate([split_heads(far_pair[:, D:]), own_values], axis=1)
    near_allowed = own_images[:, None] == own_images[None, :]
    wide_allowed = own_images[:, None] == jnp.concatenate([far_images, own_images])[None, :]
    masked_side = lax.axis_index("side") == 1

    def visible_forward():
        return lax.map(
            lambda stacked: head_forward(stacked, near_allowed), (query_heads, own_keys, own_values)
        )

    def masked_forward():
        return lax.map(
            lambda stacked: head_forward(stacked, wide_allowed),
            (query_heads, both_keys, both_values),
        )

    attended_heads, log_totals = lax.cond(masked_side, masked_forward, visible_forward)
    attended = join_heads(attended_heads)
    hidden = inputs + matmul(attended, use_proj)
    second, second_back = jax.vjp(scaled_norm, hidden, norm_set[:, 2], norm_set[:, 3])
    second_low = second.astype(jnp.bfloat16)
    inner_pre = matmul(second_low, use_up)
    activated_full, gelu_back = jax.vjp(gelu_exact, inner_pre)
    activated = activated_full.astype(jnp.bfloat16)
    block_low = (hidden + matmul(activated, use_down)).astype(jnp.bfloat16)
    condition = matmul(block_low, use_cond)
    lifted_cond, cond_back = jax.vjp(jax.nn.silu, condition)
    cond_low = lifted_cond.astype(jnp.bfloat16)
    modulation = matmul(cond_low, use_mod)
    head_shift = modulation[:, :HW]
    head_scale = modulation[:, HW : 2 * HW]
    head_gate = modulation[:, 2 * HW :]
    head_rows = head_in.astype(jnp.float32)
    shaped, shaped_back = jax.vjp(modulated, head_rows, head_shift, head_scale)
    shaped_low = shaped.astype(jnp.bfloat16)
    middle = matmul(shaped_low, use_inner)
    lifted_full, middle_back = jax.vjp(jax.nn.silu, middle)
    lifted_rows = lifted_full.astype(jnp.bfloat16)
    branch = matmul(lifted_rows, use_outer)
    head_out = (head_rows + head_gate * branch).astype(jnp.bfloat16)
    head_grad = head_cotangent.astype(jnp.float32)
    grad_branch = (head_grad * head_gate).astype(jnp.bfloat16)
    grad_outer = matmul_left(lifted_rows, grad_branch)
    grad_middle = middle_back(matmul_right(grad_branch, use_outer))[0].astype(jnp.bfloat16)
    grad_inner = matmul_left(shaped_low, grad_middle)
    head_part, grad_shift, grad_scale = shaped_back(matmul_right(grad_middle, use_inner))
    head_in_grad = head_grad + head_part
    grad_modulation = jnp.concatenate([grad_shift, grad_scale, head_grad * branch], axis=1).astype(
        jnp.bfloat16
    )
    grad_mod = matmul_left(cond_low, grad_modulation)
    grad_condition = cond_back(matmul_right(grad_modulation, use_mod))[0].astype(jnp.bfloat16)
    grad_cond = matmul_left(block_low, grad_condition)
    grad_block = out_cotangent.astype(jnp.float32) + matmul_right(grad_condition, use_cond)
    grad_feed = grad_block.astype(jnp.bfloat16)
    grad_down = matmul_left(activated, grad_feed)
    grad_inner_pre = gelu_back(matmul_right(grad_feed, use_down))[0].astype(jnp.bfloat16)
    grad_up = matmul_left(second_low, grad_inner_pre)
    hidden_part, grad_gain_two, grad_bias_two = second_back(matmul_right(grad_inner_pre, use_up))
    grad_hidden = grad_block + hidden_part
    grad_proj_out = grad_hidden.astype(jnp.bfloat16)
    grad_proj = matmul_left(attended, grad_proj_out)
    grad_attended = split_heads(matmul_right(grad_proj_out, use_proj).astype(jnp.bfloat16))

    def visible_backward():
        grad_query, grad_keys, grad_values = lax.map(
            lambda stacked: head_backward(stacked, near_allowed),
            (query_heads, own_keys, own_values, log_totals, grad_attended),
        )
        zero_fill = jnp.zeros_like(grad_keys)
        return (
            grad_query,
            jnp.concatenate([zero_fill, grad_keys], axis=1),
            jnp.concatenate([zero_fill, grad_values], axis=1),
        )

    def masked_backward():
        return lax.map(
            lambda stacked: head_backward(stacked, wide_allowed),
            (query_heads, both_keys, both_values, log_totals, grad_attended),
        )

    grad_query, grad_keys, grad_values = lax.cond(masked_side, masked_backward, visible_backward)
    far_grad = jnp.concatenate(
        [join_heads(grad_keys[:, :row_count]), join_heads(grad_values[:, :row_count])], axis=1
    )
    returned = shifted(far_grad.astype(jnp.bfloat16), "side", -1).astype(far_grad.dtype)
    near_grad = (
        jnp.concatenate(
            [join_heads(grad_keys[:, row_count:]), join_heads(grad_values[:, row_count:])], axis=1
        )
        + returned
    )
    grad_mixed = jnp.concatenate([join_heads(grad_query), near_grad], axis=1).astype(jnp.bfloat16)
    grad_attend = matmul_left(normed_low, grad_mixed)
    tokens_part, grad_gain_one, grad_bias_one = first_back(matmul_right(grad_mixed, use_attend))
    tokens_grad = grad_hidden + tokens_part
    grad_norms = jnp.stack([grad_gain_one, grad_bias_one, grad_gain_two, grad_bias_two], axis=1)
    owned = (
        lax.psum_scatter(grad_attend, AXES, scatter_dimension=0, tiled=True),
        lax.psum_scatter(grad_proj, AXES, scatter_dimension=0, tiled=True),
        lax.psum_scatter(grad_up, AXES, scatter_dimension=0, tiled=True),
        lax.psum_scatter(grad_down, AXES, scatter_dimension=0, tiled=True),
        lax.psum_scatter(grad_cond, AXES, scatter_dimension=0, tiled=True),
        lax.psum_scatter(grad_mod, AXES, scatter_dimension=0, tiled=True),
        lax.psum_scatter(grad_inner, AXES, scatter_dimension=0, tiled=True),
        lax.psum_scatter(grad_outer, AXES, scatter_dimension=0, tiled=True),
        lax.psum_scatter(grad_norms, AXES, scatter_dimension=0, tiled=True),
    )
    local_squares = sum((jnp.sum(gradient * gradient) for gradient in owned))
    grad_norm = jnp.sqrt(lax.psum(local_squares, AXES))
    factor = jnp.minimum(1.0, clip_limit / (grad_norm + 1e-06))
    masters = [
        weight_attend,
        weight_proj,
        weight_up,
        weight_down,
        weight_cond,
        weight_mod,
        weight_inner,
        weight_outer,
        norm_params,
    ]
    moments = [
        mean_attend,
        mean_proj,
        mean_up,
        mean_down,
        mean_cond,
        mean_mod,
        mean_inner,
        mean_outer,
        mean_norms,
    ]
    squares = [
        square_attend,
        square_proj,
        square_up,
        square_down,
        square_cond,
        square_mod,
        square_inner,
        square_outer,
        square_norms,
    ]
    averages = [
        ema_attend,
        ema_proj,
        ema_up,
        ema_down,
        ema_cond,
        ema_mod,
        ema_inner,
        ema_outer,
        ema_norms,
    ]
    keep_old, take_new = average_factors()
    results = []
    smoothed = []
    for position in range(9):
        decays = 1.0 if position < 8 else 0.0
        fresh = adam_step(
            masters[position],
            owned[position] * factor,
            moments[position],
            squares[position],
            decays,
            learn_rates[position],
        )
        results.extend(fresh)
        smoothed.append(keep_old * averages[position] + take_new * fresh[0])
    return (
        (block_low, head_out, tokens_grad, head_in_grad, grad_norm)
        + tuple(results)
        + tuple(smoothed)
    )


def solution(mesh):
    rows, line = P(AXES, None), P(AXES)
    in_specs = (rows, rows, line) + (rows,) * 38
    out_specs = (rows,) * 4 + (P(),) + (rows,) * 36
    return jax.shard_map(body, mesh=mesh, in_specs=in_specs, out_specs=out_specs, check_vma=False)
```

```python
import functools
from types import SimpleNamespace

import jax
import jax.numpy as jnp
from jax import lax
from jax.experimental import pallas as pl
from jax.experimental.pallas import tpu as pltpu
from jax.sharding import PartitionSpec as P

D = 768
HEADS = 12
HEAD_DIM = 64
HW = 1024
STEP = 5


norm_eps = 1e-06
clip_limit = 2048.0
learn_rates = (0.03, 0.24, 0.03, 0.03, 0.03, 0.03, 0.03, 0.03, 0.4)
beta_first = 0.9
beta_second = 0.95
weight_decay = 0.02
adam_eps = 1e-08
ema_decay = 0.9999
masked_fill = -1e30

MESH = pl.DeviceIdType.MESH
AXES = ("dp", "side", "seq")


def places():
    dp, side, seq = (lax.axis_index(name) for name in AXES)
    count = lax.axis_size("seq")
    near = dp + 1 - 2 * lax.rem(dp, 2)
    far = dp + 2 - 4 * (dp // 2)
    along = [lax.rem(seq + step, count) for step in range(1, count)]
    before = [lax.rem(seq + count - step, count) for step in range(1, count)]
    return dp, side, seq, near, far, along, before


def greet(peers):
    barrier = pltpu.get_barrier_semaphore()
    for peer in peers:
        pl.semaphore_signal(barrier, inc=1, device_id=peer, device_id_type=MESH)
    pl.semaphore_wait(barrier, len(peers))


def remote(source, target, send_sem, recv_sem, peer):
    return pltpu.make_async_remote_copy(
        src_ref=source,
        dst_ref=target,
        send_sem=send_sem,
        recv_sem=recv_sem,
        device_id=peer,
        device_id_type=MESH,
    )


class Line:
    def __init__(self):
        self.dp, self.side, self.seq, self.near, self.far, self.along, self.before = places()
        self.count = len(self.along) + 1
        self.started = {}

    def at(self, dp, side, seq=None):
        return dp, side, self.seq if seq is None else seq

    def start(self, chunk, copy, go=None):
        if go is None:
            copy.start()
        else:
            pl.when(go)(copy.start)
        self.started.setdefault(chunk, []).append((copy, go))

    def sent(self, chunk):
        for copy, go in self.started.pop(chunk):
            if go is None:
                copy.wait_send()
            else:
                pl.when(go)(copy.wait_send)

    def goes(self, step):
        if self.count != 4 or step == 1:
            return None
        return self.seq != (3 if step == 0 else 0)

    def inner(self):
        return jnp.logical_and(self.seq > 0, self.seq < self.count - 1)

    def finish(self):
        for chunk in list(self.started):
            self.sent(chunk)


class Gather(Line):
    def __init__(self, chunks, entering, masters, fulls, own, slabs, joined, plain, sems, locs):
        super().__init__()
        self.chunks, self.masters, self.fulls = chunks, masters, fulls
        self.entering = entering
        self.own, self.slabs, self.joined = own, slabs, joined
        self.plain, self.sems, self.locs = plain, sems, locs
        self.inside = {}
        self.ready = set()
        self.crossing = [at for at in range(len(chunks)) if at not in plain]
        self.places = relative(self.dp, self.near, self.far)

    def rows(self, group, dp, side):
        size = self.count * self.masters[group].shape[0]
        return pl.multiple_of((dp * 2 + side) * size, 16), size

    def packed(self, group):
        return self.masters[group].shape[0] % 16 == 0

    def part(self, chunk, start, size):
        group, first, width = self.chunks[chunk]
        return self.fulls[group].at[pl.ds(pl.multiple_of(start, 16), size), pl.ds(first, width)]

    def send(self, chunk, which, source, target, peer, go=None, into=None):
        into = which if into is None else into
        copy = remote(source, target, self.sem(0, chunk, which), self.sem(1, chunk, into), peer)
        self.start(chunk, copy, go)

    def sem(self, kind, chunk, which):
        if chunk in self.plain:
            return self.sems[kind].at[self.plain.index(chunk) % RING, which]
        return self.sems[2 + kind].at[self.crossing.index(chunk), which]

    def arrived(self, chunk, which, target):
        peer = (self.near, self.side, self.seq)
        sems = self.sem(0, chunk, which), self.sem(1, chunk, which)
        remote(target, target, *sems, peer).wait_recv()

    def local(self, chunk, source, target):
        copy = pltpu.make_async_copy(source, target, self.locs.at[chunk])
        copy.start()
        self.inside[chunk] = copy

    def cast(self, group):
        if group in self.ready:
            return
        self.ready.add(group)
        self.entering[group].wait()
        rounded = self.masters[group][...].astype(jnp.bfloat16)
        if self.packed(group):
            self.own[group][...] = rounded
        else:
            self.slabs[group][self.seq] = rounded

    def piece(self, chunk, dp, seq):
        group, start, width = self.chunks[chunk]
        if not self.packed(group):
            return self.slabs[group].at[seq, :, pl.ds(start, width)]
        rows = self.masters[group].shape[0]
        return self.part(chunk, self.rows(group, dp, self.side)[0] + seq * rows, rows)

    def line(self, chunk, base, source, dp):
        target = self.piece(chunk, dp, self.seq)
        for step, peer in enumerate(self.along):
            self.send(
                chunk, base + step, source, target, self.at(self.dp, self.side, peer), self.goes(step)
            )

    def pass_on(self, chunk, base, spare, dp):
        self.arrived(chunk, base + 1, self.piece(chunk, dp, self.before[1]))
        if self.count == 4:
            half = self.seq // 2
            origin = 3 - 3 * half
            piece = self.piece(chunk, dp, origin)
            peer = self.at(self.dp, self.side, 3 - origin)
            self.send(chunk, spare, piece, piece, peer, self.inner(), base + 2 * half)

    def line_end(self, chunk, base, dp):
        for step, peer in enumerate(self.before):
            if step != 1:
                self.arrived(chunk, base + step, self.piece(chunk, dp, peer))

    def first(self, chunk):
        group, start, width = self.chunks[chunk]
        at = self.plain.index(chunk)
        if at >= RING:
            self.sent(self.plain[at - RING])
        self.cast(group)
        target = source = self.piece(chunk, self.dp, self.seq)
        if self.packed(group):
            source = self.own[group].at[:, pl.ds(start, width)]
            self.local(chunk, source, target)
        self.line(chunk, 0, source, self.dp)

    def relay(self, chunk):
        self.pass_on(chunk, 0, self.count + 7, self.dp)

    def second(self, chunk):
        group, start, width = self.chunks[chunk]
        columns = pl.ds(start, width)
        base, size = self.rows(group, self.dp, self.side)
        self.line_end(chunk, 0, self.dp)
        block = self.part(chunk, base, size)
        if self.packed(group):
            self.inside.pop(chunk).wait()
            source = block
        else:
            tile = 256
            joined, slab = self.joined[group], self.slabs[group]

            @pl.loop(0, width // tile)
            def _(at):
                span = pl.ds(pl.multiple_of(start + at * tile, tile), tile)
                stacked = [slab[place, :, span].astype(jnp.float32) for place in range(self.count)]
                joined[:, span] = jnp.concatenate(stacked, axis=0).astype(jnp.bfloat16)

            source = joined.at[:, columns]
            self.local(chunk, source, block)
        last = self.count - 1
        self.send(chunk, last, source, block, self.at(self.near, self.side))
        self.send(chunk, last + 1, source, block, self.at(self.far, self.side))
        self.send(chunk, last + 4, source, block, self.at(self.dp, 1 - self.side))

    def third(self, chunk):
        last = self.count - 1
        size = self.rows(self.chunks[chunk][0], self.dp, self.side)[1]
        self.exchange(chunk, last, last + 1, last + 2, last + 3, 0, size, (last + 5, last + 6))

    def exchange(self, chunk, one, two, three, four, offset, size, sides):
        group = self.chunks[chunk][0]
        half = size // 2
        other = self.at(self.dp, 1 - self.side)
        for place, which, onward, shift, peer, item in (
            (self.near, one, four, 0, self.far, 0),
            (self.far, two, three, half, self.near, 1),
        ):
            base = self.rows(group, place, self.side)[0] + offset
            block = self.part(chunk, base, size)
            self.arrived(chunk, which, block)
            piece = self.part(chunk, base + shift, half)
            self.send(chunk, onward, piece, piece, self.at(peer, self.side))
            if sides:
                self.send(chunk, sides[item], block, block, other)

    def diagonal(self, chunk, three, four, offset, size):
        base = self.rows(self.chunks[chunk][0], 3 - self.dp, self.side)[0] + offset
        half = size // 2
        self.arrived(chunk, four, self.part(chunk, base, half))
        self.arrived(chunk, three, self.part(chunk, base + half, half))

    def fourth(self, chunk):
        last = self.count - 1
        base, size = self.rows(self.chunks[chunk][0], 3 - self.dp, self.side)
        self.diagonal(chunk, last + 2, last + 3, 0, size)
        block = self.part(chunk, base, size)
        self.send(chunk, last + 7, block, block, self.at(self.dp, 1 - self.side))

    def fifth(self, chunk, first=None):
        first = self.count + 3 if first is None else first
        for which, place in enumerate(self.places):
            base, size = self.rows(self.chunks[chunk][0], place, 1 - self.side)
            self.arrived(chunk, first + which, self.part(chunk, base, size))

    def cross(self, chunk, phase):
        group, start, width = self.chunks[chunk]
        rows = self.masters[group].shape[0]
        mine = self.seq * rows
        hops = self.count - 1
        spare = 4 + 4 * hops
        if phase == 0:
            self.cast(group)
            source = self.own[group].at[:, pl.ds(start, width)]
            target = self.piece(chunk, self.dp, self.seq)
            self.local(chunk, source, target)
            self.send(chunk, 0, source, target, self.at(self.near, self.side))
            self.send(chunk, 1, source, target, self.at(self.far, self.side))
        if phase == 1:
            self.exchange(chunk, 0, 1, 2, 3, mine, rows, ())
            self.inside.pop(chunk).wait()
        if phase == 2:
            self.diagonal(chunk, 2, 3, mine, rows)
        for item, place in enumerate(self.places):
            base = 4 + item * hops
            if phase == 2 + item:
                piece = self.piece(chunk, place, self.seq)
                self.line(chunk, base, piece, place)
            if phase == 4 + item:
                self.pass_on(chunk, base, spare + item, place)
            if phase == 5 + item:
                self.line_end(chunk, base, place)
                start, size = self.rows(group, place, self.side)
                block = self.part(chunk, start, size)
                self.send(chunk, spare + 4 + item, block, block, self.at(self.dp, 1 - self.side))
        if phase == CROSS_PHASES - 1:
            self.fifth(chunk, spare + 4)


RING = 6
CROSS_PHASES = 10


def relative(dp, near, far):
    return (dp, near, far, 3 - dp)


def chunk_list(masters):
    chunks = []
    for group, shape in enumerate(masters):
        rows, width = shape
        step = width
        while rows * step > 32 * 1024 and step % 512 == 0:
            step //= 2
        if rows * step > 32 * 1024 and step % 384 == 0:
            step //= 3
        chunks += [(group, start, step) for start in range(0, width, step)]
    return chunks


def cross_chunks(masters, chunks, count):
    if count != 4 or masters[5][0] % 32 or masters[6][0] % 32:
        return []
    inner = [at for at, item in enumerate(chunks) if item[0] == 5]
    return inner[1:2] + [at for at, item in enumerate(chunks) if item[0] > 5]


def shifted(value, axis, steps):
    count = lax.axis_size(axis)
    first, last = (max(0, -steps), min(count, count - steps))
    return lax.ppermute(value, axis, [(source, source + steps) for source in range(first, last)])


def layer_norm(values):
    centre = values - jnp.mean(values, axis=-1, keepdims=True)
    spread = jnp.mean(centre * centre, axis=-1, keepdims=True)
    return centre * lax.rsqrt(spread + norm_eps)


def scaled_norm(values, norm_gain, norm_bias):
    return layer_norm(values) * norm_gain + norm_bias


def modulated(values, head_shift, head_scale):
    return layer_norm(values) * (1.0 + head_scale) + head_shift


def gelu_exact(values):
    return jax.nn.gelu(values, approximate=False)


def matmul(left_side, right_side):
    return jnp.dot(left_side, right_side, preferred_element_type=jnp.float32)


def matmul_left(left_side, right_side):
    return lax.dot_general(
        left_side, right_side, (((0,), (0,)), ((), ())), preferred_element_type=jnp.float32
    )


def matmul_right(left_side, right_side):
    return lax.dot_general(
        left_side, right_side, (((1,), (1,)), ((), ())), preferred_element_type=jnp.float32
    )


def split_heads(tensor):
    return tensor.reshape(tensor.shape[0], HEADS, HEAD_DIM).transpose(1, 0, 2)


def join_heads(tensor):
    return tensor.transpose(1, 0, 2).reshape(tensor.shape[1], HEADS * HEAD_DIM)


def head_forward(stacked, allowed):
    query_rows, key_rows, value_rows = stacked
    scores = jnp.where(
        allowed, matmul_right(query_rows, key_rows) * HEAD_DIM ** (-0.5), masked_fill
    )
    largest = jnp.max(scores, axis=1, keepdims=True)
    powered = jnp.exp(scores - largest)
    totals = jnp.sum(powered, axis=1, keepdims=True)
    weights = (powered / totals).astype(jnp.bfloat16)
    attended = matmul(weights, value_rows).astype(jnp.bfloat16)
    return (attended, (largest + jnp.log(totals))[:, 0])


def head_backward(stacked, allowed):
    query_rows, key_rows, value_rows, log_total, grad_rows = stacked
    scores = jnp.where(
        allowed, matmul_right(query_rows, key_rows) * HEAD_DIM ** (-0.5), masked_fill
    )
    weights = jnp.exp(scores - log_total[:, None])
    grad_weights = matmul_right(grad_rows, value_rows)
    row_inner = jnp.sum(weights * grad_weights, axis=1, keepdims=True)
    grad_scores = (weights * (grad_weights - row_inner)).astype(jnp.bfloat16)
    grad_query = matmul(grad_scores, key_rows) * HEAD_DIM ** (-0.5)
    grad_keys = matmul_left(grad_scores, query_rows) * HEAD_DIM ** (-0.5)
    grad_values = matmul_left(weights.astype(jnp.bfloat16), grad_rows)
    return (grad_query, grad_keys, grad_values)


def adam_step(master, gradient, moment, square, decays, rate):
    new_moment = beta_first * moment + (1.0 - beta_first) * gradient
    new_square = beta_second * square + (1.0 - beta_second) * gradient * gradient
    moment_hat = new_moment / (1.0 - beta_first**STEP)
    square_hat = new_square / (1.0 - beta_second**STEP)
    shrunk = master * (1.0 - rate * weight_decay * decays)
    return (shrunk - rate * moment_hat / (jnp.sqrt(square_hat) + adam_eps), new_moment, new_square)


def average_factors():
    total = 1.0 - ema_decay**STEP
    return (ema_decay * (1.0 - ema_decay ** (STEP - 1)) / total, (1.0 - ema_decay) / total)


def norm_rows(values):
    centre = values - jnp.mean(values, axis=-1, keepdims=True)
    spread = jnp.mean(centre * centre, axis=-1, keepdims=True)
    scale = lax.rsqrt(spread + norm_eps)
    return centre * scale, scale


def span(at, size):
    return pl.ds(pl.multiple_of(at * size, size), size)


class Moves:
    def __init__(self, sems):
        self.sems, self.used, self.open = sems, 0, []

    def start(self, source, target):
        copy = pltpu.make_async_copy(source, target, self.sems.at[self.used])
        self.used += 1
        copy.start()
        self.open.append(copy)
        return copy

    def finish(self):
        for copy in self.open:
            copy.wait()
        self.open = []


class Swaps:
    def __init__(self, sends, recvs):
        self.sends, self.recvs, self.used, self.open = sends, recvs, 0, []

    def start(self, source, target, peer):
        copy = remote(source, target, self.sends.at[self.used], self.recvs.at[self.used], peer)
        self.used += 1
        copy.start()
        self.open.append(copy)
        return copy

    def finish(self):
        for copy in self.open:
            copy.wait_send()
        self.open = []


class LineSum:
    def __init__(self, box, swaps):
        self.box, self.swaps = box, swaps
        dp, side, seq, near, far, along, _ = places()
        self.count = len(along) + 1
        self.spots = (seq, self.count + dp * 2 + side)
        self.hops = (
            [(dp, side, place) for place in along],
            [(place, side, seq) for place in (near, far, 3 - dp)]
            + [(place, 1 - side, seq) for place in (dp, near, far, 3 - dp)],
        )
        self.waiting = []
        self.level = 0

    def launch(self, value):
        spot = self.spots[self.level]
        self.box[spot] = value
        for peer in self.hops[self.level]:
            self.waiting.append(self.swaps.start(self.box.at[spot], self.box.at[spot], peer))

    def land(self):
        for copy in self.waiting:
            copy.wait_recv()
        first, size = ((0, self.count), (self.count, 8))[self.level]
        total = self.box[first]
        for place in range(first + 1, first + size):
            total = total + self.box[place]
        self.waiting = []
        self.level += 1
        return total


def all_peers():
    dp, side, seq, near, far, along, _ = places()
    peers = [(place, side, seq) for place in (near, far, 3 - dp)]
    peers += [(place, 1 - side, seq) for place in (dp, near, far, 3 - dp)]
    return peers + [(dp, side, place) for place in along]


AHEAD_SEQ = 2
AHEAD_DP = 0
TASKS = 3
CROSS_GAP = 5
NORM_STEP = 1


FORWARD_OUT = (
    ("block_low", D, jnp.bfloat16),
    ("head_out", HW, jnp.bfloat16),
    ("grad_branch", HW, jnp.bfloat16),
    ("grad_gate", HW, jnp.bfloat16),
    ("scale", HW, jnp.float32),
    ("slope_middle", HW, jnp.bfloat16),
    ("slope_cond", HW, jnp.bfloat16),
    ("slope_inner", 4 * D, jnp.bfloat16),
    ("hidden", D, jnp.float32),
    ("mixed", 3 * D, jnp.bfloat16),
    ("far_pair", 2 * D, jnp.bfloat16),
)
FORWARD_LOCAL = (
    ("normed", D, jnp.bfloat16),
    ("attended", D, jnp.bfloat16),
    ("second", D, jnp.bfloat16),
    ("activated", 4 * D, jnp.bfloat16),
    ("cond_low", HW, jnp.bfloat16),
    ("shift", HW, jnp.float32),
    ("gate", HW, jnp.float32),
    ("head_norm", HW, jnp.float32),
    ("shaped", HW, jnp.bfloat16),
    ("lifted", HW, jnp.bfloat16),
)


def head_mask(which):
    lane = lax.broadcasted_iota(jnp.int32, (1, 2 * HEAD_DIM), 1)
    inside = lane < HEAD_DIM if which == 0 else lane >= HEAD_DIM
    return jnp.where(inside, 1.0, 0.0).astype(jnp.bfloat16)


def softmax_columns(keys, queries, bias):
    scores = matmul_right(keys, queries) * HEAD_DIM ** (-0.5) + bias
    powered = jnp.exp(scores - jnp.max(scores, axis=0, keepdims=True))
    return powered / jnp.sum(powered, axis=0, keepdims=True)


def fill_bias(bias, far_row, own_row, side):
    rows = own_row.shape[-1]
    row = own_row[0:1, :]

    def column(ref):
        return jnp.broadcast_to(ref[0:1, :], (128, rows)).T[:, 0:1]

    near = column(own_row) == row
    wide = jnp.logical_and(column(far_row) == row, side == 1)
    bias[pl.ds(0, rows), :] = jnp.where(wide, 0.0, masked_fill)
    bias[pl.ds(rows, rows), :] = jnp.where(near, 0.0, masked_fill)


def pair_slices(mixed, far_pair, at):
    width = 2 * HEAD_DIM
    queries = mixed[:, span(at, width)]
    second = span(at + D // width, width)
    third = span(at + 2 * (D // width), width)
    keys = jnp.concatenate([far_pair[:, span(at, width)], mixed[:, second]], axis=0)
    values = jnp.concatenate([far_pair[:, second], mixed[:, third]], axis=0)
    return queries, keys, values


def forward_kernel(chunks, crossing, count, *refs):
    rest = list(refs)

    def take(number):
        taken = rest[:number]
        del rest[:number]
        return taken

    given = take(13)
    fulls, sides = take(8), take(8)
    outs = dict(zip([name for name, _, _ in FORWARD_OUT], take(len(FORWARD_OUT))))
    bias_out, norms_out = take(2)
    held = take(13)
    masters = held[:8]
    tokens, head_in, head_cotangent, ids, norm_rows_own = held[8:]
    weights = take(8)
    v = SimpleNamespace(**dict(zip([name for name, _, _ in FORWARD_OUT + FORWARD_LOCAL], take(21))))
    bias, own_row, far_row, box, norms = take(5)
    turned = take(3)
    own, slabs, joined = {}, {}, {}
    for group in range(8):
        if masters[group].shape[0] % 16 == 0:
            own[group] = rest.pop(0)
        else:
            slabs[group] = rest.pop(0)
            joined[group] = rest.pop(0)
    entry, *sems, locs, loads, moves_sem, swap_send, swap_recv, turn_sem, turn_send, turn_recv = rest

    dp, side, seq, near, far, along, _ = places()
    other = (dp, 1 - side, seq)
    entering = [
        pltpu.make_async_copy(source, target, entry.at[item])
        for item, (source, target) in enumerate(zip(given, held))
    ]
    for item in (0, 11, 12, 5, 8, 9, 6, 7, 1, 2, 3, 4, 10):
        entering[item].start()
    greet(all_peers())
    late = [at for at, item in enumerate(chunks) if item[0] == 5 and item[1] >= 2 * HW]
    plain = [at for at in range(len(chunks)) if at not in crossing + late] + late
    flow = Gather(chunks, entering, masters, fulls, own, slabs, joined, plain, sems, locs)
    moves = Moves(moves_sem)
    swaps = Swaps(swap_send, swap_recv)
    line = LineSum(box, swaps)
    place = (dp * 2 + side) * count + seq
    width = norm_rows_own.shape[1]
    norms[...] = jnp.zeros(norms.shape, jnp.float32)
    for item in (11, 12):
        entering[item].wait()
    norms[0:4, 0:width] = norm_rows_own[...].astype(jnp.bfloat16).astype(jnp.float32)
    spread = pltpu.roll(norms[...], place * width, 1)
    own_row[...] = jnp.broadcast_to(ids[...], own_row.shape).astype(jnp.float32)
    rows = tokens.shape[0]
    loading = {}
    turning = {0: [], 1: [], 2: []}
    landing = []

    def load(chunk):
        group, start, width = chunks[chunk]
        columns = pl.ds(start, width)
        if chunk in flow.inside:
            flow.inside.pop(chunk).wait()
        copy = pltpu.make_async_copy(
            fulls[group].at[:, columns], weights[group].at[:, columns], loads.at[chunk]
        )
        copy.start()
        loading[chunk] = copy

    def put(name):
        moves.start(getattr(v, name), outs[name])

    def share(group, source, which, done=False):
        depth = source.shape[0] if done else source.shape[1]
        buffer = turned[which]
        if not done:
            free(which)

            @pl.loop(0, depth // 256)
            def _(at):
                buffer[span(at, 256), :] = source[:, span(at, 256)].T

        size = depth // 8
        for place, block in enumerate(relative(dp, near, far)):
            mine = pl.multiple_of((block * 2 + side) * size, 16)
            theirs = pl.multiple_of((block * 2 + 1 - side) * size, 16)
            into = pl.ds(place * size, size)
            kept = pltpu.make_async_copy(
                buffer.at[pl.ds(mine, size), :],
                sides[group].at[into, pl.ds(0, rows)],
                turn_sem.at[group, place],
            )
            kept.start()
            turning[which].append(kept.wait)
            sent = remote(
                buffer.at[pl.ds(theirs, size), :],
                sides[group].at[into, pl.ds(rows, rows)],
                turn_send.at[group, place],
                turn_recv.at[group, place],
                other,
            )
            sent.start()
            turning[which].append(sent.wait_send)
            landing.append(sent)

    def free(which):
        for wait in turning[which]:
            wait()
        turning[which] = []

    def tiles(group, left, emit, start=0, width=None):
        width = weights[group].shape[1] if width is None else width

        @pl.loop(0, width // 256)
        def _(at):
            columns = span(at + start // 256, 256)
            emit(columns, matmul(left[...], weights[group][:, columns]))

    def stage_norm():
        norms[...] = line.land()
        moves.start(norms, norms_out)
        gain, offset = norms[0:1, :], norms[1:2, :]

        @pl.loop(0, rows // 64)
        def _(at):
            block = span(at, 64)
            values, _ = norm_rows(tokens[block, :].astype(jnp.float32))
            v.normed[block, :] = (values * gain + offset).astype(jnp.bfloat16)

        share(0, v.normed, 0)

    def stage_head_norm():
        @pl.loop(0, rows // 64)
        def _(at):
            block = span(at, 64)
            values, _ = norm_rows(head_in[block, :].astype(jnp.float32))
            v.head_norm[block, :] = values

    def stage_mixed(start, width):
        def emit(columns, total):
            v.mixed[:, columns] = total.astype(jnp.bfloat16)

        tiles(0, v.normed, emit, start, width)

    exchange = []

    def stage_swap():
        exchange.append(swaps.start(v.mixed.at[:, pl.ds(D, 2 * D)], v.far_pair, other))
        put("mixed")

    def stage_bias():
        for copy in exchange:
            copy.wait_recv()
        fill_bias(bias, far_row, own_row, side)
        moves.start(bias, bias_out)
        put("far_pair")
        free(1)

    def stage_heads(start, stop):
        @pl.loop(start, stop)
        def _(at):
            queries, keys, values = pair_slices(v.mixed, v.far_pair, at)
            total = None
            for which in range(2):
                mask = head_mask(which)
                weights_now = softmax_columns(keys, queries * mask, bias[...]).astype(jnp.bfloat16)
                part = matmul_left(values * mask, weights_now)
                total = part if total is None else total + part
            low = total.astype(jnp.bfloat16)
            turned[1][span(at, 2 * HEAD_DIM), :] = low
            v.attended[:, span(at, 2 * HEAD_DIM)] = low.T

    def stage_proj():
        share(1, turned[1].at[pl.ds(0, D), :], 1, True)

        def emit(columns, total):
            v.hidden[:, columns] = tokens[:, columns].astype(jnp.float32) + total

        tiles(1, v.attended, emit)
        put("hidden")
        gain, offset = norms[2:3, :], norms[3:4, :]

        @pl.loop(0, rows // 64)
        def _(at):
            block = span(at, 64)
            values, _ = norm_rows(v.hidden[block, :])
            v.second[block, :] = (values * gain + offset).astype(jnp.bfloat16)

        share(2, v.second, 0)

    def stage_up(start, width):
        def emit(columns, total):
            erf = lax.erf(total * 0.5**0.5)
            half = 0.5 * (1.0 + erf)
            v.activated[:, columns] = (total * half).astype(jnp.bfloat16)
            bell = jnp.exp(-0.5 * total * total) * (2.0 * 3.141592653589793) ** -0.5
            v.slope_inner[:, columns] = (half + total * bell).astype(jnp.bfloat16)

        tiles(2, v.second, emit, start, width)

    def stage_up_end():
        put("slope_inner")
        share(3, v.activated, 2)

    def stage_down(start, width):
        def emit(columns, total):
            v.block_low[:, columns] = (v.hidden[:, columns] + total).astype(jnp.bfloat16)

        tiles(3, v.activated, emit, start, width)

    def stage_down_end():
        put("block_low")
        share(4, v.block_low, 1)

    def stage_cond():
        def emit(columns, total):
            gates = jax.nn.sigmoid(total)
            v.cond_low[:, columns] = (total * gates).astype(jnp.bfloat16)
            slope = gates * (1.0 + total * (1.0 - gates))
            v.slope_cond[:, columns] = slope.astype(jnp.bfloat16)

        tiles(4, v.block_low, emit)
        put("slope_cond")
        share(5, v.cond_low, 0)

    def stage_mod(start, width):
        for at in range(start // 256, (start + width) // 256):
            total = matmul(v.cond_low[...], weights[5][:, at * 256 : (at + 1) * 256])
            part, block = divmod(at, HW // 256)
            columns = pl.ds(block * 256, 256)
            if part == 0:
                v.shift[:, columns] = total
            elif part == 1:
                scale = 1.0 + total
                v.scale[:, columns] = scale
                shaped = v.head_norm[:, columns] * scale + v.shift[:, columns]
                v.shaped[:, columns] = shaped.astype(jnp.bfloat16)
            else:
                v.gate[:, columns] = total
                grad = head_cotangent[:, columns].astype(jnp.float32) * total
                v.grad_branch[:, columns] = grad.astype(jnp.bfloat16)

    def stage_shaped():
        put("scale")
        share(6, v.shaped, 1)

    def stage_inner():
        def emit(columns, total):
            gates = jax.nn.sigmoid(total)
            v.lifted[:, columns] = (total * gates).astype(jnp.bfloat16)
            slope = gates * (1.0 + total * (1.0 - gates))
            v.slope_middle[:, columns] = slope.astype(jnp.bfloat16)

        tiles(6, v.shaped, emit)
        put("slope_middle")
        share(7, v.lifted, 0)

    def stage_outer():
        def emit(columns, total):
            v.shift[:, columns] = total
            grad = head_cotangent[:, columns].astype(jnp.float32) * total
            v.grad_gate[:, columns] = grad.astype(jnp.bfloat16)

        tiles(7, v.lifted, emit)
        put("grad_gate")

    def stage_gate():
        put("grad_branch")

        @pl.loop(0, HW // 256)
        def _(at):
            columns = span(at, 256)
            grown = head_in[:, columns].astype(jnp.float32) + v.gate[:, columns] * v.shift[:, columns]
            v.head_out[:, columns] = grown.astype(jnp.bfloat16)

        put("head_out")

    def chunk_tasks(chunk):
        group, start, width = chunks[chunk]
        final = start + width == weights[group].shape[1]
        if group == 0:
            tasks = [lambda: stage_mixed(start, width)]
            if final:
                tasks += [stage_swap, stage_bias]
                tasks += [functools.partial(stage_heads, at, at + 2) for at in range(0, 6, 2)]
        elif group == 1:
            tasks = [stage_proj]
        elif group == 2:
            tasks = [lambda: stage_up(start, width)]
            if final:
                tasks.append(stage_up_end)
        elif group == 3:
            tasks = [lambda: stage_down(start, width)]
            if final:
                tasks.append(stage_down_end)
        elif group == 4:
            tasks = [stage_cond]
        elif group == 5:
            tasks = [lambda: stage_mod(start, width)]
        elif group == 6:
            tasks = [stage_inner]
        else:
            tasks = [stage_outer]
        return [(chunk, task) for task in tasks]

    line.launch(spread)
    exchange.append(swaps.start(own_row, far_row, other))
    queue = [item for at in range(len(chunks)) if at not in late for item in chunk_tasks(at)]
    place = next(at for at, item in enumerate(queue) if chunks[item[0]][0] == 6)
    queue.insert(place, (queue[place - 1][0], stage_shaped))
    queue += [item for at in late for item in chunk_tasks(at)]
    queue.append((queue[-1][0], stage_gate))
    total = len(plain)
    arrived = set()
    pending = []
    for step in range(-AHEAD_SEQ, total + 4):
        if step + AHEAD_SEQ < total:
            flow.first(plain[step + AHEAD_SEQ])
        for item, chunk in enumerate(crossing):
            phase = step + AHEAD_SEQ - CROSS_GAP * item
            if 0 <= phase < CROSS_PHASES:
                flow.cross(chunk, phase)
                if phase == CROSS_PHASES - 1:
                    pending.append(chunk)
        if 0 <= step + AHEAD_DP + 1 < total:
            flow.relay(plain[step + AHEAD_DP + 1])
        if 0 <= step + AHEAD_DP < total:
            flow.second(plain[step + AHEAD_DP])
        if 0 <= step - 1 < total:
            flow.third(plain[step - 1])
        if step == -2:
            for item in (8, 9, 10):
                entering[item].wait()
            stage_head_norm()
        if step == NORM_STEP:
            line.launch(line.land())
        if step == NORM_STEP + 1:
            stage_norm()
        done = 0
        while queue and queue[0][0] in arrived and (done < TASKS or step >= total):
            chunk, task = queue.pop(0)
            if chunk in loading:
                loading.pop(chunk).wait()
            task()
            done += 1
        if 0 <= step - 2 < total:
            flow.fourth(plain[step - 2])
            flow.fifth(plain[step - 2])
            pending.append(plain[step - 2])
        for chunk in pending:
            load(chunk)
            arrived.add(chunk)
        pending = []
    flow.finish()
    moves.finish()
    swaps.finish()
    for which in range(3):
        free(which)
    for copy in landing:
        copy.wait_recv()


def forward_all(masters, tokens, head_in, head_cotangent, image_ids, norm_params):
    devices = lax.axis_size("dp") * lax.axis_size("side") * lax.axis_size("seq")
    count = lax.axis_size("seq")
    chunks = chunk_list([master.shape for master in masters])
    total = len(chunks)
    crossing = cross_chunks([master.shape for master in masters], chunks, count)
    rows = tokens.shape[0]
    low, full = jnp.bfloat16, jnp.float32
    fulls = [jax.ShapeDtypeStruct((devices * m.shape[0], m.shape[1]), low) for m in masters]
    sides = [jax.ShapeDtypeStruct((devices * m.shape[0] // 2, 2 * rows), low) for m in masters]
    outs = [jax.ShapeDtypeStruct((rows, width), kind) for _, width, kind in FORWARD_OUT]
    extra = [jax.ShapeDtypeStruct((2 * rows, rows), full), jax.ShapeDtypeStruct((8, D), full)]
    given = [*masters, tokens, head_in, head_cotangent, image_ids[None, :], norm_params.T]
    scratch = [pltpu.VMEM(item.shape, item.dtype) for item in given]
    scratch += [pltpu.VMEM(item.shape, low) for item in fulls]
    scratch += [pltpu.VMEM((rows, width), kind) for _, width, kind in FORWARD_OUT + FORWARD_LOCAL]
    scratch += [
        pltpu.VMEM((2 * rows, rows), full),
        pltpu.VMEM((8, rows), full),
        pltpu.VMEM((8, rows), full),
        pltpu.VMEM((count + 8, 8, D), full),
        pltpu.VMEM((8, D), full),
        pltpu.VMEM((HW, rows), low),
        pltpu.VMEM((HW, rows), low),
        pltpu.VMEM((4 * D, rows), low),
    ]
    for master in masters:
        depth, width = master.shape
        if depth % 16 == 0:
            scratch.append(pltpu.VMEM((depth, width), low))
        else:
            scratch.append(pltpu.VMEM((count, depth, width), low))
            scratch.append(pltpu.VMEM((count * depth, width), low))
    dma = pltpu.SemaphoreType.DMA
    scratch += [
        dma((13,)),
        dma((RING, count + 8)),
        dma((RING, count + 8)),
        dma((max(1, len(crossing)), 4 * count + 8)),
        dma((max(1, len(crossing)), 4 * count + 8)),
        dma((total,)),
        dma((total,)),
        dma((16,)),
        dma((8 + count,)),
        dma((8 + count,)),
        dma((8, 4)),
        dma((8, 4)),
        dma((8, 4)),
    ]
    hbm = pl.BlockSpec(memory_space=pltpu.HBM)
    results = pl.pallas_call(
        lambda *refs: forward_kernel(chunks, crossing, count, *refs),
        out_shape=fulls + sides + outs + extra,
        in_specs=[hbm] * 13,
        out_specs=[hbm] * (16 + len(outs) + 2),
        scratch_shapes=scratch,
        compiler_params=pltpu.CompilerParams(
            collective_id=0, has_side_effects=True, vmem_limit_bytes=63 * 2**20
        ),
        name="forward",
    )(*given)
    named = dict(zip([name for name, _, _ in FORWARD_OUT], results[16:]))
    named["bias"], named["norms"] = results[-2:]
    return results[:8], results[8:16], named


class Scatter(Line):
    def __init__(
        self, chunks, crossing, parts, inbox, after, slabs, pieces, finals, squares, boxes, sems
    ):
        super().__init__()
        self.chunks, self.parts, self.inbox, self.after = chunks, parts, inbox, after
        self.slabs, self.pieces, self.finals, self.squares = slabs, pieces, finals, squares
        self.sems, self.boxes, self.crossing = sems, boxes, crossing
        self.plain = [at for at in range(len(chunks)) if at not in crossing]
        self.near, self.far = self.at(self.near, self.side), self.at(self.far, self.side)
        self.coming = {}

    def send(self, chunk, which, source, target, peer, go=None):
        if chunk in self.crossing:
            kind, slot = 2, self.crossing.index(chunk)
        else:
            kind, slot = 0, self.plain.index(chunk) % RING
        sems = self.sems[kind].at[slot, which], self.sems[kind + 1].at[slot, which]
        copy = remote(source, target, *sems, peer)
        self.start(chunk, copy, go)
        self.coming[chunk, which] = copy

    def land(self, chunk, *which):
        for item in which:
            self.coming.pop((chunk, item)).wait_recv()

    def shape(self, chunk):
        group, start, width = self.chunks[chunk]
        size = self.parts[group].shape[1]
        return group, start, width, size, size // 2

    def first(self, chunk):
        group, start, width, size, half = self.shape(chunk)
        columns, part, inbox = pl.ds(start, width), self.parts[group], self.inbox[group]
        upper, lower = pl.ds(0, half), pl.ds(half, half)
        at = self.plain.index(chunk)
        if at >= RING:
            self.sent(self.plain[at - RING])
        for item, block in enumerate((1, 3)):
            self.send(chunk, item, part.at[block, upper, columns], inbox.at[item, :, columns], self.near)
        for item, block in enumerate((2, 3)):
            self.send(
                chunk, 2 + item, part.at[block, lower, columns], inbox.at[2 + item, :, columns], self.far
            )

    def tiles(self, chunk, work):
        _, start, width, _, _ = self.shape(chunk)

        @pl.loop(0, width // 256)
        def _(at):
            work(pl.ds(pl.multiple_of(start + at * 256, 256), 256))

    def second(self, chunk):
        group, start, width, size, half = self.shape(chunk)
        columns, part, inbox = pl.ds(start, width), self.parts[group], self.inbox[group]
        upper, lower = pl.ds(0, half), pl.ds(half, half)
        self.land(chunk, 0, 1, 2, 3)

        def work(span_now):
            for block, rows, item in ((2, upper, 1), (1, lower, 3)):
                total = part[block, rows, span_now].astype(jnp.float32)
                total = total + inbox[item, :, span_now].astype(jnp.float32)
                part[block, rows, span_now] = total.astype(jnp.bfloat16)

        self.tiles(chunk, work)
        after = self.after[group]
        self.send(chunk, 4, part.at[1, lower, columns], after.at[0, :, columns], self.near)
        self.send(chunk, 5, part.at[2, upper, columns], after.at[1, :, columns], self.far)

    def third(self, chunk):
        group, start, width, size, half = self.shape(chunk)
        columns, part, inbox = pl.ds(start, width), self.parts[group], self.inbox[group]
        upper, lower = pl.ds(0, half), pl.ds(half, half)
        after = self.after[group]
        self.land(chunk, 4, 5)
        slab = self.slabs[group]
        depth = size // self.count

        def work(span_now):
            for rows, item, last, base in ((upper, 0, 1, 0), (lower, 2, 0, self.count // 2)):
                total = part[0, rows, span_now].astype(jnp.float32)
                total = total + inbox[item, :, span_now].astype(jnp.float32)
                total = total + after[last, :, span_now].astype(jnp.float32)
                for place in range(self.count // 2):
                    piece = total[place * depth : (place + 1) * depth].astype(jnp.bfloat16)
                    slab[base + place, :, span_now] = piece

        self.tiles(chunk, work)
        for step, peer in enumerate(self.along):
            self.send(
                chunk,
                6 + step,
                slab.at[peer, :, columns],
                self.pieces[group].at[step, :, columns],
                (self.dp, self.side, peer),
            )

    def fourth(self, chunk):
        group, start, width, size, half = self.shape(chunk)
        self.land(chunk, *(6 + step for step in range(self.count - 1)))
        slab, pieces, final = self.slabs[group], self.pieces[group], self.finals[group]

        def work(span_now):
            total = slab[self.seq, :, span_now].astype(jnp.float32)
            for step in range(self.count - 1):
                total = total + pieces[step, :, span_now].astype(jnp.float32)
            final[:, span_now] = total
            self.squares[0:1, :] += jnp.sum(total * total, axis=0, keepdims=True)

        self.tiles(chunk, work)

    def cross(self, chunk, phase):
        group, start, width, size, _ = self.shape(chunk)
        columns, part = pl.ds(start, width), self.parts[group]
        depth = size // self.count
        half = depth // 2
        box, got, sums, inbox, after = self.boxes[self.crossing.index(chunk)]
        final = self.finals[group]

        def rows(seq):
            return pl.ds(pl.multiple_of(seq * depth, 16), depth)

        def tiles(work):
            @pl.loop(0, width // 256)
            def _(at):
                at = pl.multiple_of(at * 256, 256)
                work(pl.ds(at, 256), pl.ds(pl.multiple_of(start + at, 256), 256))

        def pair_peer(step):
            return self.at(self.dp, self.side, self.along[step])

        if phase < 4:
            for step in (0, 2):
                self.send(
                    chunk,
                    4 * phase + step,
                    part.at[phase, rows(self.along[step]), columns],
                    got.at[phase, step],
                    pair_peer(step),
                    self.goes(step),
                )
            beside = self.seq + 1 - 2 * lax.rem(self.seq, 2)
            self.send(
                chunk,
                4 * phase + 3,
                part.at[phase, rows(3 - self.seq), columns],
                box.at[phase],
                self.at(self.dp, self.side, beside),
                jnp.logical_not(self.inner()),
            )
        if 2 <= phase < 6:
            block = phase - 2

            @pl.when(self.inner())
            def _():
                self.coming[chunk, 4 * block + 3].wait_recv()

                def work(here, there):
                    total = part[block, rows(self.along[1]), there].astype(jnp.float32)
                    total = total + box[block, :, here].astype(jnp.float32)
                    part[block, rows(self.along[1]), there] = total.astype(jnp.bfloat16)

                tiles(work)

            self.send(
                chunk,
                4 * block + 1,
                part.at[block, rows(self.along[1]), columns],
                got.at[block, 1],
                pair_peer(1),
            )
        if 4 <= phase < 8:
            block = phase - 4
            self.land(chunk, 4 * block + 1)
            pl.when(self.seq != 0)(self.coming[chunk, 4 * block].wait_recv)
            pl.when(self.seq != 3)(self.coming[chunk, 4 * block + 2].wait_recv)

            def work(here, there):
                total = part[block, rows(self.seq), there].astype(jnp.float32)
                for step in range(3):
                    total = total + got[block, step, :, here].astype(jnp.float32)
                sums[block, :, here] = total.astype(jnp.bfloat16)

            tiles(work)
        upper, lower = pl.ds(0, half), pl.ds(half, half)
        if phase == 7:
            for item, block in enumerate((1, 3)):
                self.send(chunk, 16 + item, sums.at[block, upper, :], inbox.at[item], self.near)
            for item, block in enumerate((2, 3)):
                self.send(chunk, 18 + item, sums.at[block, lower, :], inbox.at[2 + item], self.far)
        if phase == 8:
            self.land(chunk, 16, 17, 18, 19)

            def work(here, there):
                for block, part_rows, item in ((2, upper, 1), (1, lower, 3)):
                    total = sums[block, part_rows, here].astype(jnp.float32)
                    total = total + inbox[item, :, here].astype(jnp.float32)
                    sums[block, part_rows, here] = total.astype(jnp.bfloat16)

            tiles(work)
            self.send(chunk, 20, sums.at[1, lower, :], after.at[0], self.near)
            self.send(chunk, 21, sums.at[2, upper, :], after.at[1], self.far)
        if phase == 9:
            self.land(chunk, 20, 21)

            def work(here, there):
                for part_rows, item, last in ((upper, 0, 1), (lower, 2, 0)):
                    total = sums[0, part_rows, here].astype(jnp.float32)
                    total = total + inbox[item, :, here].astype(jnp.float32)
                    total = total + after[last, :, here].astype(jnp.float32)
                    final[part_rows, there] = total
                    self.squares[0:1, :] += jnp.sum(total * total, axis=0, keepdims=True)

            tiles(work)


CROSS_STEPS = (1,)
CROSS_LAST = 10
LAG = 1
MID = 1
LATE = 3
NCROSS = 1
EXTRA = (0,)


BACKWARD_IN = (
    "grad_branch",
    "slope_middle",
    "head_in",
    "head_cotangent",
    "scale",
    "grad_gate",
    "slope_cond",
    "out_cotangent",
    "slope_inner",
    "hidden",
    "norms",
    "mixed",
    "far_pair",
    "bias",
    "tokens",
)


def norm_back(grads, values, scale):
    first = jnp.mean(grads, axis=-1, keepdims=True)
    second = jnp.mean(grads * values, axis=-1, keepdims=True)
    return scale * (grads - first - values * second)


def backward_kernel(chunks, crossing, count, *refs):
    rest = list(refs)

    def take(number):
        taken = rest[:number]
        del rest[:number]
        return taken

    weights, sides = take(8), take(8)
    given = dict(zip(BACKWARD_IN, take(len(BACKWARD_IN))))
    outs = take(12)
    finals = take(8)
    head_in_grad, tokens_grad, norm_grads, norm_out = take(4)
    grads, parts, inbox, after, slabs, pieces = (take(8) for _ in range(6))
    small, large, tile_box = take(3)
    into = {
        "grad_branch": grads[7].at[pl.ds(0, grads[7].shape[0] // 2), :],
        "slope_middle": grads[6].at[pl.ds(0, grads[6].shape[0] // 2), :],
        "grad_gate": grads[5].at[pl.ds(0, grads[5].shape[0] // 2), pl.ds(2 * HW, HW)],
        "slope_cond": grads[4].at[pl.ds(0, grads[4].shape[0] // 2), :],
        "slope_inner": grads[2].at[pl.ds(0, grads[2].shape[0] // 2), :],
    }
    held = [name for name in BACKWARD_IN if name not in into]
    local = SimpleNamespace(**dict(zip(held, take(10))))
    spare, attended_grad, back_pair, squares, box, square_box = take(6)
    boxes = [take(5) for _ in crossing]
    *sems, load_sem, side_sem, tile_sem, swap_send, swap_recv, out_sem = rest

    dp, side, seq, near, far, along, _ = places()
    other = (dp, 1 - side, seq)
    for _, got, _, _, _ in boxes:
        @pl.when(seq == 0)
        def _():
            got[:, 0] = jnp.zeros(got.shape[:1] + got.shape[2:], got.dtype)

        @pl.when(seq == count - 1)
        def _():
            got[:, 2] = jnp.zeros(got.shape[:1] + got.shape[2:], got.dtype)

    greet(all_peers())
    rows = local.tokens.shape[0]
    own, pair = pl.ds(0, rows), pl.ds(rows, rows)
    swaps = Swaps(swap_send, swap_recv)
    moves = Moves(out_sem)
    flow = Scatter(
        chunks, crossing, parts, inbox, after, slabs, pieces, finals, squares, boxes, sems
    )
    loading = {}
    for item, name in enumerate(BACKWARD_IN):
        target = into[name] if name in into else getattr(local, name)
        loading[name] = pltpu.make_async_copy(given[name], target, load_sem.at[item])
    order = [group for group in range(7, -1, -1)]
    slim = [group for group in order if sides[group].shape[0] <= small.shape[1]]
    side_slot = {}
    side_copy = {}

    def side_load(group):
        depth = sides[group].shape[0]
        if group in slim:
            target = small.at[slim.index(group) % 2, pl.ds(0, depth), :]
        else:
            target = large
        side_slot[group] = target
        side_copy[group] = pltpu.make_async_copy(sides[group], target, side_sem.at[group])
        side_copy[group].start()

    def ready(*names):
        for name in names:
            loading.pop(name).wait()

    tile_list = [
        (group, at) for group in order for at in range(weights[group].shape[0] // 256)
    ]
    tile_copy = {}
    depth_box = tile_box.shape[0]

    def tile_load(item):
        if item >= len(tile_list):
            return
        group, at = tile_list[item]
        copy = pltpu.make_async_copy(
            weights[group].at[pl.ds(at * 256, 256), :],
            tile_box.at[item % depth_box, :, pl.ds(0, weights[group].shape[1])],
            tile_sem.at[item % depth_box],
        )
        tile_copy[item] = copy
        copy.start()

    loading["grad_branch"].start()
    for item in range(depth_box):
        tile_load(item)
    loading["slope_middle"].start()
    side_load(slim[0])
    side_load(slim[1])
    for name in BACKWARD_IN[2:]:
        loading[name].start()
    for group in order:
        if group not in slim:
            side_load(group)
    squares[...] = jnp.zeros_like(squares)
    norm_grads[...] = jnp.zeros_like(norm_grads)
    at_tile = [0]

    def back(group, emit):
        width = weights[group].shape[1]
        for at in range(weights[group].shape[0] // 256):
            item = at_tile[0]
            at_tile[0] += 1
            tile_copy.pop(item).wait()
            total = matmul_right(
                grads[group][own, :], tile_box[item % depth_box, :, pl.ds(0, width)]
            )
            emit(pl.ds(at * 256, 256), total)
            tile_load(item + depth_box)

    coming = {}

    def share(group):
        coming[group] = swaps.start(grads[group].at[own, :], grads[group].at[pair, :], other)

    def product(chunk):
        group, start, width = chunks[chunk]
        if group in coming:
            coming.pop(group).wait_recv()
            side_copy.pop(group).wait()
        left, part = side_slot[group], parts[group]
        size = part.shape[1]
        whole = group in slim

        @pl.loop(0, width // 256)
        def _(at):
            columns = pl.ds(pl.multiple_of(start + at * 256, 256), 256)
            right = grads[group][:, columns]
            if whole:
                total = matmul(left[...], right).astype(jnp.bfloat16)
                for block in range(4):
                    part[block, :, columns] = total[block * size : (block + 1) * size]
            else:
                for block in range(4):
                    total = matmul(left[pl.ds(block * size, size), :], right)
                    part[block, :, columns] = total.astype(jnp.bfloat16)

        if start + width == weights[group].shape[1]:
            if group in slim and slim.index(group) + 2 < len(slim):
                side_load(slim[slim.index(group) + 2])

    plain = flow.plain

    def done(chunk):
        group, start, width = chunks[chunk]
        columns = pl.ds(start, width)
        moves.start(finals[group].at[:, columns], outs[group].at[:, columns])

    def step(at):
        total = len(plain)
        if at < total:
            product(plain[at])
            flow.first(plain[at])
            earlier = plain[at - 1] if at else -1
            for chunk in range(earlier + 1, plain[at]):
                product(chunk)
        for chunk, begin in zip(crossing, CROSS_STEPS):
            if 0 <= at - begin < CROSS_LAST:
                flow.cross(chunk, at - begin)
                if at - begin == CROSS_LAST - 1:
                    done(chunk)
        if 0 <= at - LAG < total:
            flow.second(plain[at - LAG])
        if 0 <= at - LAG - MID < total:
            flow.third(plain[at - LAG - MID])
        if 0 <= at - LAG - LATE < total:
            flow.fourth(plain[at - LAG - LATE])
            done(plain[at - LAG - LATE])

    def stage_outer():
        ready("slope_middle")

        def emit(columns, total):
            slope = grads[6][own, columns].astype(jnp.float32)
            grads[6][own, columns] = (total * slope).astype(jnp.bfloat16)

        back(7, emit)
        share(6)

    def stage_inner():
        def emit(columns, total):
            spare[:, columns] = total

        back(6, emit)
        ready("head_in", "head_cotangent", "scale", "grad_gate")

        @pl.loop(0, rows // 32)
        def _(at):
            block = span(at, 32)
            values, scale = norm_rows(local.head_in[block, :].astype(jnp.float32))
            grad = spare[block, pl.ds(0, HW)]
            grads[5][block, pl.ds(0, HW)] = grad.astype(jnp.bfloat16)
            grads[5][block, pl.ds(HW, HW)] = (grad * values).astype(jnp.bfloat16)
            passed = norm_back(grad * local.scale[block, :], values, scale)
            head_in_grad[block, :] = local.head_cotangent[block, :].astype(jnp.float32) + passed

        share(5)
        moves.start(head_in_grad, outs[8])

    def stage_mod():
        ready("slope_cond")

        def emit(columns, total):
            slope = grads[4][own, columns].astype(jnp.float32)
            grads[4][own, columns] = (total * slope).astype(jnp.bfloat16)

        back(5, emit)
        share(4)

    def stage_cond():
        ready("out_cotangent")

        def emit(columns, total):
            grad = local.out_cotangent[:, columns].astype(jnp.float32) + total
            tokens_grad[:, columns] = grad
            grads[3][own, columns] = grad.astype(jnp.bfloat16)

        back(4, emit)
        share(3)

    def stage_down():
        ready("slope_inner")

        def emit(columns, total):
            slope = grads[2][own, columns].astype(jnp.float32)
            grads[2][own, columns] = (total * slope).astype(jnp.bfloat16)

        back(3, emit)
        share(2)

    def norm_stage(source, base, emit):
        gain = local.norms[base : base + 1, :]

        @pl.loop(0, rows // 32)
        def _(at):
            block = span(at, 32)
            values, scale = norm_rows(source[block, :].astype(jnp.float32))
            grad = spare[block, pl.ds(0, D)]
            norm_grads[base : base + 1, :] += jnp.sum(grad * values, axis=0, keepdims=True)
            norm_grads[base + 1 : base + 2, :] += jnp.sum(grad, axis=0, keepdims=True)
            emit(block, norm_back(grad * gain, values, scale))

    def stage_up():
        def keep(columns, total):
            spare[:, columns] = total

        back(2, keep)
        ready("hidden", "norms")

        def emit(block, passed):
            grad = tokens_grad[block, :] + passed
            tokens_grad[block, :] = grad
            grads[1][block, :] = grad.astype(jnp.bfloat16)

        norm_stage(local.hidden, 2, emit)
        share(1)

    def stage_proj():
        def emit(columns, total):
            attended_grad[:, columns] = total.astype(jnp.bfloat16)

        back(1, emit)
        ready("mixed", "far_pair", "bias")

    def stage_heads(start, stop):
        width = 2 * HEAD_DIM
        scaling = HEAD_DIM ** (-0.5)

        @pl.loop(start, stop)
        def _(at):
            queries, keys, values = pair_slices(local.mixed, local.far_pair, at)
            outer = attended_grad[:, span(at, width)]
            query_part = key_part = value_part = None
            for which in range(2):
                mask = head_mask(which)
                query_now, outer_now = queries * mask, outer * mask
                chances = softmax_columns(keys, query_now, local.bias[...])
                slopes = matmul_right(values, outer_now)
                inner = jnp.sum(chances * slopes, axis=0, keepdims=True)
                score_grad = (chances * (slopes - inner)).astype(jnp.bfloat16)
                value_now = matmul(chances.astype(jnp.bfloat16), outer_now)
                key_now = matmul(score_grad, query_now)
                query_side = matmul_left(keys * mask, score_grad)
                if which == 0:
                    query_part, key_part, value_part = query_side, key_now, value_now
                else:
                    query_part = query_part + query_side
                    key_part = key_part + key_now
                    value_part = value_part + value_now
            grads[0][own, span(at, width)] = (query_part * scaling).astype(jnp.bfloat16).T
            key_part = key_part * scaling
            first, second = span(at, width), span(at + D // width, width)
            local.far_pair[:, first] = key_part[:rows].astype(jnp.bfloat16)
            local.far_pair[:, second] = value_part[:rows].astype(jnp.bfloat16)
            spare[:, first] = key_part[rows:]
            spare[:, second] = value_part[rows:]

    def stage_return():
        coming["back"] = swaps.start(local.far_pair, back_pair, other)

    def stage_merge():
        coming.pop("back").wait_recv()

        @pl.loop(0, 2 * D // 256)
        def _(at):
            columns = span(at, 256)
            total = spare[:, columns] + back_pair[:, columns].astype(jnp.float32)
            grads[0][own, span(at + D // 256, 256)] = total.astype(jnp.bfloat16)

        share(0)

    def stage_attend():
        def keep(columns, total):
            spare[:, columns] = total

        back(0, keep)
        ready("tokens")

        def emit(block, passed):
            tokens_grad[block, :] = tokens_grad[block, :] + passed

        norm_stage(local.tokens, 0, emit)
        moves.start(tokens_grad, outs[9])

    ready("grad_branch")
    share(7)
    stages = [
        stage_outer,
        stage_inner,
        stage_mod,
        stage_cond,
        stage_down,
        stage_up,
        stage_proj,
        lambda: stage_heads(0, 2),
        lambda: stage_heads(2, 4),
        lambda: stage_heads(4, 6),
        stage_return,
        stage_merge,
        stage_attend,
    ]
    line = LineSum(box, swaps)
    total = len(plain)
    for chunk in range(max(total + LAG + LATE, CROSS_STEPS[-1] + CROSS_LAST)):
        group = chunks[plain[min(chunk, total - 1)]][0]
        needed = {7: 0, 6: 1, 5: 2, 4: 3, 3: 4, 2: 5, 1: 6, 0: 12}[group]
        while stages and 13 - len(stages) < needed:
            stages.pop(0)()
        step(chunk)
        if stages:
            stages.pop(0)()
            if chunk in EXTRA:
                stages.pop(0)()
            if not stages:
                line.launch(norm_grads[...])
        elif line.level == 0:
            line.launch(line.land())
        elif line.level == 1:
            sums = line.land()
            norm_grads[...] = sums
            moves.start(norm_grads, outs[10])
    last = LineSum(square_box, swaps)
    last.launch(squares[...])
    last.launch(last.land())
    sums = norm_grads[...]
    flat = jnp.sum(last.land(), axis=0, keepdims=True)
    whole = jnp.sum(flat, axis=1, keepdims=True)
    extra = jnp.sum(jnp.sum(sums * sums, axis=0, keepdims=True), axis=1, keepdims=True)
    norm_out[...] = jnp.broadcast_to(jnp.sqrt(whole + extra), norm_out.shape)
    moves.start(norm_out, outs[11])
    flow.finish()
    swaps.finish()
    moves.finish()


def backward_chunks(masters):
    chunks = chunk_list(masters)
    chunks = [item for group in range(7, -1, -1) for item in chunks if item[0] == group]
    group, start, width = chunks.pop()
    for size in (width - width // 2 // 256 * 256, width // 2 // 256 * 256):
        chunks.append((group, start, size)) if size else None
        start += size
    return chunks


def backward_all(masters, weights, sides, named):
    count = lax.axis_size("seq")
    shapes = [master.shape for master in masters]
    chunks = backward_chunks(shapes)
    inner = [at for at, item in enumerate(chunks) if item[0] == 5]
    crossing = [at for at, item in enumerate(chunks) if item[0] == 6][:1] + inner[1::2]
    crossing = crossing[:NCROSS]
    rows = named["tokens"].shape[0]
    low, full = jnp.bfloat16, jnp.float32
    hbm = pl.BlockSpec(memory_space=pltpu.HBM)
    given = [named[name] for name in BACKWARD_IN]
    outs = [jax.ShapeDtypeStruct(shape, full) for shape in shapes]
    outs += [
        jax.ShapeDtypeStruct((rows, HW), full),
        jax.ShapeDtypeStruct((rows, D), full),
        jax.ShapeDtypeStruct((8, D), full),
        jax.ShapeDtypeStruct((8, 128), full),
    ]
    scratch = [pltpu.VMEM(item.shape, full) for item in outs]
    scratch += [pltpu.VMEM((2 * rows, width), low) for _, width in shapes]
    scratch += [pltpu.VMEM((4, count * depth, width), low) for depth, width in shapes]
    used = {item[0] for at, item in enumerate(chunks) if at not in crossing}
    boxed = [shape if at in used else (16, 128) for at, shape in enumerate(shapes)]
    scratch += [pltpu.VMEM((4, count * depth // 2, width), low) for depth, width in boxed]
    scratch += [pltpu.VMEM((2, count * depth // 2, width), low) for depth, width in boxed]
    scratch += [pltpu.VMEM((count, depth, width), low) for depth, width in boxed]
    scratch += [pltpu.VMEM((count - 1, depth, width), low) for depth, width in boxed]
    scratch += [
        pltpu.VMEM((2, HW // 2, 2 * rows), low),
        pltpu.VMEM((2 * D, 2 * rows), low),
        pltpu.VMEM((3, 256, 3 * HW), low),
        pltpu.VMEM((rows, HW), low),
        pltpu.VMEM((rows, HW), low),
        pltpu.VMEM((rows, HW), full),
        pltpu.VMEM((rows, D), low),
        pltpu.VMEM((rows, D), full),
        pltpu.VMEM((8, D), full),
        pltpu.VMEM((rows, 3 * D), low),
        pltpu.VMEM((rows, 2 * D), low),
        pltpu.VMEM((2 * rows, rows), full),
        pltpu.VMEM((rows, D), low),
        pltpu.VMEM((rows, 2 * D), full),
        pltpu.VMEM((rows, D), low),
        pltpu.VMEM((rows, 2 * D), low),
        pltpu.VMEM((8, 256), full),
        pltpu.VMEM((count + 8, 8, D), full),
        pltpu.VMEM((count + 8, 8, 256), full),
    ]
    for chunk in crossing:
        group, _, width = chunks[chunk]
        depth = shapes[group][0]
        scratch += [
            pltpu.VMEM((4, depth, width), low),
            pltpu.VMEM((4, count - 1, depth, width), low),
            pltpu.VMEM((4, depth, width), low),
            pltpu.VMEM((4, depth // 2, width), low),
            pltpu.VMEM((2, depth // 2, width), low),
        ]
    dma = pltpu.SemaphoreType.DMA
    scratch += [
        dma((RING, 5 + count)),
        dma((RING, 5 + count)),
        dma((max(1, len(crossing)), 22)),
        dma((max(1, len(crossing)), 22)),
        dma((len(BACKWARD_IN),)),
        dma((8,)),
        dma((3,)),
        dma((21 + 2 * count,)),
        dma((21 + 2 * count,)),
        dma((len(chunks) + 4,)),
    ]
    return pl.pallas_call(
        lambda *refs: backward_kernel(chunks, crossing, count, *refs),
        out_shape=outs,
        in_specs=[hbm] * (16 + len(given)),
        out_specs=[hbm] * len(outs),
        scratch_shapes=scratch,
        compiler_params=pltpu.CompilerParams(
            collective_id=1, has_side_effects=True, vmem_limit_bytes=64 * 2**20
        ),
        name="backward",
    )(*weights, *sides, *given)


def optimizer_kernel(*refs):
    rest = list(refs)

    def take(number):
        taken = rest[:number]
        del rest[:number]
        return taken

    given = [take(5) for _ in range(8)]
    passed = take(4)
    small_given = take(6)
    results = [take(4) for _ in range(8)]
    kept = take(4)
    small_outs = take(4)
    small_held, small_results = take(6), take(4)
    small, grad_norm = small_held[:5], small_held[5]
    held = [take(5) for _ in range(8)]
    made = [take(4) for _ in range(8)]
    carried = take(4)
    load_sem, save_sem, pass_sem, small_sem = rest
    loads, saves, first = [], [], []
    for item in range(6):
        copy = pltpu.make_async_copy(small_given[item], small_held[item], small_sem.at[item])
        copy.start()
        first.append(copy)
    for group in range(8):
        for item in range(5):
            copy = pltpu.make_async_copy(
                given[group][item], held[group][item], load_sem.at[group, item]
            )
            copy.start()
            loads.append(copy)
    for item in range(4):
        pltpu.make_async_copy(passed[item], carried[item], pass_sem.at[0, item]).start()
    for copy in first:
        copy.wait()
    factor = jnp.minimum(1.0, clip_limit / (grad_norm[0:1, 0:1] + 1e-06))
    keep_old, take_new = average_factors()

    def update(source, target, columns, decays, rate):
        gradient, master, moment, square, average = (ref[:, columns] for ref in source)
        put(gradient, master, moment, square, average, target, columns, decays, rate)

    def put(gradient, master, moment, square, average, target, columns, decays, rate):
        fresh = adam_step(master, gradient * factor, moment, square, decays, rate)
        for item in range(3):
            target[item][:, columns] = fresh[item]
        target[3][:, columns] = keep_old * average + take_new * fresh[0]

    width = small[1].shape[1]
    total = small[0].shape[1]
    place = (lax.axis_index("dp") * 2 + lax.axis_index("side")) * lax.axis_size(
        "seq"
    ) + lax.axis_index("seq")
    turned = pltpu.roll(small[0][...], lax.rem(total - place * width, total), 1)
    own = [turned[0:4, 0:width]] + [ref[...] for ref in small[1:]]
    put(*own, small_results, slice(None), 0.0, learn_rates[8])
    for item in range(4):
        copy = pltpu.make_async_copy(
            small_results[item], small_outs[item], small_sem.at[6 + item]
        )
        copy.start()
        saves.append(copy)
    for group in range(8):
        for item in range(5):
            loads[group * 5 + item].wait()

        @pl.loop(0, held[group][0].shape[1] // 256)
        def _(at):
            columns = pl.ds(pl.multiple_of(at * 256, 256), 256)
            update(held[group], made[group], columns, 1.0, learn_rates[group])

        for item in range(4):
            copy = pltpu.make_async_copy(
                made[group][item], results[group][item], save_sem.at[group, item]
            )
            copy.start()
            saves.append(copy)
        if group % 2:
            item = group // 2
            pltpu.make_async_copy(passed[item], carried[item], pass_sem.at[0, item]).wait()
            copy = pltpu.make_async_copy(carried[item], kept[item], pass_sem.at[1, item])
            copy.start()
            saves.append(copy)
    for copy in saves:
        copy.wait()


def optimizer_all(gradients, passed, norm_grads, grad_norm, masters, moments, squares, averages):
    full = jnp.float32
    hbm = pl.BlockSpec(memory_space=pltpu.HBM)
    given = []
    for group in range(8):
        given += [
            gradients[group],
            masters[group],
            moments[group],
            squares[group],
            averages[group],
        ]
    small = [masters[8].T, moments[8].T, squares[8].T, averages[8].T]
    given += [*passed, norm_grads, *small, grad_norm]
    shapes = [master.shape for master in masters[:8]]
    outs = [jax.ShapeDtypeStruct(shape, full) for shape in shapes for _ in range(4)]
    outs += [jax.ShapeDtypeStruct(item.shape, item.dtype) for item in passed]
    outs += [jax.ShapeDtypeStruct(small[0].shape, full) for _ in range(4)]
    scratch = [pltpu.VMEM(item.shape, full) for item in given[44:] + outs[36:]]
    scratch += [pltpu.VMEM(shape, full) for shape in shapes for _ in range(5)]
    scratch += [pltpu.VMEM(shape, full) for shape in shapes for _ in range(4)]
    scratch += [pltpu.VMEM(item.shape, item.dtype) for item in passed]
    dma = pltpu.SemaphoreType.DMA
    scratch += [dma((8, 5)), dma((8, 4)), dma((2, 4)), dma((10,))]
    results = pl.pallas_call(
        optimizer_kernel,
        out_shape=outs,
        in_specs=[hbm] * len(given),
        out_specs=[hbm] * len(outs),
        scratch_shapes=scratch,
        compiler_params=pltpu.CompilerParams(vmem_limit_bytes=63 * 2**20),
        name="optimizer",
    )(*given)
    fresh = [results[4 * group : 4 * group + 4] for group in range(8)]
    return results[32:36], fresh + [[item.T for item in results[36:]]]


def body(*arrays):
    tokens, head_in, image_ids, out_cotangent, head_cotangent = arrays[:5]
    masters, moments, squares, averages = (arrays[at : at + 9] for at in (5, 14, 23, 32))
    sides = lax.axis_size("dp") == 4 and lax.axis_size("side") == 2
    if not sides or masters[0].shape[0] % 8 or lax.axis_size("seq") != 4:
        return plain_body(*arrays)
    weights, turned, named = forward_all(
        masters[:8], tokens, head_in, head_cotangent, image_ids, masters[8]
    )
    named = dict(
        named,
        tokens=tokens,
        head_in=head_in,
        head_cotangent=head_cotangent,
        out_cotangent=out_cotangent,
    )
    results = backward_all(masters[:8], weights, turned, named)
    gradients = results[:8]
    head_in_grad, tokens_grad, norm_grads, grad_norm = results[8:]
    passed = [named["block_low"], named["head_out"], tokens_grad, head_in_grad]
    passed, fresh = optimizer_all(
        gradients, passed, norm_grads, grad_norm, masters, moments, squares, averages
    )
    return (
        (*passed, grad_norm[0, 0])
        + tuple(item for group in fresh for item in group[:3])
        + tuple(group[3] for group in fresh)
    )


def plain_body(
    tokens,
    head_in,
    image_ids,
    out_cotangent,
    head_cotangent,
    weight_attend,
    weight_proj,
    weight_up,
    weight_down,
    weight_cond,
    weight_mod,
    weight_inner,
    weight_outer,
    norm_params,
    mean_attend,
    mean_proj,
    mean_up,
    mean_down,
    mean_cond,
    mean_mod,
    mean_inner,
    mean_outer,
    mean_norms,
    square_attend,
    square_proj,
    square_up,
    square_down,
    square_cond,
    square_mod,
    square_inner,
    square_outer,
    square_norms,
    ema_attend,
    ema_proj,
    ema_up,
    ema_down,
    ema_cond,
    ema_mod,
    ema_inner,
    ema_outer,
    ema_norms,
):
    used = (
        lax.all_gather(
            weight_attend.astype(jnp.bfloat16), AXES, axis=0, tiled=True
        ),
        lax.all_gather(weight_proj.astype(jnp.bfloat16), AXES, axis=0, tiled=True),
        lax.all_gather(weight_up.astype(jnp.bfloat16), AXES, axis=0, tiled=True),
        lax.all_gather(weight_down.astype(jnp.bfloat16), AXES, axis=0, tiled=True),
        lax.all_gather(weight_cond.astype(jnp.bfloat16), AXES, axis=0, tiled=True),
        lax.all_gather(weight_mod.astype(jnp.bfloat16), AXES, axis=0, tiled=True),
        lax.all_gather(
            weight_inner.astype(jnp.bfloat16), AXES, axis=0, tiled=True
        ),
        lax.all_gather(
            weight_outer.astype(jnp.bfloat16), AXES, axis=0, tiled=True
        ),
        lax.all_gather(norm_params.astype(jnp.bfloat16), AXES, axis=0, tiled=True),
    )
    use_attend, use_proj, use_up, use_down, use_cond, use_mod, use_inner, use_outer, use_norms = (
        used
    )
    norm_set = use_norms.astype(jnp.float32)
    inputs = tokens.astype(jnp.float32)
    row_count = tokens.shape[0]
    normed, first_back = jax.vjp(scaled_norm, inputs, norm_set[:, 0], norm_set[:, 1])
    normed_low = normed.astype(jnp.bfloat16)
    mixed_rows = matmul(normed_low, use_attend).astype(jnp.bfloat16)
    query_heads = split_heads(mixed_rows[:, :D])
    own_keys = split_heads(mixed_rows[:, D : 2 * D])
    own_values = split_heads(mixed_rows[:, 2 * D :])
    own_images = image_ids.astype(jnp.bfloat16)
    far_pair, far_images = shifted((mixed_rows[:, D:], own_images), "side", 1)
    both_keys = jnp.concatenate([split_heads(far_pair[:, :D]), own_keys], axis=1)
    both_values = jnp.concatenate([split_heads(far_pair[:, D:]), own_values], axis=1)
    near_allowed = own_images[:, None] == own_images[None, :]
    wide_allowed = own_images[:, None] == jnp.concatenate([far_images, own_images])[None, :]
    masked_side = lax.axis_index("side") == 1

    def visible_forward():
        return lax.map(
            lambda stacked: head_forward(stacked, near_allowed), (query_heads, own_keys, own_values)
        )

    def masked_forward():
        return lax.map(
            lambda stacked: head_forward(stacked, wide_allowed),
            (query_heads, both_keys, both_values),
        )

    attended_heads, log_totals = lax.cond(masked_side, masked_forward, visible_forward)
    attended = join_heads(attended_heads)
    hidden = inputs + matmul(attended, use_proj)
    second, second_back = jax.vjp(scaled_norm, hidden, norm_set[:, 2], norm_set[:, 3])
    second_low = second.astype(jnp.bfloat16)
    inner_pre = matmul(second_low, use_up)
    activated_full, gelu_back = jax.vjp(gelu_exact, inner_pre)
    activated = activated_full.astype(jnp.bfloat16)
    block_low = (hidden + matmul(activated, use_down)).astype(jnp.bfloat16)
    condition = matmul(block_low, use_cond)
    lifted_cond, cond_back = jax.vjp(jax.nn.silu, condition)
    cond_low = lifted_cond.astype(jnp.bfloat16)
    modulation = matmul(cond_low, use_mod)
    head_shift = modulation[:, :HW]
    head_scale = modulation[:, HW : 2 * HW]
    head_gate = modulation[:, 2 * HW :]
    head_rows = head_in.astype(jnp.float32)
    shaped, shaped_back = jax.vjp(modulated, head_rows, head_shift, head_scale)
    shaped_low = shaped.astype(jnp.bfloat16)
    middle = matmul(shaped_low, use_inner)
    lifted_full, middle_back = jax.vjp(jax.nn.silu, middle)
    lifted_rows = lifted_full.astype(jnp.bfloat16)
    branch = matmul(lifted_rows, use_outer)
    head_out = (head_rows + head_gate * branch).astype(jnp.bfloat16)
    head_grad = head_cotangent.astype(jnp.float32)
    grad_branch = (head_grad * head_gate).astype(jnp.bfloat16)
    grad_outer = matmul_left(lifted_rows, grad_branch)
    grad_middle = middle_back(matmul_right(grad_branch, use_outer))[0].astype(jnp.bfloat16)
    grad_inner = matmul_left(shaped_low, grad_middle)
    head_part, grad_shift, grad_scale = shaped_back(matmul_right(grad_middle, use_inner))
    head_in_grad = head_grad + head_part
    grad_modulation = jnp.concatenate([grad_shift, grad_scale, head_grad * branch], axis=1).astype(
        jnp.bfloat16
    )
    grad_mod = matmul_left(cond_low, grad_modulation)
    grad_condition = cond_back(matmul_right(grad_modulation, use_mod))[0].astype(jnp.bfloat16)
    grad_cond = matmul_left(block_low, grad_condition)
    grad_block = out_cotangent.astype(jnp.float32) + matmul_right(grad_condition, use_cond)
    grad_feed = grad_block.astype(jnp.bfloat16)
    grad_down = matmul_left(activated, grad_feed)
    grad_inner_pre = gelu_back(matmul_right(grad_feed, use_down))[0].astype(jnp.bfloat16)
    grad_up = matmul_left(second_low, grad_inner_pre)
    hidden_part, grad_gain_two, grad_bias_two = second_back(matmul_right(grad_inner_pre, use_up))
    grad_hidden = grad_block + hidden_part
    grad_proj_out = grad_hidden.astype(jnp.bfloat16)
    grad_proj = matmul_left(attended, grad_proj_out)
    grad_attended = split_heads(matmul_right(grad_proj_out, use_proj).astype(jnp.bfloat16))

    def visible_backward():
        grad_query, grad_keys, grad_values = lax.map(
            lambda stacked: head_backward(stacked, near_allowed),
            (query_heads, own_keys, own_values, log_totals, grad_attended),
        )
        zero_fill = jnp.zeros_like(grad_keys)
        return (
            grad_query,
            jnp.concatenate([zero_fill, grad_keys], axis=1),
            jnp.concatenate([zero_fill, grad_values], axis=1),
        )

    def masked_backward():
        return lax.map(
            lambda stacked: head_backward(stacked, wide_allowed),
            (query_heads, both_keys, both_values, log_totals, grad_attended),
        )

    grad_query, grad_keys, grad_values = lax.cond(masked_side, masked_backward, visible_backward)
    far_grad = jnp.concatenate(
        [join_heads(grad_keys[:, :row_count]), join_heads(grad_values[:, :row_count])], axis=1
    )
    returned = shifted(far_grad.astype(jnp.bfloat16), "side", -1).astype(far_grad.dtype)
    near_grad = (
        jnp.concatenate(
            [join_heads(grad_keys[:, row_count:]), join_heads(grad_values[:, row_count:])], axis=1
        )
        + returned
    )
    grad_mixed = jnp.concatenate([join_heads(grad_query), near_grad], axis=1).astype(jnp.bfloat16)
    grad_attend = matmul_left(normed_low, grad_mixed)
    tokens_part, grad_gain_one, grad_bias_one = first_back(matmul_right(grad_mixed, use_attend))
    tokens_grad = grad_hidden + tokens_part
    grad_norms = jnp.stack([grad_gain_one, grad_bias_one, grad_gain_two, grad_bias_two], axis=1)
    owned = (
        lax.psum_scatter(grad_attend, AXES, scatter_dimension=0, tiled=True),
        lax.psum_scatter(grad_proj, AXES, scatter_dimension=0, tiled=True),
        lax.psum_scatter(grad_up, AXES, scatter_dimension=0, tiled=True),
        lax.psum_scatter(grad_down, AXES, scatter_dimension=0, tiled=True),
        lax.psum_scatter(grad_cond, AXES, scatter_dimension=0, tiled=True),
        lax.psum_scatter(grad_mod, AXES, scatter_dimension=0, tiled=True),
        lax.psum_scatter(grad_inner, AXES, scatter_dimension=0, tiled=True),
        lax.psum_scatter(grad_outer, AXES, scatter_dimension=0, tiled=True),
        lax.psum_scatter(grad_norms, AXES, scatter_dimension=0, tiled=True),
    )
    local_squares = sum((jnp.sum(gradient * gradient) for gradient in owned))
    grad_norm = jnp.sqrt(lax.psum(local_squares, AXES))
    factor = jnp.minimum(1.0, clip_limit / (grad_norm + 1e-06))
    masters = [
        weight_attend,
        weight_proj,
        weight_up,
        weight_down,
        weight_cond,
        weight_mod,
        weight_inner,
        weight_outer,
        norm_params,
    ]
    moments = [
        mean_attend,
        mean_proj,
        mean_up,
        mean_down,
        mean_cond,
        mean_mod,
        mean_inner,
        mean_outer,
        mean_norms,
    ]
    squares = [
        square_attend,
        square_proj,
        square_up,
        square_down,
        square_cond,
        square_mod,
        square_inner,
        square_outer,
        square_norms,
    ]
    averages = [
        ema_attend,
        ema_proj,
        ema_up,
        ema_down,
        ema_cond,
        ema_mod,
        ema_inner,
        ema_outer,
        ema_norms,
    ]
    keep_old, take_new = average_factors()
    results = []
    smoothed = []
    for position in range(9):
        decays = 1.0 if position < 8 else 0.0
        fresh = adam_step(
            masters[position],
            owned[position] * factor,
            moments[position],
            squares[position],
            decays,
            learn_rates[position],
        )
        results.extend(fresh)
        smoothed.append(keep_old * averages[position] + take_new * fresh[0])
    return (
        (block_low, head_out, tokens_grad, head_in_grad, grad_norm)
        + tuple(results)
        + tuple(smoothed)
    )


def solution(mesh):
    rows, line = P(AXES, None), P(AXES)
    in_specs = (rows, rows, line) + (rows,) * 38
    out_specs = (rows,) * 4 + (P(),) + (rows,) * 36
    return jax.shard_map(body, mesh=mesh, in_specs=in_specs, out_specs=out_specs, check_vma=False)
```
